32 devices in a mesh: row: 8 (over y, x, core), col: 4 (over z).
Axes of the slice: x: 2, y: 2, z: 4, core: 2. Of those that a mesh axis runs over, the one named last changes fastest.
Arguments:
- tokens: bfloat16 [8192, 2048], P(('row', 'col')), may hold values from -6 to 6
- out_grad: bfloat16 [8192, 2048], P(('row', 'col')), may hold values from -6 to 6
- segments: int32 [8, 1024], P('row'), may hold values from 0 to 2, as said below
- routes: int32 [8192, 8], P(('row', 'col')), may hold values from 0 to 63, all different within a row; in each aligned block of 256 rows (0 to 255, 256 to 511, ...) at most 48 rows name the same one
- attn_gain: float32 [2048], replicated, may hold values from 0.25 to 1.75
- ffn_gain: float32 [2048], replicated, may hold values from 0.25 to 1.75
- query_gain: float32 [2048], P('col'), may hold values from 0.25 to 1.75
- key_gain: float32 [2048], P('col'), may hold values from 0.25 to 1.75
- w_query: bfloat16 [2048, 2048], P('row', 'col'), may hold values from -0.125 to 0.125
- w_key: bfloat16 [2048, 2048], P('row', 'col'), may hold values from -0.125 to 0.125
- w_value: bfloat16 [2048, 2048], P('row', 'col'), may hold values from -0.125 to 0.125
- w_out: bfloat16 [2048, 2048], P('col', 'row'), may hold values from -0.75 to 0.75
- router: bfloat16 [2048, 64], replicated, may hold values from -0.0625 to 0.0625
- w_gate: bfloat16 [2048, 65536], P(None, ('row', 'col')), may hold values from -0.125 to 0.125
- w_up: bfloat16 [2048, 65536], P(None, ('row', 'col')), may hold values from -0.125 to 0.125
- w_down: bfloat16 [65536, 2048], P(('row', 'col')), may hold values from -4 to 4
Outputs:
- output: bfloat16 [8192, 2048], P(('row', 'col'))
- input_grad: float32 [8192, 2048], P(('row', 'col'))
- attn_gain_grad: float32 [2048], replicated
- ffn_gain_grad: float32 [2048], replicated
- query_gain_grad: float32 [2048], P('col')
- key_gain_grad: float32 [2048], P('col')
- query_grad: float32 [2048, 2048], P('row', 'col')
- key_grad: float32 [2048, 2048], P('row', 'col')
- value_grad: float32 [2048, 2048], P('row', 'col')
- out_proj_grad: float32 [2048, 2048], P('col', 'row')
- router_grad: float32 [2048, 64], replicated
- gate_grad: float32 [2048, 65536], P(None, ('row', 'col'))
- up_grad: float32 [2048, 65536], P(None, ('row', 'col'))
- down_grad: float32 [65536, 2048], P(('row', 'col'))
The draws below stay inside these ranges and needn't reach their ends.
Inputs may be any that keep to these rules, and one draw needn't show every extreme that they name: `routes`: each token names 8 different experts; among the 256 tokens of one device (aligned blocks of 256 rows) no expert is named by more than 48 tokens, a bound that some block reaches. `segments`: never falling along a sequence.
All inputs are finite; a program needn't handle non-finite values.
Results may differ from the reference program's by a relative error of at most 0.02.
Values may be sent and summed in bfloat16 or wider, within the bound.
No kernel may reach another device: no remote copies, remote signals or barrier semaphores. Data moves between devices by JAX's collectives and lax.ppermute only.
A program may use at most 384 MiB of HBM per device.

```python
import math
import jax
import jax.numpy as jnp
import numpy as np
from jax import lax

D = 2048
HEADS = 16
HEAD_DIM = 128
FF = 1024
EXPERTS = 64
TOP = 8
SEQ = 1024
SEQS = 8
TOKENS = 8192
TOK_DEV = 256
CAP = 48
PIECES = 1


def draw_segments(key, part):
    key = jax.random.fold_in(key, 11)
    first_key, last_key = jax.random.split(key)
    leading = jax.random.randint(first_key, (SEQS, 1), 0, TOK_DEV // 2)
    trailing = jax.random.randint(last_key, (SEQS, 1), SEQ - TOK_DEV // 2 + 1, SEQ + 1)
    position = jnp.arange(SEQ, dtype=jnp.int32)[None, :]
    return (position >= leading).astype(jnp.int32) + (position >= trailing).astype(jnp.int32)


def block_scale(key, extent, cuts, smallest, largest):
    def one(axis_at, blocks):
        steps = jax.random.uniform(jax.random.fold_in(jax.random.fold_in(key, 6), axis_at), (blocks,), jnp.float32, smallest / len(cuts), largest / len(cuts))
        return jnp.repeat(jnp.exp(steps), extent[axis_at] // blocks).reshape((-1,) + (1,) * (len(extent) - axis_at - 1))

    level = one(*cuts[0])
    for cut in cuts[1:]:
        level = level * one(*cut)
    return level


def assign_block(own_key, own, number, rows, count, top, bound, lean):
    order = jax.random.permutation(own_key, count)
    crowded, ordinary = load_shares(count, rows * top, bound, lean, True), load_shares(count, rows * top, bound, lean, False)
    places = jnp.arange(count)

    def named(lengths, offset_by):
        used = int((lengths > 0).sum())
        fixed = max(1, used // 4)
        passed = fixed + (places - fixed + offset_by * (used - fixed)) % max(1, count - fixed)
        return jnp.zeros((count,), jnp.int32).at[order[jnp.where(places < fixed, places, passed)]].set(jnp.asarray(lengths, jnp.int32))

    lengths = jnp.where(number % 4 == 0, named(crowded, number // 4), named(ordinary, number - number // 4 - 1))
    mixed = jax.random.permutation(jax.random.fold_in(own, 3), count)
    giver, sink = mixed[0:count // 2 * 2:2], mixed[1:count // 2 * 2:2]
    slack = jnp.minimum(lengths[giver] - 1, bound - lengths[sink]) // 2
    slack = jnp.where((giver == order[0]) | (sink == order[0]) | (lengths[sink] == 0), 0, jnp.maximum(slack, 0))
    passed = jax.random.randint(jax.random.fold_in(own, 4), (count // 2,), 0, 1 << 20) % (slack + 1)
    lengths = lengths.at[giver].add(-passed).at[sink].add(passed)
    labels = jnp.searchsorted(jnp.cumsum(lengths), jnp.arange(rows * top), side="right").astype(jnp.int32)
    listing = labels.reshape(top, rows).T
    listing = listing[jax.random.permutation(jax.random.fold_in(own, 1), rows)]
    offset_by = jax.random.randint(jax.random.fold_in(own, 2), (rows, 1), 0, top)
    return jnp.take_along_axis(listing, (jnp.arange(top)[None, :] + offset_by) % top, axis=1)


def load_shares(number_of, total, limit, lean, full):
    weights = [(1 << 20) // math.isqrt(grade ** lean) + 1 for grade in range(1, number_of + 1)]
    largest = limit if full else min(limit, max(-(-total // number_of), total * weights[0] // sum(weights)))
    least = 1 if total - largest >= number_of - 1 else 0
    counts, surplus = [largest] + [least] * (number_of - 1), total - largest - least * (number_of - 1)
    while surplus > 0:
        movable = [i for i in range(1, number_of) if counts[i] < largest] or [i for i in range(1, number_of) if counts[i] < limit]
        whole, left = sum([weights[i] for i in movable]), surplus
        for i in movable:
            addition = min(limit - counts[i], max(1, left * weights[i] // whole), surplus)
            counts[i] = counts[i] + addition
            surplus = surplus - addition
    return np.array(counts)


def bell_draw(key, dims, scale, bound, cuts=(), held_as=jnp.bfloat16):
    drawn = scale * jax.random.normal(key, dims, jnp.float32)
    if cuts:
        drawn = drawn * block_scale(key, dims, cuts, -0.22, 0.18)
    return jnp.clip(drawn, -bound, bound).astype(held_as)


def setup_inputs(seed: int = 0) -> dict:
    seeds = jax.random.split(jax.random.key(seed), 17)
    tokens = bell_draw(seeds[0], (TOKENS, D), 1.0, 6.0, ((0, 32),))
    out_grad = bell_draw(seeds[1], (TOKENS, D), 1.0, 6.0, ((0, 32),))
    segments = draw_segments(jax.random.fold_in(seeds[16], 71), 0)
    routes_keys = jax.random.split(jax.random.fold_in(seeds[3], 1), TOKENS // TOK_DEV)
    routes_turns = jax.random.permutation(jax.random.fold_in(seeds[3], 3), TOKENS // TOK_DEV)
    routes = jax.vmap(lambda own, number: assign_block(jax.random.fold_in(seeds[3], 2), own, number, TOK_DEV, EXPERTS, TOP, CAP, 1))(routes_keys, routes_turns).reshape((TOKENS, TOP))
    attn_gain = jnp.clip(1.0 + 0.15 * jax.random.normal(seeds[4], (D,), jnp.float32), 0.25, 1.75)
    ffn_gain = jnp.clip(1.0 + 0.15 * jax.random.normal(seeds[5], (D,), jnp.float32), 0.25, 1.75)
    query_gain = jnp.clip(1.0 + 0.15 * jax.random.normal(seeds[6], (D,), jnp.float32), 0.25, 1.75)
    key_gain = jnp.clip(1.0 + 0.15 * jax.random.normal(seeds[7], (D,), jnp.float32), 0.25, 1.75)
    w_query = bell_draw(seeds[8], (D, D), D ** -0.5, 0.125, ((0, 8), (1, 4)))
    w_key = bell_draw(seeds[9], (D, D), D ** -0.5, 0.125, ((0, 8), (1, 4)))
    w_value = bell_draw(seeds[10], (D, D), D ** -0.5, 0.125, ((0, 8), (1, 4)))
    w_out = bell_draw(seeds[11], (D, D), (D // 32) ** -0.5, 0.75, ((0, 4), (1, 8)))
    router = bell_draw(seeds[12], (D, EXPERTS), (4 * D) ** -0.5, 0.0625)
    w_gate = bell_draw(seeds[13], (D, EXPERTS * FF), D ** -0.5, 0.125, ((1, 32),))
    w_up = bell_draw(seeds[14], (D, EXPERTS * FF), D ** -0.5, 0.125, ((1, 32),))
    w_down = bell_draw(seeds[15], (EXPERTS * FF, D), (max(FF // 512, 1)) ** -0.5, 4.0, ((0, 32),))
    return dict(tokens=tokens, out_grad=out_grad, segments=segments, routes=routes, attn_gain=attn_gain, ffn_gain=ffn_gain, query_gain=query_gain, key_gain=key_gain, w_query=w_query, w_key=w_key, w_value=w_value, w_out=w_out, router=router, w_gate=w_gate, w_up=w_up, w_down=w_down)


EPSILON = 1e-05
ROPE_BASE = 10000.0
MASKED = -1e+30

@jax.custom_vjp
def low(v):
    return lax.optimization_barrier(v.astype(jnp.bfloat16)).astype(jnp.float32)

@jax.custom_vjp
def low_back(v):
    return v

def low_keep(v):
    return (low(v), None)

def low_pass(kept, grad):
    return (grad,)

def back_keep(v):
    return (v, None)

def back_low(kept, grad):
    return (low(grad),)
low.defvjp(low_keep, low_pass)
low_back.defvjp(back_keep, back_low)

def matmul(left, right):
    return jnp.dot(left, right, precision=lax.Precision.HIGHEST)

def normed(values, gain):
    return values * lax.rsqrt(lax.optimization_barrier(jnp.mean(values * values, -1, keepdims=True)) + EPSILON) * gain

def rope_tables(length, head_size):
    half = head_size // 2
    freq = jnp.exp(jnp.arange(half, dtype=jnp.float32) * (-2.0 * jnp.log(ROPE_BASE) / head_size))
    angles = jnp.arange(length, dtype=jnp.float32)[:, None] * freq[None, :]
    return (jnp.cos(angles)[:, None, :], jnp.sin(angles)[:, None, :])

def rotate(values, cosines, sine_table):
    half = values.shape[-1] // 2
    first, second = (values[..., :half], values[..., half:])
    return jnp.concatenate([first * cosines - second * sine_table, second * cosines + first * sine_table], -1)

def mix_experts(inputs, gates, chosen, w_gate, w_up, w_down):
    highest = lax.Precision.HIGHEST
    blocks = SEQ // TOK_DEV
    rows_per = blocks * CAP
    chosen_blocks = chosen.reshape(blocks, TOK_DEV * TOP)
    hits = (chosen_blocks[..., None] == jnp.arange(EXPERTS, dtype=jnp.int32)).astype(jnp.int32)
    slot_index = lax.optimization_barrier(jnp.sum((jnp.cumsum(hits, 1) - hits) * hits, -1)).astype(jnp.int32)
    target = chosen_blocks * rows_per + jnp.arange(blocks, dtype=jnp.int32)[:, None] * CAP + slot_index
    flat_ids = jnp.arange(SEQ * TOP, dtype=jnp.int32).reshape(blocks, TOK_DEV * TOP)
    owner = jnp.full((EXPERTS * rows_per,), SEQ * TOP, dtype=jnp.int32).at[target.reshape(-1)].set(flat_ids.reshape(-1))
    token_ids = owner // TOP
    padded_rows = jnp.concatenate([inputs, jnp.zeros((1, D), inputs.dtype)], 0)
    padded_gates = jnp.concatenate([gates.reshape(-1), jnp.zeros((1,), gates.dtype)], 0)
    rows = padded_rows[token_ids].reshape(EXPERTS, rows_per, D)
    weights = padded_gates[owner].reshape(EXPERTS, rows_per)
    width = FF // PIECES
    gate_four = w_gate.reshape(D, EXPERTS, PIECES, width)
    up_four = w_up.reshape(D, EXPERTS, PIECES, width)
    down_four = w_down.reshape(EXPERTS, PIECES, width, D)
    summed = jnp.zeros((EXPERTS, rows_per, D), inputs.dtype)
    for piece_index in range(PIECES):
        part_rows = low_back(rows)
        gate_pre = low_back(jnp.einsum('erd,def->erf', part_rows, gate_four[:, :, piece_index], precision=highest))
        up_pre = low_back(jnp.einsum('erd,def->erf', part_rows, up_four[:, :, piece_index], precision=highest))
        hidden = low(jax.nn.silu(gate_pre) * up_pre)
        summed = summed + low(low_back(jnp.einsum('erf,efd->erd', hidden, down_four[:, piece_index], precision=highest)))
    contrib = weights[..., None] * summed
    mixed = jnp.zeros((SEQ + 1, D), inputs.dtype).at[token_ids.reshape(-1)].add(contrib.reshape(-1, D))
    return mixed[:SEQ]

def layer(inputs, doc_ids, chosen, params):
    attn_gain, ffn_gain, query_gain, key_gain, w_query, w_key, w_value, w_out, router, w_gate, w_up, w_down = params
    highest = lax.Precision.HIGHEST
    normal_a = low(normed(inputs, attn_gain))
    queries = low_back(matmul(normal_a, w_query))
    keys = low_back(matmul(normal_a, w_key))
    values = low(low_back(matmul(normal_a, w_value)))
    cosines, sine_table = rope_tables(SEQ, HEAD_DIM)
    query_heads = low(rotate(normed(queries, query_gain).reshape(SEQ, HEADS, HEAD_DIM), cosines, sine_table))
    key_heads = low(rotate(normed(keys, key_gain).reshape(SEQ, HEADS, HEAD_DIM), cosines, sine_table))
    value_heads = values.reshape(SEQ, HEADS, HEAD_DIM)
    scores = low_back(jnp.einsum('qhd,khd->hqk', query_heads, key_heads, precision=highest) / jnp.sqrt(jnp.float32(HEAD_DIM)))
    position = jnp.arange(SEQ, dtype=jnp.int32)
    allowed = (position[None, :] <= position[:, None]) & (doc_ids[:, None] == doc_ids[None, :])
    scores = jnp.where(allowed[None], scores, MASKED)
    probs = low(jax.nn.softmax(scores, axis=-1))
    attended = jnp.einsum('hqk,khd->qhd', probs, value_heads, precision=highest).reshape(SEQ, D)
    attn = low_back(matmul(low(low_back(attended)), w_out))
    residual = inputs + attn
    normal_b = low(normed(residual, ffn_gain))
    expert_probs = jax.nn.softmax(low_back(matmul(normal_b, router)), axis=-1)
    gates = jnp.take_along_axis(expert_probs, chosen, axis=1)
    return residual + mix_experts(normal_b, gates, chosen, w_gate, w_up, w_down)

def reference(tokens, out_grad, segments, routes, attn_gain, ffn_gain, query_gain, key_gain, w_query, w_key, w_value, w_out, router, w_gate, w_up, w_down):
    params = tuple((arr.astype(jnp.float32) for arr in (attn_gain, ffn_gain, query_gain, key_gain, w_query, w_key, w_value, w_out, router, w_gate, w_up, w_down)))
    inputs = tokens.astype(jnp.float32).reshape(SEQS, SEQ, D)
    chosen = routes.reshape(SEQS, SEQ, TOP)

    def forward(all_inputs, *weights):

        def sequence_step(carried, pieces):
            seq_inputs, seq_docs, seq_chosen = pieces
            return (carried, layer(seq_inputs, seq_docs, seq_chosen, weights))
        unused, outputs = lax.scan(jax.checkpoint(sequence_step), jnp.zeros((), jnp.float32), (all_inputs, segments, chosen))
        return outputs
    outputs, pullback = jax.vjp(forward, inputs, *params)
    grads = pullback(out_grad.astype(jnp.float32).reshape(SEQS, SEQ, D))
    return (outputs.reshape(TOKENS, D).astype(jnp.bfloat16), grads[0].reshape(TOKENS, D), grads[1], grads[2], grads[3], grads[4], grads[5], grads[6], grads[7], grads[8], grads[9], grads[10], grads[11], grads[12])
```

```python
import functools

import jax
import jax.numpy as jnp
from jax import lax
from jax.experimental import pallas as pl
from jax.experimental.pallas import tpu as pltpu
from jax.sharding import PartitionSpec as P

HEAD_DIM = 128
VMEM_BYTES = 52 * 2**20


EPSILON = 1e-05
ROPE_BASE = 10000.0
MASKED = -1e30


def rms_scale(values):
    return lax.rsqrt(jnp.mean(values * values, -1, keepdims=True) + EPSILON)


def norm_back(values, scale, gain, grad_in):
    scaled_grad = grad_in * gain
    gain_grad = jnp.sum(grad_in * values * scale, 0)
    value_grad = scale * scaled_grad - values * scale * scale * scale * jnp.mean(
        scaled_grad * values, -1, keepdims=True
    )
    return (value_grad, gain_grad)


def times_t(left, right):
    return lax.dot_general(
        left, right, (((1,), (1,)), ((), ())), preferred_element_type=jnp.float32
    )


def rope_tables(length, head_size):
    half = head_size // 2
    freq = jnp.exp(jnp.arange(half, dtype=jnp.float32) * (-2.0 * jnp.log(ROPE_BASE) / head_size))
    angles = jnp.arange(length, dtype=jnp.float32)[:, None] * freq[None, :]
    return (jnp.cos(angles), jnp.sin(angles))


def first_t(left, right):
    return lax.dot_general(
        left, right, (((0,), (0,)), ((), ())), preferred_element_type=jnp.float32
    )


def shift(value, axis, step=1):
    count = lax.axis_size(axis)
    return lax.ppermute(value, axis, [(i, (i + step) % count) for i in range(count)])


def after(value, *earlier):
    return lax.optimization_barrier((value,) + earlier)[0]


def ring_blocks(value, axis, waits=()):
    blocks = [value]
    for hop in range(lax.axis_size(axis) - 1):
        sent = blocks[-1]
        if hop < len(waits):
            sent = after(sent, waits[hop])
        blocks.append(shift(sent, axis))
    return blocks


def hop_blocks(value, axis):
    return [value] + [shift(value, axis, step) for step in range(1, lax.axis_size(axis))]


def ring_sum(parts, axis):
    total = parts[1].astype(jnp.bfloat16)
    for part in parts[2:]:
        total = (shift(total, axis).astype(jnp.float32) + part).astype(jnp.bfloat16)
    return shift(total, axis).astype(jnp.float32) + parts[0]


def exchange_sum(value, axis, place=None):
    parts = [value] + [shift(value, axis, step) for step in range(1, lax.axis_size(axis))]
    if place is None:
        return sum(parts[1:], parts[0])
    return jnp.sum(natural([part[None] for part in parts], place), 0)


def butterfly_sum(value, axis):
    count = lax.axis_size(axis)
    step = 1
    while step < count:
        value = value + lax.ppermute(value, axis, [(i, i ^ step) for i in range(count)])
        step *= 2
    return value


def natural(blocks, place):
    size = blocks[0].shape[0]
    count = len(blocks)
    whole = jnp.zeros((count * size,) + blocks[0].shape[1:], blocks[0].dtype)
    for back, block in enumerate(blocks):
        whole = lax.dynamic_update_slice_in_dim(
            whole, block, ((place - back) % count) * size, 0
        )
    return whole


def block_of(whole, index, count):
    size = whole.shape[0] // count
    return lax.dynamic_slice_in_dim(whole, (index % count) * size, size, 0)


def split_two(values):
    high = lax.reduce_precision(values, 8, 7)
    return high.astype(jnp.bfloat16), (values - high).astype(jnp.bfloat16)


def kernel_params():
    return pltpu.CompilerParams(vmem_limit_bytes=VMEM_BYTES)


def cost(flops, moved):
    return pl.CostEstimate(flops=int(flops), bytes_accessed=int(moved), transcendentals=0)


def down_t_kernel(grad_ref, down_ref, out_ref):
    rows = out_ref.shape[1]
    grads = grad_ref[...].reshape(rows, grad_ref.shape[-1])
    out_ref[0] = times_t(grads, down_ref[...])


def down_t(grads, w_down, units):
    sources, owned, cap, width = grads.shape
    rows = sources * cap
    tile = min(units, 512)
    tiles = units // tile
    return pl.pallas_call(
        down_t_kernel,
        grid=(owned, tiles),
        in_specs=[
            pl.BlockSpec((sources, 1, cap, width), lambda l, f: (0, l, 0, 0)),
            pl.BlockSpec((tile, width), lambda l, f: (l * tiles + f, 0)),
        ],
        out_specs=pl.BlockSpec((1, rows, tile), lambda l, f: (l, 0, f)),
        out_shape=jax.ShapeDtypeStruct((owned, rows, units), jnp.float32),
        compiler_params=kernel_params(),
        cost_estimate=cost(
            2 * owned * rows * units * width, 2 * owned * (rows + units) * width
        ),
        name="down_t",
    )(grads, w_down)


def expert_kernel(
    rows_ref, gate_ref, up_ref, down_grad_ref, mark_ref, back_ref, hid_ref, dgate_ref, dup_ref,
    total, scalar
):
    step = pl.program_id(1)
    rows, width = total.shape
    packed = rows_ref[...].reshape(rows, rows_ref.shape[-1])
    inputs = packed[:, :width]
    mark = mark_ref[0]
    gate = jnp.sum(
        packed[:, width:].astype(jnp.float32) * (mark[0:1] + mark[1:2]), -1, keepdims=True
    )
    gate_pre = jnp.dot(inputs, gate_ref[...], preferred_element_type=jnp.float32)
    up_pre = jnp.dot(inputs, up_ref[...], preferred_element_type=jnp.float32)
    sigmoid = jax.nn.sigmoid(gate_pre)
    active = gate_pre * sigmoid
    hidden = active * up_pre
    raw_grad = down_grad_ref[0]
    gate_part = jnp.sum(hidden * raw_grad, -1, keepdims=True)
    grad_hidden = raw_grad * gate
    grad_gate = (grad_hidden * up_pre * sigmoid * (1.0 + gate_pre * (1.0 - sigmoid))).astype(
        jnp.bfloat16
    )
    grad_up = (grad_hidden * active).astype(jnp.bfloat16)
    hid_ref[0] = (hidden * gate).astype(jnp.bfloat16)
    dgate_ref[0] = grad_gate
    dup_ref[0] = grad_up
    back = times_t(grad_gate, gate_ref[...]) + times_t(grad_up, up_ref[...])

    @pl.when(step == 0)
    def _():
        total[...] = back
        scalar[...] = jnp.broadcast_to(gate_part, scalar.shape)

    @pl.when(step > 0)
    def _():
        total[...] += back
        scalar[...] += jnp.broadcast_to(gate_part, scalar.shape)

    @pl.when(step == pl.num_programs(1) - 1)
    def _():
        sources, _, cap, packed_width = back_ref.shape
        back_ref[:, :, :, :width] = (
            total[...].astype(jnp.bfloat16).reshape(sources, 1, cap, width)
        )
        value = scalar[:, 0:1]
        high = value.astype(jnp.bfloat16).astype(jnp.float32)
        low = value - high
        extra = high * mark[0:1] + low * mark[1:2]
        back_ref[:, :, :, width:] = extra.astype(jnp.bfloat16).reshape(
            sources, 1, cap, packed_width - width
        )


def expert_core(packed, w_gate, w_up, raw_grad, marks, units):
    sources, owned, cap, packed_width = packed.shape
    rows = sources * cap
    width = w_gate.shape[0]
    tile = min(units, 512)
    tiles = units // tile
    hidden_shape = jax.ShapeDtypeStruct((owned, rows, units), jnp.bfloat16)
    hidden_spec = pl.BlockSpec((1, rows, tile), lambda l, f: (l, 0, f))
    weight_spec = pl.BlockSpec((width, tile), lambda l, f: (0, l * tiles + f))
    packed_spec = pl.BlockSpec((sources, 1, cap, packed_width), lambda l, f: (0, l, 0, 0))
    return pl.pallas_call(
        expert_kernel,
        grid=(owned, tiles),
        in_specs=[
            packed_spec,
            weight_spec,
            weight_spec,
            hidden_spec,
            pl.BlockSpec((1, 8, packed_width - width), lambda l, f: (l, 0, 0)),
        ],
        out_specs=[packed_spec, hidden_spec, hidden_spec, hidden_spec],
        out_shape=[
            jax.ShapeDtypeStruct(packed.shape, jnp.bfloat16),
            hidden_shape,
            hidden_shape,
            hidden_shape,
        ],
        scratch_shapes=[
            pltpu.VMEM((rows, width), jnp.float32),
            pltpu.VMEM((rows, 128), jnp.float32),
        ],
        compiler_params=kernel_params(),
        cost_estimate=cost(
            8 * owned * rows * units * width, 4 * owned * (rows + 2 * units) * width
        ),
        name="expert_core",
    )(packed, w_gate, w_up, raw_grad, marks)


def expert_out_kernel(*refs):
    *hid_refs, down_ref, out_ref = refs

    for block, hid_ref in enumerate(hid_refs):

        @pl.when(pl.program_id(0) == block)
        def _():
            out = jnp.dot(hid_ref[0], down_ref[...], preferred_element_type=jnp.float32)
            out_ref[...] = out.astype(jnp.bfloat16).reshape(out_ref.shape)


def expert_out(hiddens, w_down, sources):
    count = len(hiddens)
    owned, rows, units = hiddens[0].shape
    width = w_down.shape[1]
    cap = rows // sources
    tile = min(width, 1024)
    return pl.pallas_call(
        expert_out_kernel,
        grid=(count, owned, width // tile),
        in_specs=[pl.BlockSpec((1, rows, units), lambda b, l, d: (l, 0, 0))] * count
        + [pl.BlockSpec((units, tile), lambda b, l, d: (l, d))],
        out_specs=pl.BlockSpec(
            (sources, 1, cap, tile), lambda b, l, d: (0, b * owned + l, 0, d)
        ),
        out_shape=jax.ShapeDtypeStruct((sources, count * owned, cap, width), jnp.bfloat16),
        compiler_params=kernel_params(),
        cost_estimate=cost(
            2 * count * owned * rows * units * width, 2 * count * owned * (rows + units) * width
        ),
        name="expert_out",
    )(*hiddens, w_down)


def in_grads_kernel(count, *refs):
    row_refs, grad_refs, out_ref = refs[:count], refs[count : 2 * count], refs[2 * count]
    rows = grad_refs[0].shape[1]
    total = None
    for row_ref, grad_ref in zip(row_refs, grad_refs):
        part = first_t(row_ref[...].reshape(rows, row_ref.shape[-1]), grad_ref[0])
        total = part if total is None else total + part
    out_ref[...] = total


def in_grads(packed, grads, width):
    count = len(packed)
    sources, owned, cap, _ = packed[0].shape
    _, rows, units = grads[0].shape
    tile = min(width, 512)
    return pl.pallas_call(
        functools.partial(in_grads_kernel, count),
        grid=(owned, width // tile),
        in_specs=[pl.BlockSpec((sources, 1, cap, tile), lambda l, d: (0, l, 0, d))] * count
        + [pl.BlockSpec((1, rows, units), lambda l, d: (l, 0, 0))] * count,
        out_specs=pl.BlockSpec((tile, units), lambda l, d: (d, l)),
        out_shape=jax.ShapeDtypeStruct((width, owned * units), jnp.float32),
        compiler_params=kernel_params(),
        cost_estimate=cost(
            2 * owned * count * rows * units * width, 4 * owned * units * width
        ),
        name="in_grads",
    )(*packed, *grads)


def down_grads_kernel(count, *refs):
    hid_refs, grad_refs = refs[:count], refs[count : 2 * count]
    out_ref = refs[2 * count]
    rows = hid_refs[0].shape[1]
    total = None
    for hid_ref, grad_ref in zip(hid_refs, grad_refs):
        part = first_t(hid_ref[0], grad_ref[...].reshape(rows, grad_ref.shape[-1]))
        total = part if total is None else total + part
    out_ref[...] = total


def down_grads(hiddens, grads):
    count = len(hiddens)
    sources, owned, cap, width = grads[0].shape
    _, rows, units = hiddens[0].shape
    tile = min(units, 256)
    tiles = units // tile
    return pl.pallas_call(
        functools.partial(down_grads_kernel, count),
        grid=(owned, tiles),
        in_specs=[pl.BlockSpec((1, rows, tile), lambda l, f: (l, 0, f))] * count
        + [pl.BlockSpec((sources, 1, cap, width), lambda l, f: (0, l, 0, 0))] * count,
        out_specs=pl.BlockSpec((tile, width), lambda l, f: (l * tiles + f, 0)),
        out_shape=jax.ShapeDtypeStruct((owned * units, width), jnp.float32),
        compiler_params=kernel_params(),
        cost_estimate=cost(
            2 * owned * count * rows * units * width, 4 * owned * units * width
        ),
        name="down_grads",
    )(*hiddens, *grads)


def turn(values, cosines, sines):
    return values * cosines + pltpu.roll(values, values.shape[-1] // 2, 1) * sines


def score_t(keys, queries, key_docs, query_docs, first, factor):
    scores = times_t(keys, queries) * factor
    key_pos = lax.broadcasted_iota(jnp.int32, scores.shape, 0)
    query_pos = first + lax.broadcasted_iota(jnp.int32, scores.shape, 1)
    return jnp.where((key_pos <= query_pos) & (key_docs == query_docs), scores, MASKED)


def attend_kernel(
    block, factor, query_ref, key_ref, value_ref, inv_query_ref, inv_key_ref, query_gain_ref,
    key_gain_ref, cos_ref, sin_ref, doc_col_ref, doc_row_ref, query_out, key_out, value_out,
    attended_ref, log_ref
):
    cosines, sines = cos_ref[...], sin_ref[...]
    queries = turn(query_ref[...] * inv_query_ref[...] * query_gain_ref[...], cosines, sines)
    keys = turn(key_ref[...] * inv_key_ref[...] * key_gain_ref[...], cosines, sines)
    query_out[...] = queries.astype(jnp.bfloat16)
    key_out[...] = keys.astype(jnp.bfloat16)
    value_out[...] = value_ref[...].astype(jnp.bfloat16)
    for first in range(0, query_ref.shape[0], block):
        stop = first + block
        scores = score_t(
            key_out[:stop, :],
            query_out[first:stop, :],
            doc_col_ref[:stop, :],
            doc_row_ref[:, first:stop],
            first,
            factor,
        )
        peak = jnp.max(scores, 0, keepdims=True)
        exps = jnp.exp(scores - peak)
        total = jnp.sum(exps, 0, keepdims=True)
        log_ref[0, :, first:stop] = peak + jnp.log(total)
        weights = (exps * (1.0 / total)).astype(jnp.bfloat16)
        attended_ref[first:stop, :] = first_t(value_out[:stop, :], weights).T.astype(jnp.bfloat16)


def attend(qkv, inv_query, inv_key, query_gain, key_gain, tables, doc_ids, block, factor):
    length = qkv.shape[0]
    head_cols = qkv.shape[1] // 3
    heads = head_cols // HEAD_DIM
    head_spec = pl.BlockSpec((length, HEAD_DIM), lambda h: (0, h))
    gain_spec = pl.BlockSpec((1, HEAD_DIM), lambda h: (0, h))

    def whole(shape):
        return pl.BlockSpec(shape, lambda h: (0, 0))

    out = jax.ShapeDtypeStruct((length, head_cols), jnp.bfloat16)
    return pl.pallas_call(
        functools.partial(attend_kernel, block, factor),
        grid=(heads,),
        in_specs=[
            head_spec,
            pl.BlockSpec((length, HEAD_DIM), lambda h: (0, heads + h)),
            pl.BlockSpec((length, HEAD_DIM), lambda h: (0, 2 * heads + h)),
            whole((length, 1)),
            whole((length, 1)),
            gain_spec,
            gain_spec,
            whole((length, HEAD_DIM)),
            whole((length, HEAD_DIM)),
            whole((length, 1)),
            whole((1, length)),
        ],
        out_specs=[head_spec] * 4 + [pl.BlockSpec((1, 1, length), lambda h: (h, 0, 0))],
        out_shape=[out] * 4 + [jax.ShapeDtypeStruct((heads, 1, length), jnp.float32)],
        compiler_params=kernel_params(),
        cost_estimate=cost(24 * head_cols * length * length, 20 * length * head_cols),
        name="attend",
    )(
        qkv,
        qkv,
        qkv,
        inv_query,
        inv_key,
        query_gain[None, :],
        key_gain[None, :],
        tables[0],
        tables[1],
        doc_ids[:, None],
        doc_ids[None, :],
    )


def attend_back_kernel(
    block, factor, query_ref, key_ref, value_ref, out_grad_ref, log_ref, raw_query_ref,
    raw_key_ref, inv_query_ref, inv_key_ref, query_gain_ref, key_gain_ref, cos_ref, sin_ref,
    doc_col_ref, doc_row_ref, query_out, key_out, value_out, query_sum_ref, key_sum_ref,
    query_gain_out, key_gain_out, query_grad, key_grad, value_grad
):
    key_grad[...] = jnp.zeros(key_grad.shape, jnp.float32)
    value_grad[...] = jnp.zeros(value_grad.shape, jnp.float32)
    for first in range(0, query_ref.shape[0], block):
        stop = first + block
        keys = key_ref[:stop, :]
        queries = query_ref[first:stop, :]
        out_grads = out_grad_ref[first:stop, :]
        scores = score_t(
            keys, queries, doc_col_ref[:stop, :], doc_row_ref[:, first:stop], first, factor
        )
        probs = jnp.exp(scores - log_ref[0, :, first:stop])
        prob_grads = times_t(value_ref[:stop, :], out_grads)
        mean = jnp.sum(probs * prob_grads, 0, keepdims=True)
        score_grads = (probs * (prob_grads - mean)).astype(jnp.bfloat16)
        value_grad[:stop, :] += jnp.dot(
            probs.astype(jnp.bfloat16), out_grads, preferred_element_type=jnp.float32
        )
        key_grad[:stop, :] += jnp.dot(score_grads, queries, preferred_element_type=jnp.float32)
        query_grad[first:stop, :] = first_t(keys, score_grads).T
    cosines, sines = cos_ref[...], -sin_ref[...]
    value_out[...] = value_grad[...].astype(jnp.bfloat16)
    head = pl.program_id(0)
    for grad, raw_ref, inv_ref, gain_ref, out_ref, sum_ref, gain_out in (
        (
            query_grad, raw_query_ref, inv_query_ref, query_gain_ref, query_out, query_sum_ref,
            query_gain_out
        ),
        (key_grad, raw_key_ref, inv_key_ref, key_gain_ref, key_out, key_sum_ref, key_gain_out),
    ):
        norm_grad = turn(grad[...] * factor, cosines, sines)
        raw = raw_ref[...]
        scaled = norm_grad * gain_ref[...]
        out_ref[...] = scaled
        part = jnp.sum(scaled * raw, -1, keepdims=True)
        gain_out[...] = jnp.sum(norm_grad * raw * inv_ref[...], 0, keepdims=True)

        @pl.when(head == 0)
        def _():
            sum_ref[...] = part

        @pl.when(head > 0)
        def _():
            sum_ref[...] += part


def attend_back(
    parts, out_grads, logs, qkv, inv_query, inv_key, query_gain, key_gain, tables, doc_ids, block,
    factor
):
    length = qkv.shape[0]
    head_cols = qkv.shape[1] // 3
    heads = head_cols // HEAD_DIM
    head_spec = pl.BlockSpec((length, HEAD_DIM), lambda h: (0, h))
    gain_spec = pl.BlockSpec((1, HEAD_DIM), lambda h: (0, h))

    def whole(shape):
        return pl.BlockSpec(shape, lambda h: (0, 0))

    wide = jax.ShapeDtypeStruct((length, head_cols), jnp.float32)
    narrow = jax.ShapeDtypeStruct((length, head_cols), jnp.bfloat16)
    column = jax.ShapeDtypeStruct((length, 1), jnp.float32)
    gains = jax.ShapeDtypeStruct((1, head_cols), jnp.float32)
    return pl.pallas_call(
        functools.partial(attend_back_kernel, block, factor),
        grid=(heads,),
        in_specs=[head_spec] * 4
        + [
            pl.BlockSpec((1, 1, length), lambda h: (h, 0, 0)),
            head_spec,
            pl.BlockSpec((length, HEAD_DIM), lambda h: (0, heads + h)),
            whole((length, 1)),
            whole((length, 1)),
            gain_spec,
            gain_spec,
            whole((length, HEAD_DIM)),
            whole((length, HEAD_DIM)),
            whole((length, 1)),
            whole((1, length)),
        ],
        out_specs=[
            head_spec,
            head_spec,
            head_spec,
            whole((length, 1)),
            whole((length, 1)),
            gain_spec,
            gain_spec,
        ],
        out_shape=[wide, wide, narrow, column, column, gains, gains],
        scratch_shapes=[pltpu.VMEM((length, HEAD_DIM), jnp.float32)] * 3,
        compiler_params=kernel_params(),
        cost_estimate=cost(40 * head_cols * length * length, 40 * length * head_cols),
        name="attend_back",
    )(
        *parts,
        out_grads,
        logs,
        qkv,
        qkv,
        inv_query,
        inv_key,
        query_gain[None, :],
        key_gain[None, :],
        tables[0],
        tables[1],
        doc_ids[:, None],
        doc_ids[None, :],
    )


def placings(routes, owners, capacity):
    tok_count = routes.shape[0]
    named = jnp.any(owners[:, None, None] == routes[None, :, :], -1)
    before = (
        jnp.arange(tok_count)[:, None] < jnp.arange(tok_count)[None, :]
    ).astype(jnp.bfloat16)
    slot = jnp.dot(named.astype(jnp.bfloat16), before, preferred_element_type=jnp.float32)
    hit = (slot[:, None, :] == jnp.arange(capacity, dtype=jnp.float32)[None, :, None]) & named[
        :, None, :
    ]
    return hit.astype(jnp.bfloat16).reshape(owners.shape[0] * capacity, tok_count)


def local(
    tokens,
    out_grad,
    segments,
    routes,
    attn_gain,
    ffn_gain,
    query_gain,
    key_gain,
    w_query,
    w_key,
    w_value,
    w_out,
    router,
    w_gate,
    w_up,
    w_down,
):
    rows_total = lax.axis_size("row")
    cols_total = lax.axis_size("col")
    devices = rows_total * cols_total
    place = lax.axis_index("col")
    tok_count, width = tokens.shape
    top_count = routes.shape[1]
    expert_count = router.shape[1]
    capacity = tok_count * top_count * 3 // (expert_count * 2)
    capacity = -(-capacity // 16) * 16
    local_units = w_gate.shape[1]
    ff_units = local_units * devices // expert_count
    units = min(local_units, ff_units)
    owned = local_units // units
    head_cols = w_query.shape[1]
    doc_ids = segments[0]
    length = doc_ids.shape[0]
    block = min(length, 256)
    factor = 1.0 / HEAD_DIM**0.5
    extra = -(-2 * expert_count // 128) * 128

    inputs_f = tokens.astype(jnp.float32)
    inv_first = rms_scale(inputs_f)
    normal_a = (inputs_f * inv_first * attn_gain).astype(jnp.bfloat16)
    wqkv = lax.all_gather(
        jnp.concatenate([w_query, w_key, w_value], 1), "row", axis=0, tiled=True
    )
    wo_full = lax.all_gather(w_out, "row", axis=1, tiled=True)
    a_blocks = ring_blocks(normal_a, "col")
    g_blocks = [out_grad, shift(after(out_grad, a_blocks[-1]), "col")]

    route_blocks = hop_blocks(routes, "col")
    plane_ids = (jnp.arange(rows_total) * cols_total + place)[:, None] * local_units
    owners = ((plane_ids + jnp.arange(owned)[None, :] * units) // ff_units).reshape(-1)
    row_place = lax.axis_index("row")
    my_ids = (
        (row_place * cols_total + place) * local_units + jnp.arange(owned) * units
    ) // ff_units
    extra_ids = jnp.arange(extra)
    marks = jnp.concatenate(
        [
            (extra_ids[None, None, :] == my_ids[:, None, None]).astype(jnp.float32),
            (extra_ids[None, None, :] == my_ids[:, None, None] + expert_count).astype(
                jnp.float32
            ),
            jnp.zeros((owned, 6, extra), jnp.float32),
        ],
        1,
    )
    placed = [placings(block_routes, owners, capacity) for block_routes in route_blocks]

    queue = []

    def in_plane(table, *earlier):
        if queue or earlier:
            table = after(table, *queue[-1:], *earlier)
        queue.append(lax.all_to_all(table, "row", split_axis=0, concat_axis=0, tiled=True))
        return queue[-1]

    def to_experts(values, back, *earlier):
        table = jnp.dot(placed[back], values, preferred_element_type=jnp.float32)
        table = table.astype(jnp.bfloat16).reshape(rows_total, owned, capacity, -1)
        return in_plane(table, *earlier)

    def to_tokens(table, back, *earlier):
        home = in_plane(table, *earlier)
        return first_t(
            placed[back], home.reshape(rows_total * owned * capacity, table.shape[-1])
        )

    g_rows = [to_experts(out_grad, 0)]
    seq_rows = after(natural(a_blocks, place), g_rows[0])
    qkv = jnp.dot(seq_rows, wqkv, preferred_element_type=jnp.float32)
    query_raw = qkv[:, :head_cols]
    key_raw = qkv[:, head_cols : 2 * head_cols]
    squares = exchange_sum(
        jnp.stack([jnp.sum(query_raw * query_raw, -1), jnp.sum(key_raw * key_raw, -1)]), "col"
    )
    g_blocks.append(shift(after(g_blocks[1], squares), "col"))
    g_rows.append(to_experts(after(g_blocks[1], qkv), 1))
    inv_query = lax.rsqrt(squares[0] / width + EPSILON)[:, None]
    inv_key = lax.rsqrt(squares[1] / width + EPSILON)[:, None]
    cosines, sine_table = rope_tables(length, HEAD_DIM)
    tables = (
        jnp.concatenate([cosines, cosines], -1),
        jnp.concatenate([-sine_table, sine_table], -1),
    )
    *heads_out, attended, logs = attend(
        qkv, inv_query, inv_key, query_gain, key_gain, tables, doc_ids, block, factor
    )
    attended = after(attended, g_blocks[2])
    raw_grads = [down_t(rows, w_down, units) for rows in g_rows]
    g_rows.append(to_experts(g_blocks[2], 2))
    parts = [
        jnp.dot(
            block_of(attended, place - back, cols_total),
            wo_full,
            preferred_element_type=jnp.float32,
        )
        for back in range(cols_total)
    ]
    parts[2] = after(parts[2], raw_grads[0])
    parts[3] = after(parts[3], raw_grads[1])
    parts[0] = after(parts[0], g_rows[2])
    attn = ring_sum(parts, "col")
    residual = inputs_f + attn
    inv_second = rms_scale(residual)
    normal_b = (residual * inv_second * ffn_gain).astype(jnp.bfloat16)
    expert_probs = jax.nn.softmax(
        jnp.dot(normal_b, router, preferred_element_type=jnp.float32), axis=-1
    )

    high, low = split_two(expert_probs)
    packed_b = jnp.concatenate(
        [normal_b, high, low, jnp.zeros((tok_count, extra - 2 * expert_count), jnp.bfloat16)], 1
    )
    b_blocks = [packed_b, shift(packed_b, "col")]
    b_rows = [to_experts(packed_b, 0)]
    raw_grads.append(down_t(g_rows[2], w_down, units))
    core = []

    def run_core():
        back = len(core)
        core.append(expert_core(b_rows[back], w_gate, w_up, raw_grads[back], marks, units))

    b_rows.append(to_experts(after(b_blocks[1], raw_grads[2]), 1))
    run_core()
    for back in range(2, cols_total):
        if back > 2:
            g_blocks.append(shift(after(g_blocks[-1], b_blocks[-1]), "col"))
            b_blocks[-1] = after(b_blocks[-1], g_blocks[-1])
        b_blocks.append(shift(b_blocks[-1], "col"))
        if back > 2:
            g_rows.append(to_experts(after(g_blocks[back], core[-1][1]), back))
            run_core()
            raw_grads.append(down_t(g_rows[back], w_down, units))
        b_rows.append(to_experts(after(b_blocks[back], core[-1][1]), back))
        if back == 2:
            run_core()
    last = cols_total - 1
    share = to_tokens(core[1][0], 1, raw_grads[last], core[-1][1])
    grad_packed = share.astype(jnp.bfloat16)
    run_core()
    hiddens = [part[1] for part in core]
    gate_grad = in_grads(b_rows, [part[2] for part in core], width)
    up_grad = in_grads(b_rows, [part[3] for part in core], width)
    down_grad = down_grads(hiddens, g_rows)
    order = list(range(1, cols_total)) + [0]
    out_groups = [order[i : i + 2] for i in range(0, cols_total, 2)]
    outs = [
        expert_out([hiddens[back] for back in group], w_down, rows_total)
        for group in out_groups
    ]
    totals = [None, None, grad_packed]
    for back in range(2, cols_total):
        beside = {2: [hiddens[last]], last: [gate_grad, outs[0]]}.get(back, [])
        if totals[back - 1] is not None:
            beside = beside + [totals[back - 1]]
        share = to_tokens(core[back][0], back, *beside)
        grad_packed = (shift(grad_packed, "col").astype(jnp.float32) + share).astype(
            jnp.bfloat16
        )
        totals.append(grad_packed)
    share = to_tokens(core[0][0], 0, up_grad, totals[-2], *outs[1:])
    share = after(share, down_grad)
    grad_packed = shift(grad_packed, "col").astype(jnp.float32) + share

    def outs_home(number):
        home = in_plane(outs[number])
        for slot, back in enumerate(out_groups[number]):
            rows = home[:, slot * owned : (slot + 1) * owned]
            rows = rows.reshape(rows_total * owned * capacity, width)
            out_shares[back] = first_t(placed[back], rows)

    out_shares = {}
    outs_home(0)

    grad_f = out_grad.astype(jnp.float32)
    grad_probs = (
        grad_packed[:, width : width + expert_count]
        + grad_packed[:, width + expert_count : width + 2 * expert_count]
    )
    grad_logits = (
        expert_probs * (grad_probs - jnp.sum(expert_probs * grad_probs, -1, keepdims=True))
    ).astype(jnp.bfloat16)
    grad_normal_b = grad_packed[:, :width] + times_t(grad_logits, router)
    grad_norm_second, ffn_gain_local = norm_back(residual, inv_second, ffn_gain, grad_normal_b)
    grad_residual = grad_f + grad_norm_second
    grad_attn = grad_residual.astype(jnp.bfloat16)
    small = jnp.concatenate(
        [grad_logits]
        + [part.reshape(tok_count, -1) for part in split_two(ffn_gain_local)]
        + [jnp.zeros((tok_count, 128 - expert_count - 2 * width // tok_count), jnp.bfloat16)],
        1,
    )

    grad_blocks = ring_blocks(grad_attn, "col")
    incoming = after(natural(grad_blocks, place), out_shares[1])
    for number in range(1, len(outs)):
        outs_home(number)
    moe = after(out_shares[1].astype(jnp.bfloat16), grad_blocks[-1])
    moe = (shift(moe, "col").astype(jnp.float32) + out_shares[2]).astype(jnp.bfloat16)
    wout_local = first_t(incoming, attended).astype(jnp.bfloat16)
    grad_out_heads = times_t(incoming, wo_full).astype(jnp.bfloat16)
    (
        query_scaled,
        key_scaled,
        grad_value_b,
        query_sum,
        key_sum,
        query_gain_local,
        key_gain_local,
    ) = attend_back(
        heads_out,
        grad_out_heads,
        logs,
        qkv,
        inv_query,
        inv_key,
        query_gain,
        key_gain,
        tables,
        doc_ids,
        block,
        factor,
    )
    sums = exchange_sum(jnp.stack([query_sum[:, 0], key_sum[:, 0]]), "col")
    small_blocks = hop_blocks(after(small, query_sum), "col")
    small_rows = natural(small_blocks, place)
    router_local = first_t(natural(b_blocks, place)[:, :width], small_rows[:, :expert_count])
    gain_width = width // tok_count
    gain_parts = small_rows[:, expert_count : expert_count + 2 * gain_width].astype(jnp.float32)
    gain_parts = gain_parts[:, :gain_width] + gain_parts[:, gain_width:]
    ffn_gain_part = jnp.sum(gain_parts.reshape(cols_total, width), 0)
    early = jnp.concatenate(
        [
            router_local.reshape(rows_total, -1, expert_count),
            ffn_gain_part.reshape(rows_total, -1, expert_count),
        ],
        1,
    )
    early = jnp.sum(in_plane(early), 0)
    moe = after(moe, sums)
    for back in order[2:]:
        moe = shift(moe, "col").astype(jnp.float32) + out_shares[back]
        if back:
            moe = moe.astype(jnp.bfloat16)
    output = (residual + moe).astype(jnp.bfloat16)
    grad_query_b = (
        inv_query * query_scaled
        - query_raw * inv_query * inv_query * inv_query * (sums[0] / width)[:, None]
    ).astype(jnp.bfloat16)
    grad_key_b = (
        inv_key * key_scaled - key_raw * inv_key * inv_key * inv_key * (sums[1] / width)[:, None]
    ).astype(jnp.bfloat16)
    grad_qkv = jnp.concatenate([grad_query_b, grad_key_b, grad_value_b], 1)
    da_parts = [
        times_t(block_of(grad_qkv, place - back, cols_total), wqkv) for back in range(cols_total)
    ]
    da_total = da_parts[1].astype(jnp.bfloat16)
    for back in range(2, cols_total):
        da_came = shift(da_total, "col")
        if back == 2:
            first_came = da_came
        da_total = (da_came.astype(jnp.float32) + da_parts[back]).astype(jnp.bfloat16)
    grad_normal_a = shift(da_total, "col").astype(jnp.float32) + da_parts[0]
    wqkv_local = first_t(seq_rows, after(grad_qkv, first_came)).astype(jnp.bfloat16)
    attn_gain_local = (
        jnp.sum(wqkv.astype(jnp.float32) * wqkv_local.astype(jnp.float32), -1) / attn_gain
    )
    core_place = row_place % 2

    def over_cores(value):
        halves = value.reshape(rows_total // 2, 2, -1, value.shape[-1])
        other = lax.ppermute(
            lax.dynamic_index_in_dim(halves, 1 - core_place, 1, False),
            "row",
            [(i, i ^ 1) for i in range(rows_total)],
        )
        return (
            lax.dynamic_index_in_dim(halves, core_place, 1, False).astype(jnp.float32) + other
        ).astype(jnp.bfloat16)

    pair = jnp.concatenate([over_cores(wqkv_local), over_cores(wout_local)], -1)
    pair = lax.all_to_all(
        after(pair, queue[-1]),
        "row",
        split_axis=0,
        concat_axis=0,
        tiled=True,
        axis_index_groups=[list(range(core, rows_total, 2)) for core in range(2)],
    )
    queue.append(pair)
    late = jnp.concatenate([attn_gain_local, query_gain_local[0], key_gain_local[0]])
    late = jnp.concatenate([early.reshape(-1), late]).reshape(1, -1, 128)
    spread = in_plane(jnp.broadcast_to(late, (rows_total,) + late.shape[1:]))
    spread = spread.reshape(rows_total, -1)
    late = jnp.sum(spread[:, early.size :], 0)
    early = spread[:, : early.size].reshape((rows_total,) + early.shape)
    attn_gain_grad = exchange_sum(late[:width], "col", place)

    weight_grads = jnp.sum(pair.astype(jnp.float32), 0)
    wqkv_grad = weight_grads[:, : 3 * head_cols]
    out_proj_grad = weight_grads[:, 3 * head_cols :].T
    router_grad = early[:, : width // rows_total].reshape(width, expert_count)
    ffn_gain_grad = early[:, width // rows_total :].reshape(width)
    grad_norm_first, _ = norm_back(inputs_f, inv_first, attn_gain, grad_normal_a)
    input_grad = grad_residual + grad_norm_first
    return (
        output,
        input_grad,
        attn_gain_grad,
        ffn_gain_grad,
        late[width : width + head_cols],
        late[width + head_cols :],
        wqkv_grad[:, :head_cols],
        wqkv_grad[:, head_cols : 2 * head_cols],
        wqkv_grad[:, 2 * head_cols :],
        out_proj_grad,
        router_grad,
        gate_grad,
        up_grad,
        down_grad,
    )


def solution(mesh):
    return jax.shard_map(
        local,
        mesh=mesh,
        in_specs=(
            P(("row", "col"), None),
            P(("row", "col"), None),
            P("row", None),
            P(("row", "col"), None),
            P(),
            P(),
            P("col"),
            P("col"),
            P("row", "col"),
            P("row", "col"),
            P("row", "col"),
            P("col", "row"),
            P(),
            P(None, ("row", "col")),
            P(None, ("row", "col")),
            P(("row", "col"), None),
        ),
        out_specs=(
            P(("row", "col"), None),
            P(("row", "col"), None),
            P(),
            P(),
            P("col"),
            P("col"),
            P("row", "col"),
            P("row", "col"),
            P("row", "col"),
            P("col", "row"),
            P(),
            P(None, ("row", "col")),
            P(None, ("row", "col")),
            P(("row", "col"), None),
        ),
        check_vma=False,
    )
```

```python
import functools

import jax
import jax.numpy as jnp
from jax import lax
from jax.experimental import pallas as pl
from jax.experimental.pallas import tpu as pltpu
from jax.sharding import PartitionSpec as P

HEAD_DIM = 128
VMEM_BYTES = 52 * 2**20


EPSILON = 1e-05
ROPE_BASE = 10000.0
MASKED = -1e30


def rms_scale(values):
    return lax.rsqrt(jnp.mean(values * values, -1, keepdims=True) + EPSILON)


def norm_back(values, scale, gain, grad_in):
    scaled_grad = grad_in * gain
    gain_grad = jnp.sum(grad_in * values * scale, 0)
    value_grad = scale * scaled_grad - values * scale * scale * scale * jnp.mean(
        scaled_grad * values, -1, keepdims=True
    )
    return (value_grad, gain_grad)


def times_t(left, right):
    return lax.dot_general(
        left, right, (((1,), (1,)), ((), ())), preferred_element_type=jnp.float32
    )


def rope_tables(length, head_size):
    half = head_size // 2
    freq = jnp.exp(jnp.arange(half, dtype=jnp.float32) * (-2.0 * jnp.log(ROPE_BASE) / head_size))
    angles = jnp.arange(length, dtype=jnp.float32)[:, None] * freq[None, :]
    return (jnp.cos(angles), jnp.sin(angles))


def first_t(left, right):
    return lax.dot_general(
        left, right, (((0,), (0,)), ((), ())), preferred_element_type=jnp.float32
    )


def shift(value, axis, step=1):
    count = lax.axis_size(axis)
    return lax.ppermute(value, axis, [(i, (i + step) % count) for i in range(count)])


def after(value, *earlier):
    return lax.optimization_barrier((value,) + earlier)[0]


def ring_blocks(value, axis, waits=()):
    blocks = [value]
    for hop in range(lax.axis_size(axis) - 1):
        sent = blocks[-1]
        if hop < len(waits):
            sent = after(sent, waits[hop])
        blocks.append(shift(sent, axis))
    return blocks


def hop_blocks(value, axis):
    return [value] + [shift(value, axis, step) for step in range(1, lax.axis_size(axis))]


def ring_sum(parts, axis):
    total = parts[1].astype(jnp.bfloat16)
    for part in parts[2:]:
        total = (shift(total, axis).astype(jnp.float32) + part).astype(jnp.bfloat16)
    return shift(total, axis).astype(jnp.float32) + parts[0]


def exchange_sum(value, axis, place=None):
    parts = [value] + [shift(value, axis, step) for step in range(1, lax.axis_size(axis))]
    if place is None:
        return sum(parts[1:], parts[0])
    return jnp.sum(natural([part[None] for part in parts], place), 0)


def butterfly_sum(value, axis):
    count = lax.axis_size(axis)
    step = 1
    while step < count:
        value = value + lax.ppermute(value, axis, [(i, i ^ step) for i in range(count)])
        step *= 2
    return value


def natural(blocks, place):
    size = blocks[0].shape[0]
    count = len(blocks)
    whole = jnp.zeros((count * size,) + blocks[0].shape[1:], blocks[0].dtype)
    for back, block in enumerate(blocks):
        whole = lax.dynamic_update_slice_in_dim(
            whole, block, ((place - back) % count) * size, 0
        )
    return whole


def block_of(whole, index, count):
    size = whole.shape[0] // count
    return lax.dynamic_slice_in_dim(whole, (index % count) * size, size, 0)


def split_two(values):
    high = lax.reduce_precision(values, 8, 7)
    return high.astype(jnp.bfloat16), (values - high).astype(jnp.bfloat16)


def kernel_params():
    return pltpu.CompilerParams(vmem_limit_bytes=VMEM_BYTES)


def cost(flops, moved):
    return pl.CostEstimate(flops=int(flops), bytes_accessed=int(moved), transcendentals=0)


def down_t_kernel(grad_ref, down_ref, out_ref):
    rows = out_ref.shape[1]
    grads = grad_ref[...].reshape(rows, grad_ref.shape[-1])
    out_ref[0] = times_t(grads, down_ref[...])


def down_t(grads, w_down, units):
    sources, owned, cap, width = grads.shape
    rows = sources * cap
    tile = min(units, 512)
    tiles = units // tile
    return pl.pallas_call(
        down_t_kernel,
        grid=(owned, tiles),
        in_specs=[
            pl.BlockSpec((sources, 1, cap, width), lambda l, f: (0, l, 0, 0)),
            pl.BlockSpec((tile, width), lambda l, f: (l * tiles + f, 0)),
        ],
        out_specs=pl.BlockSpec((1, rows, tile), lambda l, f: (l, 0, f)),
        out_shape=jax.ShapeDtypeStruct((owned, rows, units), jnp.float32),
        compiler_params=kernel_params(),
        cost_estimate=cost(
            2 * owned * rows * units * width, 2 * owned * (rows + units) * width
        ),
        name="down_t",
    )(grads, w_down)


def expert_kernel(
    rows_ref, gate_ref, up_ref, down_grad_ref, mark_ref, back_ref, hid_ref, dgate_ref, dup_ref,
    total, scalar
):
    step = pl.program_id(1)
    rows, width = total.shape
    packed = rows_ref[...].reshape(rows, rows_ref.shape[-1])
    inputs = packed[:, :width]
    mark = mark_ref[0]
    gate = jnp.sum(
        packed[:, width:].astype(jnp.float32) * (mark[0:1] + mark[1:2]), -1, keepdims=True
    )
    gate_pre = jnp.dot(inputs, gate_ref[...], preferred_element_type=jnp.float32)
    up_pre = jnp.dot(inputs, up_ref[...], preferred_element_type=jnp.float32)
    sigmoid = jax.nn.sigmoid(gate_pre)
    active = gate_pre * sigmoid
    hidden = active * up_pre
    raw_grad = down_grad_ref[0]
    gate_part = jnp.sum(hidden * raw_grad, -1, keepdims=True)
    grad_hidden = raw_grad * gate
    grad_gate = (grad_hidden * up_pre * sigmoid * (1.0 + gate_pre * (1.0 - sigmoid))).astype(
        jnp.bfloat16
    )
    grad_up = (grad_hidden * active).astype(jnp.bfloat16)
    hid_ref[0] = (hidden * gate).astype(jnp.bfloat16)
    dgate_ref[0] = grad_gate
    dup_ref[0] = grad_up
    back = times_t(grad_gate, gate_ref[...]) + times_t(grad_up, up_ref[...])

    @pl.when(step == 0)
    def _():
        total[...] = back
        scalar[...] = jnp.broadcast_to(gate_part, scalar.shape)

    @pl.when(step > 0)
    def _():
        total[...] += back
        scalar[...] += jnp.broadcast_to(gate_part, scalar.shape)

    @pl.when(step == pl.num_programs(1) - 1)
    def _():
        sources, _, cap, packed_width = back_ref.shape
        back_ref[:, :, :, :width] = (
            total[...].astype(jnp.bfloat16).reshape(sources, 1, cap, width)
        )
        value = scalar[:, 0:1]
        high = value.astype(jnp.bfloat16).astype(jnp.float32)
        low = value - high
        extra = high * mark[0:1] + low * mark[1:2]
        back_ref[:, :, :, width:] = extra.astype(jnp.bfloat16).reshape(
            sources, 1, cap, packed_width - width
        )


def expert_core(packed, w_gate, w_up, raw_grad, marks, units):
    sources, owned, cap, packed_width = packed.shape
    rows = sources * cap
    width = w_gate.shape[0]
    tile = min(units, 512)
    tiles = units // tile
    hidden_shape = jax.ShapeDtypeStruct((owned, rows, units), jnp.bfloat16)
    hidden_spec = pl.BlockSpec((1, rows, tile), lambda l, f: (l, 0, f))
    weight_spec = pl.BlockSpec((width, tile), lambda l, f: (0, l * tiles + f))
    packed_spec = pl.BlockSpec((sources, 1, cap, packed_width), lambda l, f: (0, l, 0, 0))
    return pl.pallas_call(
        expert_kernel,
        grid=(owned, tiles),
        in_specs=[
            packed_spec,
            weight_spec,
            weight_spec,
            hidden_spec,
            pl.BlockSpec((1, 8, packed_width - width), lambda l, f: (l, 0, 0)),
        ],
        out_specs=[packed_spec, hidden_spec, hidden_spec, hidden_spec],
        out_shape=[
            jax.ShapeDtypeStruct(packed.shape, jnp.bfloat16),
            hidden_shape,
            hidden_shape,
            hidden_shape,
        ],
        scratch_shapes=[
            pltpu.VMEM((rows, width), jnp.float32),
            pltpu.VMEM((rows, 128), jnp.float32),
        ],
        compiler_params=kernel_params(),
        cost_estimate=cost(
            8 * owned * rows * units * width, 4 * owned * (rows + 2 * units) * width
        ),
        name="expert_core",
    )(packed, w_gate, w_up, raw_grad, marks)


def expert_out_kernel(*refs):
    *hid_refs, down_ref, out_ref = refs

    for block, hid_ref in enumerate(hid_refs):

        @pl.when(pl.program_id(0) == block)
        def _():
            out = jnp.dot(hid_ref[0], down_ref[...], preferred_element_type=jnp.float32)
            out_ref[...] = out.astype(jnp.bfloat16).reshape(out_ref.shape)


def expert_out(hiddens, w_down, sources):
    count = len(hiddens)
    owned, rows, units = hiddens[0].shape
    width = w_down.shape[1]
    cap = rows // sources
    tile = min(width, 1024)
    return pl.pallas_call(
        expert_out_kernel,
        grid=(count, owned, width // tile),
        in_specs=[pl.BlockSpec((1, rows, units), lambda b, l, d: (l, 0, 0))] * count
        + [pl.BlockSpec((units, tile), lambda b, l, d: (l, d))],
        out_specs=pl.BlockSpec(
            (sources, 1, cap, tile), lambda b, l, d: (0, b * owned + l, 0, d)
        ),
        out_shape=jax.ShapeDtypeStruct((sources, count * owned, cap, width), jnp.bfloat16),
        compiler_params=kernel_params(),
        cost_estimate=cost(
            2 * count * owned * rows * units * width, 2 * count * owned * (rows + units) * width
        ),
        name="expert_out",
    )(*hiddens, w_down)


def in_grads_kernel(count, *refs):
    row_refs, grad_refs, out_ref = refs[:count], refs[count : 2 * count], refs[2 * count]
    rows = grad_refs[0].shape[1]
    total = None
    for row_ref, grad_ref in zip(row_refs, grad_refs):
        part = first_t(row_ref[...].reshape(rows, row_ref.shape[-1]), grad_ref[0])
        total = part if total is None else total + part
    out_ref[...] = total


def in_grads(packed, grads, width):
    count = len(packed)
    sources, owned, cap, _ = packed[0].shape
    _, rows, units = grads[0].shape
    tile = min(width, 512)
    return pl.pallas_call(
        functools.partial(in_grads_kernel, count),
        grid=(owned, width // tile),
        in_specs=[pl.BlockSpec((sources, 1, cap, tile), lambda l, d: (0, l, 0, d))] * count
        + [pl.BlockSpec((1, rows, units), lambda l, d: (l, 0, 0))] * count,
        out_specs=pl.BlockSpec((tile, units), lambda l, d: (d, l)),
        out_shape=jax.ShapeDtypeStruct((width, owned * units), jnp.float32),
        compiler_params=kernel_params(),
        cost_estimate=cost(
            2 * owned * count * rows * units * width, 4 * owned * units * width
        ),
        name="in_grads",
    )(*packed, *grads)


def down_grads_kernel(count, *refs):
    hid_refs, grad_refs = refs[:count], refs[count : 2 * count]
    out_ref = refs[2 * count]
    rows = hid_refs[0].shape[1]
    total = None
    for hid_ref, grad_ref in zip(hid_refs, grad_refs):
        part = first_t(hid_ref[0], grad_ref[...].reshape(rows, grad_ref.shape[-1]))
        total = part if total is None else total + part
    out_ref[...] = total


def down_grads(hiddens, grads):
    count = len(hiddens)
    sources, owned, cap, width = grads[0].shape
    _, rows, units = hiddens[0].shape
    tile = min(units, 256)
    tiles = units // tile
    return pl.pallas_call(
        functools.partial(down_grads_kernel, count),
        grid=(owned, tiles),
        in_specs=[pl.BlockSpec((1, rows, tile), lambda l, f: (l, 0, f))] * count
        + [pl.BlockSpec((sources, 1, cap, width), lambda l, f: (0, l, 0, 0))] * count,
        out_specs=pl.BlockSpec((tile, width), lambda l, f: (l * tiles + f, 0)),
        out_shape=jax.ShapeDtypeStruct((owned * units, width), jnp.float32),
        compiler_params=kernel_params(),
        cost_estimate=cost(
            2 * owned * count * rows * units * width, 4 * owned * units * width
        ),
        name="down_grads",
    )(*hiddens, *grads)


def turn(values, cosines, sines):
    return values * cosines + pltpu.roll(values, values.shape[-1] // 2, 1) * sines


def score_t(keys, queries, key_docs, query_docs, first, factor):
    scores = times_t(keys, queries) * factor
    key_pos = lax.broadcasted_iota(jnp.int32, scores.shape, 0)
    query_pos = first + lax.broadcasted_iota(jnp.int32, scores.shape, 1)
    return jnp.where((key_pos <= query_pos) & (key_docs == query_docs), scores, MASKED)


def attend_kernel(
    block, factor, query_ref, key_ref, value_ref, inv_query_ref, inv_key_ref, query_gain_ref,
    key_gain_ref, cos_ref, sin_ref, doc_col_ref, doc_row_ref, query_out, key_out, value_out,
    attended_ref, log_ref
):
    cosines, sines = cos_ref[...], sin_ref[...]
    queries = turn(query_ref[...] * inv_query_ref[...] * query_gain_ref[...], cosines, sines)
    keys = turn(key_ref[...] * inv_key_ref[...] * key_gain_ref[...], cosines, sines)
    query_out[...] = queries.astype(jnp.bfloat16)
    key_out[...] = keys.astype(jnp.bfloat16)
    value_out[...] = value_ref[...].astype(jnp.bfloat16)
    for first in range(0, query_ref.shape[0], block):
        stop = first + block
        scores = score_t(
            key_out[:stop, :],
            query_out[first:stop, :],
            doc_col_ref[:stop, :],
            doc_row_ref[:, first:stop],
            first,
            factor,
        )
        peak = jnp.max(scores, 0, keepdims=True)
        exps = jnp.exp(scores - peak)
        total = jnp.sum(exps, 0, keepdims=True)
        log_ref[0, :, first:stop] = peak + jnp.log(total)
        weights = (exps * (1.0 / total)).astype(jnp.bfloat16)
        attended_ref[first:stop, :] = first_t(value_out[:stop, :], weights).T.astype(jnp.bfloat16)


def attend(qkv, inv_query, inv_key, query_gain, key_gain, tables, doc_ids, block, factor):
    length = qkv.shape[0]
    head_cols = qkv.shape[1] // 3
    heads = head_cols // HEAD_DIM
    head_spec = pl.BlockSpec((length, HEAD_DIM), lambda h: (0, h))
    gain_spec = pl.BlockSpec((1, HEAD_DIM), lambda h: (0, h))

    def whole(shape):
        return pl.BlockSpec(shape, lambda h: (0, 0))

    out = jax.ShapeDtypeStruct((length, head_cols), jnp.bfloat16)
    return pl.pallas_call(
        functools.partial(attend_kernel, block, factor),
        grid=(heads,),
        in_specs=[
            head_spec,
            pl.BlockSpec((length, HEAD_DIM), lambda h: (0, heads + h)),
            pl.BlockSpec((length, HEAD_DIM), lambda h: (0, 2 * heads + h)),
            whole((length, 1)),
            whole((length, 1)),
            gain_spec,
            gain_spec,
            whole((length, HEAD_DIM)),
            whole((length, HEAD_DIM)),
            whole((length, 1)),
            whole((1, length)),
        ],
        out_specs=[head_spec] * 4 + [pl.BlockSpec((1, 1, length), lambda h: (h, 0, 0))],
        out_shape=[out] * 4 + [jax.ShapeDtypeStruct((heads, 1, length), jnp.float32)],
        compiler_params=kernel_params(),
        cost_estimate=cost(24 * head_cols * length * length, 20 * length * head_cols),
        name="attend",
    )(
        qkv,
        qkv,
        qkv,
        inv_query,
        inv_key,
        query_gain[None, :],
        key_gain[None, :],
        tables[0],
        tables[1],
        doc_ids[:, None],
        doc_ids[None, :],
    )


def attend_back_kernel(
    block, factor, query_ref, key_ref, value_ref, out_grad_ref, log_ref, raw_query_ref,
    raw_key_ref, inv_query_ref, inv_key_ref, query_gain_ref, key_gain_ref, cos_ref, sin_ref,
    doc_col_ref, doc_row_ref, query_out, key_out, value_out, query_sum_ref, key_sum_ref,
    query_gain_out, key_gain_out, query_grad, key_grad, value_grad
):
    key_grad[...] = jnp.zeros(key_grad.shape, jnp.float32)
    value_grad[...] = jnp.zeros(value_grad.shape, jnp.float32)
    for first in range(0, query_ref.shape[0], block):
        stop = first + block
        keys = key_ref[:stop, :]
        queries = query_ref[first:stop, :]
        out_grads = out_grad_ref[first:stop, :]
        scores = score_t(
            keys, queries, doc_col_ref[:stop, :], doc_row_ref[:, first:stop], first, factor
        )
        probs = jnp.exp(scores - log_ref[0, :, first:stop])
        prob_grads = times_t(value_ref[:stop, :], out_grads)
        mean = jnp.sum(probs * prob_grads, 0, keepdims=True)
        score_grads = (probs * (prob_grads - mean)).astype(jnp.bfloat16)
        value_grad[:stop, :] += jnp.dot(
            probs.astype(jnp.bfloat16), out_grads, preferred_element_type=jnp.float32
        )
        key_grad[:stop, :] += jnp.dot(score_grads, queries, preferred_element_type=jnp.float32)
        query_grad[first:stop, :] = first_t(keys, score_grads).T
    cosines, sines = cos_ref[...], -sin_ref[...]
    value_out[...] = value_grad[...].astype(jnp.bfloat16)
    head = pl.program_id(0)
    for grad, raw_ref, inv_ref, gain_ref, out_ref, sum_ref, gain_out in (
        (
            query_grad, raw_query_ref, inv_query_ref, query_gain_ref, query_out, query_sum_ref,
            query_gain_out
        ),
        (key_grad, raw_key_ref, inv_key_ref, key_gain_ref, key_out, key_sum_ref, key_gain_out),
    ):
        norm_grad = turn(grad[...] * factor, cosines, sines)
        raw = raw_ref[...]
        scaled = norm_grad * gain_ref[...]
        out_ref[...] = scaled
        part = jnp.sum(scaled * raw, -1, keepdims=True)
        gain_out[...] = jnp.sum(norm_grad * raw * inv_ref[...], 0, keepdims=True)

        @pl.when(head == 0)
        def _():
            sum_ref[...] = part

        @pl.when(head > 0)
        def _():
            sum_ref[...] += part


def attend_back(
    parts, out_grads, logs, qkv, inv_query, inv_key, query_gain, key_gain, tables, doc_ids, block,
    factor
):
    length = qkv.shape[0]
    head_cols = qkv.shape[1] // 3
    heads = head_cols // HEAD_DIM
    head_spec = pl.BlockSpec((length, HEAD_DIM), lambda h: (0, h))
    gain_spec = pl.BlockSpec((1, HEAD_DIM), lambda h: (0, h))

    def whole(shape):
        return pl.BlockSpec(shape, lambda h: (0, 0))

    wide = jax.ShapeDtypeStruct((length, head_cols), jnp.float32)
    narrow = jax.ShapeDtypeStruct((length, head_cols), jnp.bfloat16)
    column = jax.ShapeDtypeStruct((length, 1), jnp.float32)
    gains = jax.ShapeDtypeStruct((1, head_cols), jnp.float32)
    return pl.pallas_call(
        functools.partial(attend_back_kernel, block, factor),
        grid=(heads,),
        in_specs=[head_spec] * 4
        + [
            pl.BlockSpec((1, 1, length), lambda h: (h, 0, 0)),
            head_spec,
            pl.BlockSpec((length, HEAD_DIM), lambda h: (0, heads + h)),
            whole((length, 1)),
            whole((length, 1)),
            gain_spec,
            gain_spec,
            whole((length, HEAD_DIM)),
            whole((length, HEAD_DIM)),
            whole((length, 1)),
            whole((1, length)),
        ],
        out_specs=[
            head_spec,
            head_spec,
            head_spec,
            whole((length, 1)),
            whole((length, 1)),
            gain_spec,
            gain_spec,
        ],
        out_shape=[wide, wide, narrow, column, column, gains, gains],
        scratch_shapes=[pltpu.VMEM((length, HEAD_DIM), jnp.float32)] * 3,
        compiler_params=kernel_params(),
        cost_estimate=cost(40 * head_cols * length * length, 40 * length * head_cols),
        name="attend_back",
    )(
        *parts,
        out_grads,
        logs,
        qkv,
        qkv,
        inv_query,
        inv_key,
        query_gain[None, :],
        key_gain[None, :],
        tables[0],
        tables[1],
        doc_ids[:, None],
        doc_ids[None, :],
    )


def placings(routes, owners, capacity):
    tok_count = routes.shape[0]
    named = jnp.any(owners[:, None, None] == routes[None, :, :], -1)
    before = (
        jnp.arange(tok_count)[:, None] < jnp.arange(tok_count)[None, :]
    ).astype(jnp.bfloat16)
    slot = jnp.dot(named.astype(jnp.bfloat16), before, preferred_element_type=jnp.float32)
    hit = (slot[:, None, :] == jnp.arange(capacity, dtype=jnp.float32)[None, :, None]) & named[
        :, None, :
    ]
    return hit.astype(jnp.bfloat16).reshape(owners.shape[0] * capacity, tok_count)


def local(
    tokens,
    out_grad,
    segments,
    routes,
    attn_gain,
    ffn_gain,
    query_gain,
    key_gain,
    w_query,
    w_key,
    w_value,
    w_out,
    router,
    w_gate,
    w_up,
    w_down,
):
    rows_total = lax.axis_size("row")
    cols_total = lax.axis_size("col")
    devices = rows_total * cols_total
    place = lax.axis_index("col")
    tok_count, width = tokens.shape
    top_count = routes.shape[1]
    expert_count = router.shape[1]
    capacity = tok_count * top_count * 3 // (expert_count * 2)
    capacity = -(-capacity // 16) * 16
    local_units = w_gate.shape[1]
    ff_units = local_units * devices // expert_count
    units = min(local_units, ff_units)
    owned = local_units // units
    head_cols = w_query.shape[1]
    doc_ids = segments[0]
    length = doc_ids.shape[0]
    block = min(length, 256)
    factor = 1.0 / HEAD_DIM**0.5
    extra = -(-2 * expert_count // 128) * 128

    inputs_f = tokens.astype(jnp.float32)
    inv_first = rms_scale(inputs_f)
    normal_a = (inputs_f * inv_first * attn_gain).astype(jnp.bfloat16)
    wqkv = lax.all_gather(
        jnp.concatenate([w_query, w_key, w_value], 1), "row", axis=0, tiled=True
    )
    wo_full = lax.all_gather(w_out, "row", axis=1, tiled=True)
    a_blocks = ring_blocks(normal_a, "col")
    g_blocks = [out_grad, shift(after(out_grad, a_blocks[-1]), "col")]

    route_blocks = hop_blocks(routes, "col")
    plane_ids = (jnp.arange(rows_total) * cols_total + place)[:, None] * local_units
    owners = ((plane_ids + jnp.arange(owned)[None, :] * units) // ff_units).reshape(-1)
    row_place = lax.axis_index("row")
    my_ids = (
        (row_place * cols_total + place) * local_units + jnp.arange(owned) * units
    ) // ff_units
    extra_ids = jnp.arange(extra)
    marks = jnp.concatenate(
        [
            (extra_ids[None, None, :] == my_ids[:, None, None]).astype(jnp.float32),
            (extra_ids[None, None, :] == my_ids[:, None, None] + expert_count).astype(
                jnp.float32
            ),
            jnp.zeros((owned, 6, extra), jnp.float32),
        ],
        1,
    )
    placed = [placings(block_routes, owners, capacity) for block_routes in route_blocks]

    queue = []

    def in_plane(table, *earlier):
        if queue or earlier:
            table = after(table, *queue[-1:], *earlier)
        queue.append(lax.all_to_all(table, "row", split_axis=0, concat_axis=0, tiled=True))
        return queue[-1]

    def to_experts(values, back, *earlier):
        table = jnp.dot(placed[back], values, preferred_element_type=jnp.float32)
        table = table.astype(jnp.bfloat16).reshape(rows_total, owned, capacity, -1)
        return in_plane(table, *earlier)

    def to_tokens(table, back, *earlier):
        home = in_plane(table, *earlier)
        return first_t(
            placed[back], home.reshape(rows_total * owned * capacity, table.shape[-1])
        )

    g_rows = [to_experts(out_grad, 0)]
    seq_rows = after(natural(a_blocks, place), g_rows[0])
    qkv = jnp.dot(seq_rows, wqkv, preferred_element_type=jnp.float32)
    query_raw = qkv[:, :head_cols]
    key_raw = qkv[:, head_cols : 2 * head_cols]
    squares = exchange_sum(
        jnp.stack([jnp.sum(query_raw * query_raw, -1), jnp.sum(key_raw * key_raw, -1)]), "col"
    )
    squares = after(squares, g_blocks[1])
    g_blocks.append(shift(after(g_blocks[1], squares), "col"))
    inv_query = lax.rsqrt(squares[0] / width + EPSILON)[:, None]
    inv_key = lax.rsqrt(squares[1] / width + EPSILON)[:, None]
    cosines, sine_table = rope_tables(length, HEAD_DIM)
    tables = (
        jnp.concatenate([cosines, cosines], -1),
        jnp.concatenate([-sine_table, sine_table], -1),
    )
    *heads_out, attended, logs = attend(
        qkv, inv_query, inv_key, query_gain, key_gain, tables, doc_ids, block, factor
    )
    g_rows.append(to_experts(after(g_blocks[1], attended), 1))
    raw_grads = [down_t(rows, w_down, units) for rows in g_rows]
    g_rows.append(to_experts(g_blocks[2], 2))
    parts = [
        jnp.dot(
            block_of(attended, place - back, cols_total),
            wo_full,
            preferred_element_type=jnp.float32,
        )
        for back in range(cols_total)
    ]
    parts[2] = after(parts[2], raw_grads[0], g_blocks[2])
    parts[3] = after(parts[3], raw_grads[1])
    parts[0] = after(parts[0], g_rows[2])
    attn = ring_sum(parts, "col")
    residual = inputs_f + attn
    inv_second = rms_scale(residual)
    normal_b = (residual * inv_second * ffn_gain).astype(jnp.bfloat16)
    expert_probs = jax.nn.softmax(
        jnp.dot(normal_b, router, preferred_element_type=jnp.float32), axis=-1
    )

    high, low = split_two(expert_probs)
    packed_b = jnp.concatenate(
        [normal_b, high, low, jnp.zeros((tok_count, extra - 2 * expert_count), jnp.bfloat16)], 1
    )
    b_blocks = [packed_b, shift(packed_b, "col")]
    b_rows = [to_experts(packed_b, 0)]
    raw_grads.append(down_t(g_rows[2], w_down, units))
    core = []

    def run_core():
        back = len(core)
        core.append(expert_core(b_rows[back], w_gate, w_up, raw_grads[back], marks, units))

    b_rows.append(to_experts(after(b_blocks[1], raw_grads[2]), 1))
    run_core()
    for back in range(2, cols_total):
        if back > 2:
            g_blocks.append(shift(after(g_blocks[-1], b_blocks[-1]), "col"))
            b_blocks[-1] = after(b_blocks[-1], g_blocks[-1])
        b_blocks.append(shift(b_blocks[-1], "col"))
        if back > 2:
            g_rows.append(to_experts(after(g_blocks[back], core[-1][1]), back))
            run_core()
            raw_grads.append(down_t(g_rows[back], w_down, units))
        b_rows.append(to_experts(after(b_blocks[back], core[-1][1]), back))
        if back == 2:
            run_core()
    last = cols_total - 1
    share = to_tokens(core[1][0], 1, raw_grads[last], core[-1][1])
    grad_packed = share.astype(jnp.bfloat16)
    run_core()
    hiddens = [part[1] for part in core]
    order = list(range(1, cols_total)) + [0]
    out_groups = [order[:2]] + [[back] for back in order[2:]]

    def expert_outs(group, *earlier):
        first = after(hiddens[group[0]], *earlier)
        return expert_out([first] + [hiddens[b] for b in group[1:]], w_down, rows_total)

    grad_gates = [after(core[0][2], grad_packed)] + [part[2] for part in core[1:]]
    gate_grad = in_grads(b_rows, grad_gates, width)
    outs = [expert_outs(out_groups[0], grad_packed)]
    beside = [hiddens[last]]
    for back in range(2, cols_total):
        share = to_tokens(core[back][0], back, *beside)
        grad_packed = (shift(grad_packed, "col").astype(jnp.float32) + share).astype(
            jnp.bfloat16
        )
        if back == 2:
            grad_ups = [after(core[0][3], grad_packed)] + [part[3] for part in core[1:]]
            up_grad = in_grads(b_rows, grad_ups, width)
        if back < last:
            outs.append(expert_outs(out_groups[back - 1], grad_packed))
            beside = [gate_grad, outs[0]] if back == 2 else [outs[-2]]
    share = to_tokens(core[0][0], 0, up_grad, outs[-1])
    down_grad = down_grads([after(hiddens[0], grad_packed)] + hiddens[1:], g_rows)
    outs += [expert_outs(group, grad_packed) for group in out_groups[len(outs) :]]
    share = after(share, down_grad, *outs)
    grad_packed = shift(grad_packed, "col").astype(jnp.float32) + share

    homes = []

    def outs_home(number):
        home = in_plane(outs[number])
        homes.append(home)
        for slot, back in enumerate(out_groups[number]):
            rows = home[:, slot * owned : (slot + 1) * owned]
            rows = rows.reshape(rows_total * owned * capacity, width)
            out_shares[back] = first_t(placed[back], rows)

    out_shares = {}
    outs_home(0)

    grad_f = out_grad.astype(jnp.float32)
    grad_probs = (
        grad_packed[:, width : width + expert_count]
        + grad_packed[:, width + expert_count : width + 2 * expert_count]
    )
    grad_logits = (
        expert_probs * (grad_probs - jnp.sum(expert_probs * grad_probs, -1, keepdims=True))
    ).astype(jnp.bfloat16)
    grad_normal_b = grad_packed[:, :width] + times_t(grad_logits, router)
    grad_norm_second, ffn_gain_local = norm_back(residual, inv_second, ffn_gain, grad_normal_b)
    grad_residual = grad_f + grad_norm_second
    grad_attn = grad_residual.astype(jnp.bfloat16)
    small = jnp.concatenate(
        [grad_logits]
        + [part.reshape(tok_count, -1) for part in split_two(ffn_gain_local)]
        + [jnp.zeros((tok_count, 128 - expert_count - 2 * width // tok_count), jnp.bfloat16)],
        1,
    )

    grad_blocks = ring_blocks(grad_attn, "col")
    incoming = after(natural(grad_blocks, place), out_shares[1])
    for number in range(1, len(outs)):
        outs_home(number)
    moe = shift(after(out_shares[1].astype(jnp.bfloat16), grad_blocks[-1]), "col")
    wout_local = first_t(incoming, attended).astype(jnp.bfloat16)
    grad_out_heads = times_t(incoming, wo_full).astype(jnp.bfloat16)
    (
        query_scaled,
        key_scaled,
        grad_value_b,
        query_sum,
        key_sum,
        query_gain_local,
        key_gain_local,
    ) = attend_back(
        heads_out,
        grad_out_heads,
        logs,
        qkv,
        inv_query,
        inv_key,
        query_gain,
        key_gain,
        tables,
        doc_ids,
        block,
        factor,
    )
    query_sum = after(query_sum, moe)
    sums = exchange_sum(jnp.stack([query_sum[:, 0], key_sum[:, 0]]), "col")
    moe = (moe.astype(jnp.float32) + out_shares[2]).astype(jnp.bfloat16)
    small_blocks = hop_blocks(after(small, query_sum), "col")
    small_rows = natural(small_blocks, place)
    router_local = first_t(natural(b_blocks, place)[:, :width], small_rows[:, :expert_count])
    gain_width = width // tok_count
    gain_parts = small_rows[:, expert_count : expert_count + 2 * gain_width].astype(jnp.float32)
    gain_parts = gain_parts[:, :gain_width] + gain_parts[:, gain_width:]
    ffn_gain_part = jnp.sum(gain_parts.reshape(cols_total, width), 0)
    early = jnp.concatenate(
        [
            router_local.reshape(rows_total, -1, expert_count),
            ffn_gain_part.reshape(rows_total, -1, expert_count),
        ],
        1,
    )
    early = jnp.sum(in_plane(early), 0)
    grad_query_b = (
        inv_query * query_scaled
        - query_raw * inv_query * inv_query * inv_query * (sums[0] / width)[:, None]
    ).astype(jnp.bfloat16)
    grad_key_b = (
        inv_key * key_scaled - key_raw * inv_key * inv_key * inv_key * (sums[1] / width)[:, None]
    ).astype(jnp.bfloat16)
    grad_qkv = jnp.concatenate([grad_query_b, grad_key_b, grad_value_b], 1)
    grad_qkv = after(grad_qkv, homes[1], *small_blocks[1:])
    da_parts = [
        times_t(block_of(grad_qkv, place - back, cols_total), wqkv) for back in range(cols_total)
    ]
    da_total = da_parts[1].astype(jnp.bfloat16)
    for back in range(2, cols_total):
        da_came = shift(da_total, "col")
        da_total = (da_came.astype(jnp.float32) + da_parts[back]).astype(jnp.bfloat16)
        if back == 2:
            da_second = da_total
        if back == last:
            da_total = after(da_total, early)
    moe = after(moe, da_came)
    for back in order[2:]:
        moe = shift(moe, "col").astype(jnp.float32) + out_shares[back]
        if back:
            moe = moe.astype(jnp.bfloat16)
    output = (residual + moe).astype(jnp.bfloat16)
    grad_normal_a = shift(da_total, "col").astype(jnp.float32) + da_parts[0]
    wqkv_local = first_t(seq_rows, after(grad_qkv, da_second, homes[-1])).astype(jnp.bfloat16)
    attn_gain_local = (
        jnp.sum(wqkv.astype(jnp.float32) * wqkv_local.astype(jnp.float32), -1) / attn_gain
    )
    late = jnp.concatenate([attn_gain_local, query_gain_local[0], key_gain_local[0]])
    late = jnp.concatenate([early.reshape(-1), late]).reshape(1, -1, 128)
    spread = in_plane(jnp.broadcast_to(late, (rows_total,) + late.shape[1:]))
    spread = spread.reshape(rows_total, -1)
    late = jnp.sum(spread[:, early.size :], 0)
    early = spread[:, : early.size].reshape((rows_total,) + early.shape)
    attn_gain_grad = exchange_sum(late[:width], "col", place)

    core_place = row_place % 2

    def over_cores(value):
        halves = value.reshape(rows_total // 2, 2, -1, value.shape[-1])
        other = lax.ppermute(
            lax.dynamic_index_in_dim(halves, 1 - core_place, 1, False),
            "row",
            [(i, i ^ 1) for i in range(rows_total)],
        )
        return (
            lax.dynamic_index_in_dim(halves, core_place, 1, False).astype(jnp.float32) + other
        ).astype(jnp.bfloat16)

    pair = jnp.concatenate([over_cores(wqkv_local), over_cores(wout_local)], -1)
    pair = lax.all_to_all(
        after(pair, queue[-1]),
        "row",
        split_axis=0,
        concat_axis=0,
        tiled=True,
        axis_index_groups=[list(range(core, rows_total, 2)) for core in range(2)],
    )
    weight_grads = jnp.sum(pair.astype(jnp.float32), 0)
    wqkv_grad = weight_grads[:, : 3 * head_cols]
    out_proj_grad = weight_grads[:, 3 * head_cols :].T
    router_grad = early[:, : width // rows_total].reshape(width, expert_count)
    ffn_gain_grad = early[:, width // rows_total :].reshape(width)
    grad_norm_first, _ = norm_back(inputs_f, inv_first, attn_gain, grad_normal_a)
    input_grad = grad_residual + grad_norm_first
    return (
        output,
        input_grad,
        attn_gain_grad,
        ffn_gain_grad,
        late[width : width + head_cols],
        late[width + head_cols :],
        wqkv_grad[:, :head_cols],
        wqkv_grad[:, head_cols : 2 * head_cols],
        wqkv_grad[:, 2 * head_cols :],
        out_proj_grad,
        router_grad,
        gate_grad,
        up_grad,
        down_grad,
    )


def solution(mesh):
    return jax.shard_map(
        local,
        mesh=mesh,
        in_specs=(
            P(("row", "col"), None),
            P(("row", "col"), None),
            P("row", None),
            P(("row", "col"), None),
            P(),
            P(),
            P("col"),
            P("col"),
            P("row", "col"),
            P("row", "col"),
            P("row", "col"),
            P("col", "row"),
            P(),
            P(None, ("row", "col")),
            P(None, ("row", "col")),
            P(("row", "col"), None),
        ),
        out_specs=(
            P(("row", "col"), None),
            P(("row", "col"), None),
            P(),
            P(),
            P("col"),
            P("col"),
            P("row", "col"),
            P("row", "col"),
            P("row", "col"),
            P("col", "row"),
            P(),
            P(None, ("row", "col")),
            P(None, ("row", "col")),
            P(("row", "col"), None),
        ),
        check_vma=False,
    )
```

```python
import functools

import jax
import jax.numpy as jnp
from jax import lax
from jax.experimental import pallas as pl
from jax.experimental.pallas import tpu as pltpu
from jax.sharding import PartitionSpec as P

HEAD_DIM = 128
VMEM_BYTES = 52 * 2**20


EPSILON = 1e-05
ROPE_BASE = 10000.0
MASKED = -1e30


def rms_scale(values):
    return lax.rsqrt(jnp.mean(values * values, -1, keepdims=True) + EPSILON)


def norm_back(values, scale, gain, grad_in):
    scaled_grad = grad_in * gain
    gain_grad = jnp.sum(grad_in * values * scale, 0)
    value_grad = scale * scaled_grad - values * scale * scale * scale * jnp.mean(
        scaled_grad * values, -1, keepdims=True
    )
    return (value_grad, gain_grad)


def times_t(left, right):
    return lax.dot_general(
        left, right, (((1,), (1,)), ((), ())), preferred_element_type=jnp.float32
    )


def rope_tables(length, head_size):
    half = head_size // 2
    freq = jnp.exp(jnp.arange(half, dtype=jnp.float32) * (-2.0 * jnp.log(ROPE_BASE) / head_size))
    angles = jnp.arange(length, dtype=jnp.float32)[:, None] * freq[None, :]
    return (jnp.cos(angles), jnp.sin(angles))


def first_t(left, right):
    return lax.dot_general(
        left, right, (((0,), (0,)), ((), ())), preferred_element_type=jnp.float32
    )


def shift(value, axis, step=1):
    count = lax.axis_size(axis)
    return lax.ppermute(value, axis, [(i, (i + step) % count) for i in range(count)])


def after(value, *earlier):
    return lax.optimization_barrier((value,) + earlier)[0]


def ring_blocks(value, axis, waits=()):
    blocks = [value]
    for hop in range(lax.axis_size(axis) - 1):
        sent = blocks[-1]
        if hop < len(waits):
            sent = after(sent, waits[hop])
        blocks.append(shift(sent, axis))
    return blocks


def hop_blocks(value, axis):
    return [value] + [shift(value, axis, step) for step in range(1, lax.axis_size(axis))]


def ring_sum(parts, axis):
    total = parts[1].astype(jnp.bfloat16)
    for part in parts[2:]:
        total = (shift(total, axis).astype(jnp.float32) + part).astype(jnp.bfloat16)
    return shift(total, axis).astype(jnp.float32) + parts[0]


def exchange_sum(value, axis, place=None):
    parts = [value] + [shift(value, axis, step) for step in range(1, lax.axis_size(axis))]
    if place is None:
        return sum(parts[1:], parts[0])
    return jnp.sum(natural([part[None] for part in parts], place), 0)


def butterfly_sum(value, axis):
    count = lax.axis_size(axis)
    step = 1
    while step < count:
        value = value + lax.ppermute(value, axis, [(i, i ^ step) for i in range(count)])
        step *= 2
    return value


def natural(blocks, place):
    size = blocks[0].shape[0]
    count = len(blocks)
    whole = jnp.zeros((count * size,) + blocks[0].shape[1:], blocks[0].dtype)
    for back, block in enumerate(blocks):
        whole = lax.dynamic_update_slice_in_dim(
            whole, block, ((place - back) % count) * size, 0
        )
    return whole


def block_of(whole, index, count):
    size = whole.shape[0] // count
    return lax.dynamic_slice_in_dim(whole, (index % count) * size, size, 0)


def split_two(values):
    high = lax.reduce_precision(values, 8, 7)
    return high.astype(jnp.bfloat16), (values - high).astype(jnp.bfloat16)


def kernel_params():
    return pltpu.CompilerParams(vmem_limit_bytes=VMEM_BYTES)


def cost(flops, moved):
    return pl.CostEstimate(flops=int(flops), bytes_accessed=int(moved), transcendentals=0)


def down_t_kernel(grad_ref, down_ref, out_ref):
    rows = out_ref.shape[1]
    grads = grad_ref[...].reshape(rows, grad_ref.shape[-1])
    out_ref[0] = times_t(grads, down_ref[...])


def down_t(grads, w_down, units):
    sources, owned, cap, width = grads.shape
    rows = sources * cap
    tile = min(units, 512)
    tiles = units // tile
    return pl.pallas_call(
        down_t_kernel,
        grid=(owned, tiles),
        in_specs=[
            pl.BlockSpec((sources, 1, cap, width), lambda l, f: (0, l, 0, 0)),
            pl.BlockSpec((tile, width), lambda l, f: (l * tiles + f, 0)),
        ],
        out_specs=pl.BlockSpec((1, rows, tile), lambda l, f: (l, 0, f)),
        out_shape=jax.ShapeDtypeStruct((owned, rows, units), jnp.float32),
        compiler_params=kernel_params(),
        cost_estimate=cost(
            2 * owned * rows * units * width, 2 * owned * (rows + units) * width
        ),
        name="down_t",
    )(grads, w_down)


def expert_kernel(
    rows_ref, gate_ref, up_ref, down_grad_ref, mark_ref, back_ref, hid_ref, dgate_ref, dup_ref,
    total, scalar
):
    step = pl.program_id(1)
    rows, width = total.shape
    packed = rows_ref[...].reshape(rows, rows_ref.shape[-1])
    inputs = packed[:, :width]
    mark = mark_ref[0]
    gate = jnp.sum(
        packed[:, width:].astype(jnp.float32) * (mark[0:1] + mark[1:2]), -1, keepdims=True
    )
    gate_pre = jnp.dot(inputs, gate_ref[...], preferred_element_type=jnp.float32)
    up_pre = jnp.dot(inputs, up_ref[...], preferred_element_type=jnp.float32)
    sigmoid = jax.nn.sigmoid(gate_pre)
    active = gate_pre * sigmoid
    hidden = active * up_pre
    raw_grad = down_grad_ref[0]
    gate_part = jnp.sum(hidden * raw_grad, -1, keepdims=True)
    grad_hidden = raw_grad * gate
    grad_gate = (grad_hidden * up_pre * sigmoid * (1.0 + gate_pre * (1.0 - sigmoid))).astype(
        jnp.bfloat16
    )
    grad_up = (grad_hidden * active).astype(jnp.bfloat16)
    hid_ref[0] = (hidden * gate).astype(jnp.bfloat16)
    dgate_ref[0] = grad_gate
    dup_ref[0] = grad_up
    back = times_t(grad_gate, gate_ref[...]) + times_t(grad_up, up_ref[...])

    @pl.when(step == 0)
    def _():
        total[...] = back
        scalar[...] = jnp.broadcast_to(gate_part, scalar.shape)

    @pl.when(step > 0)
    def _():
        total[...] += back
        scalar[...] += jnp.broadcast_to(gate_part, scalar.shape)

    @pl.when(step == pl.num_programs(1) - 1)
    def _():
        sources, _, cap, packed_width = back_ref.shape
        back_ref[:, :, :, :width] = (
            total[...].astype(jnp.bfloat16).reshape(sources, 1, cap, width)
        )
        value = scalar[:, 0:1]
        high = value.astype(jnp.bfloat16).astype(jnp.float32)
        low = value - high
        extra = high * mark[0:1] + low * mark[1:2]
        back_ref[:, :, :, width:] = extra.astype(jnp.bfloat16).reshape(
            sources, 1, cap, packed_width - width
        )


def expert_core(packed, w_gate, w_up, raw_grad, marks, units):
    sources, owned, cap, packed_width = packed.shape
    rows = sources * cap
    width = w_gate.shape[0]
    tile = min(units, 512)
    tiles = units // tile
    hidden_shape = jax.ShapeDtypeStruct((owned, rows, units), jnp.bfloat16)
    hidden_spec = pl.BlockSpec((1, rows, tile), lambda l, f: (l, 0, f))
    weight_spec = pl.BlockSpec((width, tile), lambda l, f: (0, l * tiles + f))
    packed_spec = pl.BlockSpec((sources, 1, cap, packed_width), lambda l, f: (0, l, 0, 0))
    return pl.pallas_call(
        expert_kernel,
        grid=(owned, tiles),
        in_specs=[
            packed_spec,
            weight_spec,
            weight_spec,
            hidden_spec,
            pl.BlockSpec((1, 8, packed_width - width), lambda l, f: (l, 0, 0)),
        ],
        out_specs=[packed_spec, hidden_spec, hidden_spec, hidden_spec],
        out_shape=[
            jax.ShapeDtypeStruct(packed.shape, jnp.bfloat16),
            hidden_shape,
            hidden_shape,
            hidden_shape,
        ],
        scratch_shapes=[
            pltpu.VMEM((rows, width), jnp.float32),
            pltpu.VMEM((rows, 128), jnp.float32),
        ],
        compiler_params=kernel_params(),
        cost_estimate=cost(
            8 * owned * rows * units * width, 4 * owned * (rows + 2 * units) * width
        ),
        name="expert_core",
    )(packed, w_gate, w_up, raw_grad, marks)


def expert_out_kernel(*refs):
    *hid_refs, down_ref, out_ref = refs

    for block, hid_ref in enumerate(hid_refs):

        @pl.when(pl.program_id(0) == block)
        def _():
            out = jnp.dot(hid_ref[0], down_ref[...], preferred_element_type=jnp.float32)
            out_ref[...] = out.astype(jnp.bfloat16).reshape(out_ref.shape)


def expert_out(hiddens, w_down, sources):
    count = len(hiddens)
    owned, rows, units = hiddens[0].shape
    width = w_down.shape[1]
    cap = rows // sources
    tile = min(width, 1024)
    return pl.pallas_call(
        expert_out_kernel,
        grid=(count, owned, width // tile),
        in_specs=[pl.BlockSpec((1, rows, units), lambda b, l, d: (l, 0, 0))] * count
        + [pl.BlockSpec((units, tile), lambda b, l, d: (l, d))],
        out_specs=pl.BlockSpec(
            (sources, 1, cap, tile), lambda b, l, d: (0, b * owned + l, 0, d)
        ),
        out_shape=jax.ShapeDtypeStruct((sources, count * owned, cap, width), jnp.bfloat16),
        compiler_params=kernel_params(),
        cost_estimate=cost(
            2 * count * owned * rows * units * width, 2 * count * owned * (rows + units) * width
        ),
        name="expert_out",
    )(*hiddens, w_down)


def in_grads_kernel(count, *refs):
    row_refs, grad_refs, out_ref = refs[:count], refs[count : 2 * count], refs[2 * count]
    rows = grad_refs[0].shape[1]
    total = None
    for row_ref, grad_ref in zip(row_refs, grad_refs):
        part = first_t(row_ref[...].reshape(rows, row_ref.shape[-1]), grad_ref[0])
        total = part if total is None else total + part
    out_ref[...] = total


def in_grads(packed, grads, width):
    count = len(packed)
    sources, owned, cap, _ = packed[0].shape
    _, rows, units = grads[0].shape
    tile = min(width, 512)
    return pl.pallas_call(
        functools.partial(in_grads_kernel, count),
        grid=(owned, width // tile),
        in_specs=[pl.BlockSpec((sources, 1, cap, tile), lambda l, d: (0, l, 0, d))] * count
        + [pl.BlockSpec((1, rows, units), lambda l, d: (l, 0, 0))] * count,
        out_specs=pl.BlockSpec((tile, units), lambda l, d: (d, l)),
        out_shape=jax.ShapeDtypeStruct((width, owned * units), jnp.float32),
        compiler_params=kernel_params(),
        cost_estimate=cost(
            2 * owned * count * rows * units * width, 4 * owned * units * width
        ),
        name="in_grads",
    )(*packed, *grads)


def down_grads_kernel(count, *refs):
    hid_refs, grad_refs = refs[:count], refs[count : 2 * count]
    out_ref = refs[2 * count]
    rows = hid_refs[0].shape[1]
    total = None
    for hid_ref, grad_ref in zip(hid_refs, grad_refs):
        part = first_t(hid_ref[0], grad_ref[...].reshape(rows, grad_ref.shape[-1]))
        total = part if total is None else total + part
    out_ref[...] = total


def down_grads(hiddens, grads):
    count = len(hiddens)
    sources, owned, cap, width = grads[0].shape
    _, rows, units = hiddens[0].shape
    tile = min(units, 256)
    tiles = units // tile
    return pl.pallas_call(
        functools.partial(down_grads_kernel, count),
        grid=(owned, tiles),
        in_specs=[pl.BlockSpec((1, rows, tile), lambda l, f: (l, 0, f))] * count
        + [pl.BlockSpec((sources, 1, cap, width), lambda l, f: (0, l, 0, 0))] * count,
        out_specs=pl.BlockSpec((tile, width), lambda l, f: (l * tiles + f, 0)),
        out_shape=jax.ShapeDtypeStruct((owned * units, width), jnp.float32),
        compiler_params=kernel_params(),
        cost_estimate=cost(
            2 * owned * count * rows * units * width, 4 * owned * units * width
        ),
        name="down_grads",
    )(*hiddens, *grads)


def turn(values, cosines, sines):
    return values * cosines + pltpu.roll(values, values.shape[-1] // 2, 1) * sines


def score_t(keys, queries, key_docs, query_docs, first, factor):
    scores = times_t(keys, queries) * factor
    key_pos = lax.broadcasted_iota(jnp.int32, scores.shape, 0)
    query_pos = first + lax.broadcasted_iota(jnp.int32, scores.shape, 1)
    return jnp.where((key_pos <= query_pos) & (key_docs == query_docs), scores, MASKED)


def attend_kernel(
    block, factor, query_ref, key_ref, value_ref, inv_query_ref, inv_key_ref, query_gain_ref,
    key_gain_ref, cos_ref, sin_ref, doc_col_ref, doc_row_ref, query_out, key_out, value_out,
    attended_ref, log_ref
):
    cosines, sines = cos_ref[...], sin_ref[...]
    queries = turn(query_ref[...] * inv_query_ref[...] * query_gain_ref[...], cosines, sines)
    keys = turn(key_ref[...] * inv_key_ref[...] * key_gain_ref[...], cosines, sines)
    query_out[...] = queries.astype(jnp.bfloat16)
    key_out[...] = keys.astype(jnp.bfloat16)
    value_out[...] = value_ref[...].astype(jnp.bfloat16)
    for first in range(0, query_ref.shape[0], block):
        stop = first + block
        scores = score_t(
            key_out[:stop, :],
            query_out[first:stop, :],
            doc_col_ref[:stop, :],
            doc_row_ref[:, first:stop],
            first,
            factor,
        )
        peak = jnp.max(scores, 0, keepdims=True)
        exps = jnp.exp(scores - peak)
        total = jnp.sum(exps, 0, keepdims=True)
        log_ref[0, :, first:stop] = peak + jnp.log(total)
        weights = (exps * (1.0 / total)).astype(jnp.bfloat16)
        attended_ref[first:stop, :] = first_t(value_out[:stop, :], weights).T.astype(jnp.bfloat16)


def attend(qkv, inv_query, inv_key, query_gain, key_gain, tables, doc_ids, block, factor):
    length = qkv.shape[0]
    head_cols = qkv.shape[1] // 3
    heads = head_cols // HEAD_DIM
    head_spec = pl.BlockSpec((length, HEAD_DIM), lambda h: (0, h))
    gain_spec = pl.BlockSpec((1, HEAD_DIM), lambda h: (0, h))

    def whole(shape):
        return pl.BlockSpec(shape, lambda h: (0, 0))

    out = jax.ShapeDtypeStruct((length, head_cols), jnp.bfloat16)
    return pl.pallas_call(
        functools.partial(attend_kernel, block, factor),
        grid=(heads,),
        in_specs=[
            head_spec,
            pl.BlockSpec((length, HEAD_DIM), lambda h: (0, heads + h)),
            pl.BlockSpec((length, HEAD_DIM), lambda h: (0, 2 * heads + h)),
            whole((length, 1)),
            whole((length, 1)),
            gain_spec,
            gain_spec,
            whole((length, HEAD_DIM)),
            whole((length, HEAD_DIM)),
            whole((length, 1)),
            whole((1, length)),
        ],
        out_specs=[head_spec] * 4 + [pl.BlockSpec((1, 1, length), lambda h: (h, 0, 0))],
        out_shape=[out] * 4 + [jax.ShapeDtypeStruct((heads, 1, length), jnp.float32)],
        compiler_params=kernel_params(),
        cost_estimate=cost(24 * head_cols * length * length, 20 * length * head_cols),
        name="attend",
    )(
        qkv,
        qkv,
        qkv,
        inv_query,
        inv_key,
        query_gain[None, :],
        key_gain[None, :],
        tables[0],
        tables[1],
        doc_ids[:, None],
        doc_ids[None, :],
    )


def attend_back_kernel(
    block, factor, query_ref, key_ref, value_ref, out_grad_ref, log_ref, raw_query_ref,
    raw_key_ref, inv_query_ref, inv_key_ref, query_gain_ref, key_gain_ref, cos_ref, sin_ref,
    doc_col_ref, doc_row_ref, query_out, key_out, value_out, query_sum_ref, key_sum_ref,
    query_gain_out, key_gain_out, query_grad, key_grad, value_grad
):
    key_grad[...] = jnp.zeros(key_grad.shape, jnp.float32)
    value_grad[...] = jnp.zeros(value_grad.shape, jnp.float32)
    for first in range(0, query_ref.shape[0], block):
        stop = first + block
        keys = key_ref[:stop, :]
        queries = query_ref[first:stop, :]
        out_grads = out_grad_ref[first:stop, :]
        scores = score_t(
            keys, queries, doc_col_ref[:stop, :], doc_row_ref[:, first:stop], first, factor
        )
        probs = jnp.exp(scores - log_ref[0, :, first:stop])
        prob_grads = times_t(value_ref[:stop, :], out_grads)
        mean = jnp.sum(probs * prob_grads, 0, keepdims=True)
        score_grads = (probs * (prob_grads - mean)).astype(jnp.bfloat16)
        value_grad[:stop, :] += jnp.dot(
            probs.astype(jnp.bfloat16), out_grads, preferred_element_type=jnp.float32
        )
        key_grad[:stop, :] += jnp.dot(score_grads, queries, preferred_element_type=jnp.float32)
        query_grad[first:stop, :] = first_t(keys, score_grads).T
    cosines, sines = cos_ref[...], -sin_ref[...]
    value_out[...] = value_grad[...].astype(jnp.bfloat16)
    head = pl.program_id(0)
    for grad, raw_ref, inv_ref, gain_ref, out_ref, sum_ref, gain_out in (
        (
            query_grad, raw_query_ref, inv_query_ref, query_gain_ref, query_out, query_sum_ref,
            query_gain_out
        ),
        (key_grad, raw_key_ref, inv_key_ref, key_gain_ref, key_out, key_sum_ref, key_gain_out),
    ):
        norm_grad = turn(grad[...] * factor, cosines, sines)
        raw = raw_ref[...]
        scaled = norm_grad * gain_ref[...]
        out_ref[...] = scaled
        part = jnp.sum(scaled * raw, -1, keepdims=True)
        gain_out[...] = jnp.sum(norm_grad * raw * inv_ref[...], 0, keepdims=True)

        @pl.when(head == 0)
        def _():
            sum_ref[...] = part

        @pl.when(head > 0)
        def _():
            sum_ref[...] += part


def attend_back(
    parts, out_grads, logs, qkv, inv_query, inv_key, query_gain, key_gain, tables, doc_ids, block,
    factor
):
    length = qkv.shape[0]
    head_cols = qkv.shape[1] // 3
    heads = head_cols // HEAD_DIM
    head_spec = pl.BlockSpec((length, HEAD_DIM), lambda h: (0, h))
    gain_spec = pl.BlockSpec((1, HEAD_DIM), lambda h: (0, h))

    def whole(shape):
        return pl.BlockSpec(shape, lambda h: (0, 0))

    wide = jax.ShapeDtypeStruct((length, head_cols), jnp.float32)
    narrow = jax.ShapeDtypeStruct((length, head_cols), jnp.bfloat16)
    column = jax.ShapeDtypeStruct((length, 1), jnp.float32)
    gains = jax.ShapeDtypeStruct((1, head_cols), jnp.float32)
    return pl.pallas_call(
        functools.partial(attend_back_kernel, block, factor),
        grid=(heads,),
        in_specs=[head_spec] * 4
        + [
            pl.BlockSpec((1, 1, length), lambda h: (h, 0, 0)),
            head_spec,
            pl.BlockSpec((length, HEAD_DIM), lambda h: (0, heads + h)),
            whole((length, 1)),
            whole((length, 1)),
            gain_spec,
            gain_spec,
            whole((length, HEAD_DIM)),
            whole((length, HEAD_DIM)),
            whole((length, 1)),
            whole((1, length)),
        ],
        out_specs=[
            head_spec,
            head_spec,
            head_spec,
            whole((length, 1)),
            whole((length, 1)),
            gain_spec,
            gain_spec,
        ],
        out_shape=[wide, wide, narrow, column, column, gains, gains],
        scratch_shapes=[pltpu.VMEM((length, HEAD_DIM), jnp.float32)] * 3,
        compiler_params=kernel_params(),
        cost_estimate=cost(40 * head_cols * length * length, 40 * length * head_cols),
        name="attend_back",
    )(
        *parts,
        out_grads,
        logs,
        qkv,
        qkv,
        inv_query,
        inv_key,
        query_gain[None, :],
        key_gain[None, :],
        tables[0],
        tables[1],
        doc_ids[:, None],
        doc_ids[None, :],
    )


def placings(routes, owners, capacity):
    tok_count = routes.shape[0]
    named = jnp.any(owners[:, None, None] == routes[None, :, :], -1)
    before = (
        jnp.arange(tok_count)[:, None] < jnp.arange(tok_count)[None, :]
    ).astype(jnp.bfloat16)
    slot = jnp.dot(named.astype(jnp.bfloat16), before, preferred_element_type=jnp.float32)
    hit = (slot[:, None, :] == jnp.arange(capacity, dtype=jnp.float32)[None, :, None]) & named[
        :, None, :
    ]
    return hit.astype(jnp.bfloat16).reshape(owners.shape[0] * capacity, tok_count)


def local(
    tokens,
    out_grad,
    segments,
    routes,
    attn_gain,
    ffn_gain,
    query_gain,
    key_gain,
    w_query,
    w_key,
    w_value,
    w_out,
    router,
    w_gate,
    w_up,
    w_down,
):
    rows_total = lax.axis_size("row")
    cols_total = lax.axis_size("col")
    devices = rows_total * cols_total
    place = lax.axis_index("col")
    tok_count, width = tokens.shape
    top_count = routes.shape[1]
    expert_count = router.shape[1]
    capacity = tok_count * top_count * 3 // (expert_count * 2)
    capacity = -(-capacity // 16) * 16
    local_units = w_gate.shape[1]
    ff_units = local_units * devices // expert_count
    units = min(local_units, ff_units)
    owned = local_units // units
    head_cols = w_query.shape[1]
    doc_ids = segments[0]
    length = doc_ids.shape[0]
    block = min(length, 256)
    factor = 1.0 / HEAD_DIM**0.5
    extra = -(-2 * expert_count // 128) * 128

    inputs_f = tokens.astype(jnp.float32)
    inv_first = rms_scale(inputs_f)
    normal_a = (inputs_f * inv_first * attn_gain).astype(jnp.bfloat16)
    wqkv = lax.all_gather(
        jnp.concatenate([w_query, w_key, w_value], 1), "row", axis=0, tiled=True
    )
    wo_full = lax.all_gather(w_out, "row", axis=1, tiled=True)
    a_blocks = ring_blocks(normal_a, "col")
    g_blocks = [out_grad, shift(after(out_grad, a_blocks[-1]), "col")]

    route_blocks = hop_blocks(routes, "col")
    plane_ids = (jnp.arange(rows_total) * cols_total + place)[:, None] * local_units
    owners = ((plane_ids + jnp.arange(owned)[None, :] * units) // ff_units).reshape(-1)
    row_place = lax.axis_index("row")
    my_ids = (
        (row_place * cols_total + place) * local_units + jnp.arange(owned) * units
    ) // ff_units
    extra_ids = jnp.arange(extra)
    marks = jnp.concatenate(
        [
            (extra_ids[None, None, :] == my_ids[:, None, None]).astype(jnp.float32),
            (extra_ids[None, None, :] == my_ids[:, None, None] + expert_count).astype(
                jnp.float32
            ),
            jnp.zeros((owned, 6, extra), jnp.float32),
        ],
        1,
    )
    placed = [placings(block_routes, owners, capacity) for block_routes in route_blocks]

    queue = []

    def in_plane(table, *earlier):
        if queue or earlier:
            table = after(table, *queue[-1:], *earlier)
        queue.append(lax.all_to_all(table, "row", split_axis=0, concat_axis=0, tiled=True))
        return queue[-1]

    def to_experts(values, back, *earlier):
        table = jnp.dot(placed[back], values, preferred_element_type=jnp.float32)
        table = table.astype(jnp.bfloat16).reshape(rows_total, owned, capacity, -1)
        return in_plane(table, *earlier)

    def to_tokens(table, back, *earlier):
        home = in_plane(table, *earlier)
        return first_t(
            placed[back], home.reshape(rows_total * owned * capacity, table.shape[-1])
        )

    g_rows = [to_experts(out_grad, 0)]
    seq_rows = after(natural(a_blocks, place), g_rows[0])
    qkv = jnp.dot(seq_rows, wqkv, preferred_element_type=jnp.float32)
    query_raw = qkv[:, :head_cols]
    key_raw = qkv[:, head_cols : 2 * head_cols]
    squares = exchange_sum(
        jnp.stack([jnp.sum(query_raw * query_raw, -1), jnp.sum(key_raw * key_raw, -1)]), "col"
    )
    squares = after(squares, g_blocks[1])
    g_blocks.append(shift(after(g_blocks[1], squares), "col"))
    inv_query = lax.rsqrt(squares[0] / width + EPSILON)[:, None]
    inv_key = lax.rsqrt(squares[1] / width + EPSILON)[:, None]
    cosines, sine_table = rope_tables(length, HEAD_DIM)
    tables = (
        jnp.concatenate([cosines, cosines], -1),
        jnp.concatenate([-sine_table, sine_table], -1),
    )
    *heads_out, attended, logs = attend(
        qkv, inv_query, inv_key, query_gain, key_gain, tables, doc_ids, block, factor
    )
    g_rows.append(to_experts(after(g_blocks[1], attended), 1))
    attended = after(attended, g_blocks[2])
    raw_grads = [down_t(rows, w_down, units) for rows in g_rows]
    g_rows.append(to_experts(g_blocks[2], 2))
    parts = [
        jnp.dot(
            block_of(attended, place - back, cols_total),
            wo_full,
            preferred_element_type=jnp.float32,
        )
        for back in range(cols_total)
    ]
    parts[2] = after(parts[2], raw_grads[0])
    parts[3] = after(parts[3], raw_grads[1])
    parts[0] = after(parts[0], g_rows[2])
    attn = ring_sum(parts, "col")
    residual = inputs_f + attn
    inv_second = rms_scale(residual)
    normal_b = (residual * inv_second * ffn_gain).astype(jnp.bfloat16)
    expert_probs = jax.nn.softmax(
        jnp.dot(normal_b, router, preferred_element_type=jnp.float32), axis=-1
    )

    high, low = split_two(expert_probs)
    packed_b = jnp.concatenate(
        [normal_b, high, low, jnp.zeros((tok_count, extra - 2 * expert_count), jnp.bfloat16)], 1
    )
    b_blocks = [packed_b, shift(packed_b, "col")]
    b_rows = [to_experts(packed_b, 0)]
    raw_grads.append(down_t(g_rows[2], w_down, units))
    core = []

    def run_core():
        back = len(core)
        core.append(expert_core(b_rows[back], w_gate, w_up, raw_grads[back], marks, units))

    b_rows.append(to_experts(after(b_blocks[1], raw_grads[2]), 1))
    run_core()
    for back in range(2, cols_total):
        if back > 2:
            g_blocks.append(shift(after(g_blocks[-1], b_blocks[-1]), "col"))
            b_blocks[-1] = after(b_blocks[-1], g_blocks[-1])
        b_blocks.append(shift(b_blocks[-1], "col"))
        if back > 2:
            g_rows.append(to_experts(after(g_blocks[back], core[-1][1]), back))
            run_core()
            raw_grads.append(down_t(g_rows[back], w_down, units))
        b_rows.append(to_experts(after(b_blocks[back], core[-1][1]), back))
        if back == 2:
            run_core()
    last = cols_total - 1
    share = to_tokens(core[1][0], 1, raw_grads[last], core[-1][1])
    grad_packed = share.astype(jnp.bfloat16)
    run_core()
    hiddens = [part[1] for part in core]
    order = list(range(1, cols_total)) + [0]
    out_groups = [order[:2]] + [[back] for back in order[2:]]

    def expert_outs(group, *earlier):
        first = after(hiddens[group[0]], *earlier)
        return expert_out([first] + [hiddens[b] for b in group[1:]], w_down, rows_total)

    grad_gates = [after(core[0][2], grad_packed)] + [part[2] for part in core[1:]]
    gate_grad = in_grads(b_rows, grad_gates, width)
    outs = [expert_outs(out_groups[0], grad_packed)]
    beside = [hiddens[last]]
    for back in range(2, cols_total):
        share = to_tokens(core[back][0], back, *beside)
        grad_packed = (shift(grad_packed, "col").astype(jnp.float32) + share).astype(
            jnp.bfloat16
        )
        if back == 2:
            grad_ups = [after(core[0][3], grad_packed)] + [part[3] for part in core[1:]]
            up_grad = in_grads(b_rows, grad_ups, width)
        if back < last:
            outs.append(expert_outs(out_groups[back - 1], grad_packed))
            beside = [gate_grad, outs[0]] if back == 2 else [outs[-2]]
    share = to_tokens(core[0][0], 0, up_grad, outs[-1])
    down_grad = down_grads([after(hiddens[0], grad_packed)] + hiddens[1:], g_rows)
    outs += [expert_outs(group, grad_packed) for group in out_groups[len(outs) :]]
    share = after(share, down_grad, *outs)
    grad_packed = shift(grad_packed, "col").astype(jnp.float32) + share

    homes = []

    def outs_home(number):
        home = in_plane(outs[number])
        homes.append(home)
        for slot, back in enumerate(out_groups[number]):
            rows = home[:, slot * owned : (slot + 1) * owned]
            rows = rows.reshape(rows_total * owned * capacity, width)
            out_shares[back] = first_t(placed[back], rows)

    out_shares = {}
    outs_home(0)

    grad_f = out_grad.astype(jnp.float32)
    grad_probs = (
        grad_packed[:, width : width + expert_count]
        + grad_packed[:, width + expert_count : width + 2 * expert_count]
    )
    grad_logits = (
        expert_probs * (grad_probs - jnp.sum(expert_probs * grad_probs, -1, keepdims=True))
    ).astype(jnp.bfloat16)
    grad_normal_b = grad_packed[:, :width] + times_t(grad_logits, router)
    grad_norm_second, ffn_gain_local = norm_back(residual, inv_second, ffn_gain, grad_normal_b)
    grad_residual = grad_f + grad_norm_second
    grad_attn = grad_residual.astype(jnp.bfloat16)
    small = jnp.concatenate(
        [grad_logits]
        + [part.reshape(tok_count, -1) for part in split_two(ffn_gain_local)]
        + [jnp.zeros((tok_count, 128 - expert_count - 2 * width // tok_count), jnp.bfloat16)],
        1,
    )

    grad_blocks = ring_blocks(grad_attn, "col")
    grad_out_heads = natural(
        [times_t(block_grad, wo_full).astype(jnp.bfloat16) for block_grad in grad_blocks], place
    )
    grad_out_heads = after(grad_out_heads, out_shares[1])
    for number in range(1, len(outs)):
        outs_home(number)
    moe = shift(after(out_shares[1].astype(jnp.bfloat16), grad_blocks[-1]), "col")
    (
        query_scaled,
        key_scaled,
        grad_value_b,
        query_sum,
        key_sum,
        query_gain_local,
        key_gain_local,
    ) = attend_back(
        heads_out,
        grad_out_heads,
        logs,
        qkv,
        inv_query,
        inv_key,
        query_gain,
        key_gain,
        tables,
        doc_ids,
        block,
        factor,
    )
    wout_local = first_t(
        after(natural(grad_blocks, place), query_sum), attended
    ).astype(jnp.bfloat16)
    query_sum = after(query_sum, moe)
    sums = exchange_sum(jnp.stack([query_sum[:, 0], key_sum[:, 0]]), "col")
    moe = (moe.astype(jnp.float32) + out_shares[2]).astype(jnp.bfloat16)
    small_blocks = hop_blocks(after(small, query_sum), "col")
    small_rows = natural(small_blocks, place)
    router_local = first_t(natural(b_blocks, place)[:, :width], small_rows[:, :expert_count])
    gain_width = width // tok_count
    gain_parts = small_rows[:, expert_count : expert_count + 2 * gain_width].astype(jnp.float32)
    gain_parts = gain_parts[:, :gain_width] + gain_parts[:, gain_width:]
    ffn_gain_part = jnp.sum(gain_parts.reshape(cols_total, width), 0)
    early = jnp.concatenate(
        [
            router_local.reshape(rows_total, -1, expert_count),
            ffn_gain_part.reshape(rows_total, -1, expert_count),
        ],
        1,
    )
    early_table = early
    early = jnp.sum(in_plane(early), 0)
    grad_query_b = (
        inv_query * query_scaled
        - query_raw * inv_query * inv_query * inv_query * (sums[0] / width)[:, None]
    ).astype(jnp.bfloat16)
    grad_key_b = (
        inv_key * key_scaled - key_raw * inv_key * inv_key * inv_key * (sums[1] / width)[:, None]
    ).astype(jnp.bfloat16)
    grad_qkv = jnp.concatenate([grad_query_b, grad_key_b, grad_value_b], 1)
    grad_qkv = after(grad_qkv, homes[1], *small_blocks[1:])
    da_parts = [
        times_t(block_of(grad_qkv, place - back, cols_total), wqkv) for back in range(cols_total)
    ]
    da_total = da_parts[1].astype(jnp.bfloat16)
    wqkv_local = first_t(seq_rows, after(grad_qkv, da_total)).astype(jnp.bfloat16)
    moe = shift(after(moe, sums), "col")
    for back in range(2, cols_total):
        da_came = shift(da_total, "col")
        if back == 2:
            da_came = after(da_came, wqkv_local, early_table, moe)
        da_total = (da_came.astype(jnp.float32) + da_parts[back]).astype(jnp.bfloat16)
        if back == last:
            da_total = after(da_total, early)
    grad_normal_a = shift(da_total, "col").astype(jnp.float32) + da_parts[0]
    for back in order[2:]:
        moe = moe.astype(jnp.float32) + out_shares[back]
        if back:
            moe = shift(moe.astype(jnp.bfloat16), "col")
    output = (residual + moe).astype(jnp.bfloat16)
    attn_gain_local = (
        jnp.sum(wqkv.astype(jnp.float32) * wqkv_local.astype(jnp.float32), -1) / attn_gain
    )
    late = jnp.concatenate([attn_gain_local, query_gain_local[0], key_gain_local[0]])
    late = jnp.concatenate([early.reshape(-1), late]).reshape(1, -1, 128)
    spread = in_plane(jnp.broadcast_to(late, (rows_total,) + late.shape[1:]))
    spread = spread.reshape(rows_total, -1)
    late = jnp.sum(spread[:, early.size :], 0)
    early = spread[:, : early.size].reshape((rows_total,) + early.shape)
    attn_gain_grad = exchange_sum(late[:width], "col", place)

    core_place = row_place % 2

    def over_cores(value):
        halves = value.reshape(rows_total // 2, 2, -1, value.shape[-1])
        other = lax.ppermute(
            lax.dynamic_index_in_dim(halves, 1 - core_place, 1, False),
            "row",
            [(i, i ^ 1) for i in range(rows_total)],
        )
        return (
            lax.dynamic_index_in_dim(halves, core_place, 1, False).astype(jnp.float32) + other
        ).astype(jnp.bfloat16)

    pair = jnp.concatenate([over_cores(wqkv_local), over_cores(wout_local)], -1)
    pair = lax.all_to_all(
        after(pair, queue[-1]),
        "row",
        split_axis=0,
        concat_axis=0,
        tiled=True,
        axis_index_groups=[list(range(core, rows_total, 2)) for core in range(2)],
    )
    weight_grads = jnp.sum(pair.astype(jnp.float32), 0)
    wqkv_grad = weight_grads[:, : 3 * head_cols]
    out_proj_grad = weight_grads[:, 3 * head_cols :].T
    router_grad = early[:, : width // rows_total].reshape(width, expert_count)
    ffn_gain_grad = early[:, width // rows_total :].reshape(width)
    grad_norm_first, _ = norm_back(inputs_f, inv_first, attn_gain, grad_normal_a)
    input_grad = grad_residual + grad_norm_first
    return (
        output,
        input_grad,
        attn_gain_grad,
        ffn_gain_grad,
        late[width : width + head_cols],
        late[width + head_cols :],
        wqkv_grad[:, :head_cols],
        wqkv_grad[:, head_cols : 2 * head_cols],
        wqkv_grad[:, 2 * head_cols :],
        out_proj_grad,
        router_grad,
        gate_grad,
        up_grad,
        down_grad,
    )


def solution(mesh):
    return jax.shard_map(
        local,
        mesh=mesh,
        in_specs=(
            P(("row", "col"), None),
            P(("row", "col"), None),
            P("row", None),
            P(("row", "col"), None),
            P(),
            P(),
            P("col"),
            P("col"),
            P("row", "col"),
            P("row", "col"),
            P("row", "col"),
            P("col", "row"),
            P(),
            P(None, ("row", "col")),
            P(None, ("row", "col")),
            P(("row", "col"), None),
        ),
        out_specs=(
            P(("row", "col"), None),
            P(("row", "col"), None),
            P(),
            P(),
            P("col"),
            P("col"),
            P("row", "col"),
            P("row", "col"),
            P("row", "col"),
            P("col", "row"),
            P(),
            P(None, ("row", "col")),
            P(None, ("row", "col")),
            P(("row", "col"), None),
        ),
        check_vma=False,
    )
```

```python
import functools

import jax
import jax.numpy as jnp
from jax import lax
from jax.experimental import pallas as pl
from jax.experimental.pallas import tpu as pltpu
from jax.sharding import PartitionSpec as P

HEAD_DIM = 128
VMEM_BYTES = 52 * 2**20


EPSILON = 1e-05
ROPE_BASE = 10000.0
MASKED = -1e30


def rms_scale(values):
    return lax.rsqrt(jnp.mean(values * values, -1, keepdims=True) + EPSILON)


def norm_back(values, scale, gain, grad_in):
    scaled_grad = grad_in * gain
    gain_grad = jnp.sum(grad_in * values * scale, 0)
    value_grad = scale * scaled_grad - values * scale * scale * scale * jnp.mean(
        scaled_grad * values, -1, keepdims=True
    )
    return (value_grad, gain_grad)


def times_t(left, right):
    return lax.dot_general(
        left, right, (((1,), (1,)), ((), ())), preferred_element_type=jnp.float32
    )


def rope_tables(length, head_size):
    half = head_size // 2
    freq = jnp.exp(jnp.arange(half, dtype=jnp.float32) * (-2.0 * jnp.log(ROPE_BASE) / head_size))
    angles = jnp.arange(length, dtype=jnp.float32)[:, None] * freq[None, :]
    return (jnp.cos(angles), jnp.sin(angles))


def first_t(left, right):
    return lax.dot_general(
        left, right, (((0,), (0,)), ((), ())), preferred_element_type=jnp.float32
    )


def shift(value, axis, step=1):
    count = lax.axis_size(axis)
    return lax.ppermute(value, axis, [(i, (i + step) % count) for i in range(count)])


def after(value, *earlier):
    return lax.optimization_barrier((value,) + earlier)[0]


def ring_blocks(value, axis, waits=()):
    blocks = [value]
    for hop in range(lax.axis_size(axis) - 1):
        sent = blocks[-1]
        if hop < len(waits):
            sent = after(sent, waits[hop])
        blocks.append(shift(sent, axis))
    return blocks


def hop_blocks(value, axis):
    return [value] + [shift(value, axis, step) for step in range(1, lax.axis_size(axis))]


def ring_sum(parts, axis):
    total = parts[1].astype(jnp.bfloat16)
    for part in parts[2:]:
        total = (shift(total, axis).astype(jnp.float32) + part).astype(jnp.bfloat16)
    return shift(total, axis).astype(jnp.float32) + parts[0]


def exchange_sum(value, axis, place=None):
    parts = [value] + [shift(value, axis, step) for step in range(1, lax.axis_size(axis))]
    if place is None:
        return sum(parts[1:], parts[0])
    return jnp.sum(natural([part[None] for part in parts], place), 0)


def butterfly_sum(value, axis):
    count = lax.axis_size(axis)
    step = 1
    while step < count:
        value = value + lax.ppermute(value, axis, [(i, i ^ step) for i in range(count)])
        step *= 2
    return value


def natural(blocks, place):
    size = blocks[0].shape[0]
    count = len(blocks)
    whole = jnp.zeros((count * size,) + blocks[0].shape[1:], blocks[0].dtype)
    for back, block in enumerate(blocks):
        whole = lax.dynamic_update_slice_in_dim(
            whole, block, ((place - back) % count) * size, 0
        )
    return whole


def block_of(whole, index, count):
    size = whole.shape[0] // count
    return lax.dynamic_slice_in_dim(whole, (index % count) * size, size, 0)


def split_two(values):
    high = lax.reduce_precision(values, 8, 7)
    return high.astype(jnp.bfloat16), (values - high).astype(jnp.bfloat16)


def kernel_params():
    return pltpu.CompilerParams(vmem_limit_bytes=VMEM_BYTES)


def cost(flops, moved):
    return pl.CostEstimate(flops=int(flops), bytes_accessed=int(moved), transcendentals=0)


def down_t_kernel(grad_ref, down_ref, out_ref):
    rows = out_ref.shape[1]
    grads = grad_ref[...].reshape(rows, grad_ref.shape[-1])
    out_ref[0] = times_t(grads, down_ref[...])


def down_t(grads, w_down, units):
    sources, owned, cap, width = grads.shape
    rows = sources * cap
    tile = min(units, 512)
    tiles = units // tile
    return pl.pallas_call(
        down_t_kernel,
        grid=(owned, tiles),
        in_specs=[
            pl.BlockSpec((sources, 1, cap, width), lambda l, f: (0, l, 0, 0)),
            pl.BlockSpec((tile, width), lambda l, f: (l * tiles + f, 0)),
        ],
        out_specs=pl.BlockSpec((1, rows, tile), lambda l, f: (l, 0, f)),
        out_shape=jax.ShapeDtypeStruct((owned, rows, units), jnp.float32),
        compiler_params=kernel_params(),
        cost_estimate=cost(
            2 * owned * rows * units * width, 2 * owned * (rows + units) * width
        ),
        name="down_t",
    )(grads, w_down)


def expert_kernel(
    rows_ref, gate_ref, up_ref, down_grad_ref, mark_ref, back_ref, hid_ref, dgate_ref, dup_ref,
    total, scalar
):
    step = pl.program_id(1)
    rows, width = total.shape
    packed = rows_ref[...].reshape(rows, rows_ref.shape[-1])
    inputs = packed[:, :width]
    mark = mark_ref[0]
    gate = jnp.sum(
        packed[:, width:].astype(jnp.float32) * (mark[0:1] + mark[1:2]), -1, keepdims=True
    )
    gate_pre = jnp.dot(inputs, gate_ref[...], preferred_element_type=jnp.float32)
    up_pre = jnp.dot(inputs, up_ref[...], preferred_element_type=jnp.float32)
    sigmoid = jax.nn.sigmoid(gate_pre)
    active = gate_pre * sigmoid
    hidden = active * up_pre
    raw_grad = down_grad_ref[0]
    gate_part = jnp.sum(hidden * raw_grad, -1, keepdims=True)
    grad_hidden = raw_grad * gate
    grad_gate = (grad_hidden * up_pre * sigmoid * (1.0 + gate_pre * (1.0 - sigmoid))).astype(
        jnp.bfloat16
    )
    grad_up = (grad_hidden * active).astype(jnp.bfloat16)
    hid_ref[0] = (hidden * gate).astype(jnp.bfloat16)
    dgate_ref[0] = grad_gate
    dup_ref[0] = grad_up
    back = times_t(grad_gate, gate_ref[...]) + times_t(grad_up, up_ref[...])

    @pl.when(step == 0)
    def _():
        total[...] = back
        scalar[...] = jnp.broadcast_to(gate_part, scalar.shape)

    @pl.when(step > 0)
    def _():
        total[...] += back
        scalar[...] += jnp.broadcast_to(gate_part, scalar.shape)

    @pl.when(step == pl.num_programs(1) - 1)
    def _():
        sources, _, cap, packed_width = back_ref.shape
        back_ref[:, :, :, :width] = (
            total[...].astype(jnp.bfloat16).reshape(sources, 1, cap, width)
        )
        value = scalar[:, 0:1]
        high = value.astype(jnp.bfloat16).astype(jnp.float32)
        low = value - high
        extra = high * mark[0:1] + low * mark[1:2]
        back_ref[:, :, :, width:] = extra.astype(jnp.bfloat16).reshape(
            sources, 1, cap, packed_width - width
        )


def expert_core(packed, w_gate, w_up, raw_grad, marks, units):
    sources, owned, cap, packed_width = packed.shape
    rows = sources * cap
    width = w_gate.shape[0]
    tile = min(units, 512)
    tiles = units // tile
    hidden_shape = jax.ShapeDtypeStruct((owned, rows, units), jnp.bfloat16)
    hidden_spec = pl.BlockSpec((1, rows, tile), lambda l, f: (l, 0, f))
    weight_spec = pl.BlockSpec((width, tile), lambda l, f: (0, l * tiles + f))
    packed_spec = pl.BlockSpec((sources, 1, cap, packed_width), lambda l, f: (0, l, 0, 0))
    return pl.pallas_call(
        expert_kernel,
        grid=(owned, tiles),
        in_specs=[
            packed_spec,
            weight_spec,
            weight_spec,
            hidden_spec,
            pl.BlockSpec((1, 8, packed_width - width), lambda l, f: (l, 0, 0)),
        ],
        out_specs=[packed_spec, hidden_spec, hidden_spec, hidden_spec],
        out_shape=[
            jax.ShapeDtypeStruct(packed.shape, jnp.bfloat16),
            hidden_shape,
            hidden_shape,
            hidden_shape,
        ],
        scratch_shapes=[
            pltpu.VMEM((rows, width), jnp.float32),
            pltpu.VMEM((rows, 128), jnp.float32),
        ],
        compiler_params=kernel_params(),
        cost_estimate=cost(
            8 * owned * rows * units * width, 4 * owned * (rows + 2 * units) * width
        ),
        name="expert_core",
    )(packed, w_gate, w_up, raw_grad, marks)


def expert_out_kernel(*refs):
    *hid_refs, down_ref, out_ref = refs

    for block, hid_ref in enumerate(hid_refs):

        @pl.when(pl.program_id(0) == block)
        def _():
            out = jnp.dot(hid_ref[0], down_ref[...], preferred_element_type=jnp.float32)
            out_ref[...] = out.astype(jnp.bfloat16).reshape(out_ref.shape)


def expert_out(hiddens, w_down, sources):
    count = len(hiddens)
    owned, rows, units = hiddens[0].shape
    width = w_down.shape[1]
    cap = rows // sources
    tile = min(width, 1024)
    return pl.pallas_call(
        expert_out_kernel,
        grid=(count, owned, width // tile),
        in_specs=[pl.BlockSpec((1, rows, units), lambda b, l, d: (l, 0, 0))] * count
        + [pl.BlockSpec((units, tile), lambda b, l, d: (l, d))],
        out_specs=pl.BlockSpec(
            (sources, 1, cap, tile), lambda b, l, d: (0, b * owned + l, 0, d)
        ),
        out_shape=jax.ShapeDtypeStruct((sources, count * owned, cap, width), jnp.bfloat16),
        compiler_params=kernel_params(),
        cost_estimate=cost(
            2 * count * owned * rows * units * width, 2 * count * owned * (rows + units) * width
        ),
        name="expert_out",
    )(*hiddens, w_down)


def in_grads_kernel(count, *refs):
    row_refs, grad_refs, out_ref = refs[:count], refs[count : 2 * count], refs[2 * count]
    rows = grad_refs[0].shape[1]
    total = None
    for row_ref, grad_ref in zip(row_refs, grad_refs):
        part = first_t(row_ref[...].reshape(rows, row_ref.shape[-1]), grad_ref[0])
        total = part if total is None else total + part
    out_ref[...] = total


def in_grads(packed, grads, width):
    count = len(packed)
    sources, owned, cap, _ = packed[0].shape
    _, rows, units = grads[0].shape
    tile = min(width, 512)
    return pl.pallas_call(
        functools.partial(in_grads_kernel, count),
        grid=(owned, width // tile),
        in_specs=[pl.BlockSpec((sources, 1, cap, tile), lambda l, d: (0, l, 0, d))] * count
        + [pl.BlockSpec((1, rows, units), lambda l, d: (l, 0, 0))] * count,
        out_specs=pl.BlockSpec((tile, units), lambda l, d: (d, l)),
        out_shape=jax.ShapeDtypeStruct((width, owned * units), jnp.float32),
        compiler_params=kernel_params(),
        cost_estimate=cost(
            2 * owned * count * rows * units * width, 4 * owned * units * width
        ),
        name="in_grads",
    )(*packed, *grads)


def down_grads_kernel(count, *refs):
    hid_refs, grad_refs = refs[:count], refs[count : 2 * count]
    out_ref = refs[2 * count]
    rows = hid_refs[0].shape[1]
    total = None
    for hid_ref, grad_ref in zip(hid_refs, grad_refs):
        part = first_t(hid_ref[0], grad_ref[...].reshape(rows, grad_ref.shape[-1]))
        total = part if total is None else total + part
    out_ref[...] = total


def down_grads(hiddens, grads):
    count = len(hiddens)
    sources, owned, cap, width = grads[0].shape
    _, rows, units = hiddens[0].shape
    tile = min(units, 256)
    tiles = units // tile
    return pl.pallas_call(
        functools.partial(down_grads_kernel, count),
        grid=(owned, tiles),
        in_specs=[pl.BlockSpec((1, rows, tile), lambda l, f: (l, 0, f))] * count
        + [pl.BlockSpec((sources, 1, cap, width), lambda l, f: (0, l, 0, 0))] * count,
        out_specs=pl.BlockSpec((tile, width), lambda l, f: (l * tiles + f, 0)),
        out_shape=jax.ShapeDtypeStruct((owned * units, width), jnp.float32),
        compiler_params=kernel_params(),
        cost_estimate=cost(
            2 * owned * count * rows * units * width, 4 * owned * units * width
        ),
        name="down_grads",
    )(*hiddens, *grads)


def turn(values, cosines, sines):
    return values * cosines + pltpu.roll(values, values.shape[-1] // 2, 1) * sines


def score_t(keys, queries, key_docs, query_docs, first, factor):
    scores = times_t(keys, queries) * factor
    key_pos = lax.broadcasted_iota(jnp.int32, scores.shape, 0)
    query_pos = first + lax.broadcasted_iota(jnp.int32, scores.shape, 1)
    return jnp.where((key_pos <= query_pos) & (key_docs == query_docs), scores, MASKED)


def attend_kernel(
    block, factor, query_ref, key_ref, value_ref, inv_query_ref, inv_key_ref, query_gain_ref,
    key_gain_ref, cos_ref, sin_ref, doc_col_ref, doc_row_ref, query_out, key_out, value_out,
    attended_ref, log_ref
):
    cosines, sines = cos_ref[...], sin_ref[...]
    queries = turn(query_ref[...] * inv_query_ref[...] * query_gain_ref[...], cosines, sines)
    keys = turn(key_ref[...] * inv_key_ref[...] * key_gain_ref[...], cosines, sines)
    query_out[...] = queries.astype(jnp.bfloat16)
    key_out[...] = keys.astype(jnp.bfloat16)
    value_out[...] = value_ref[...].astype(jnp.bfloat16)
    for first in range(0, query_ref.shape[0], block):
        stop = first + block
        scores = score_t(
            key_out[:stop, :],
            query_out[first:stop, :],
            doc_col_ref[:stop, :],
            doc_row_ref[:, first:stop],
            first,
            factor,
        )
        peak = jnp.max(scores, 0, keepdims=True)
        exps = jnp.exp(scores - peak)
        total = jnp.sum(exps, 0, keepdims=True)
        log_ref[0, :, first:stop] = peak + jnp.log(total)
        weights = (exps * (1.0 / total)).astype(jnp.bfloat16)
        attended_ref[first:stop, :] = first_t(value_out[:stop, :], weights).T.astype(jnp.bfloat16)


def attend(qkv, inv_query, inv_key, query_gain, key_gain, tables, doc_ids, block, factor):
    length = qkv.shape[0]
    head_cols = qkv.shape[1] // 3
    heads = head_cols // HEAD_DIM
    head_spec = pl.BlockSpec((length, HEAD_DIM), lambda h: (0, h))
    gain_spec = pl.BlockSpec((1, HEAD_DIM), lambda h: (0, h))

    def whole(shape):
        return pl.BlockSpec(shape, lambda h: (0, 0))

    out = jax.ShapeDtypeStruct((length, head_cols), jnp.bfloat16)
    return pl.pallas_call(
        functools.partial(attend_kernel, block, factor),
        grid=(heads,),
        in_specs=[
            head_spec,
            pl.BlockSpec((length, HEAD_DIM), lambda h: (0, heads + h)),
            pl.BlockSpec((length, HEAD_DIM), lambda h: (0, 2 * heads + h)),
            whole((length, 1)),
            whole((length, 1)),
            gain_spec,
            gain_spec,
            whole((length, HEAD_DIM)),
            whole((length, HEAD_DIM)),
            whole((length, 1)),
            whole((1, length)),
        ],
        out_specs=[head_spec] * 4 + [pl.BlockSpec((1, 1, length), lambda h: (h, 0, 0))],
        out_shape=[out] * 4 + [jax.ShapeDtypeStruct((heads, 1, length), jnp.float32)],
        compiler_params=kernel_params(),
        cost_estimate=cost(24 * head_cols * length * length, 20 * length * head_cols),
        name="attend",
    )(
        qkv,
        qkv,
        qkv,
        inv_query,
        inv_key,
        query_gain[None, :],
        key_gain[None, :],
        tables[0],
        tables[1],
        doc_ids[:, None],
        doc_ids[None, :],
    )


def attend_back_kernel(
    block, factor, query_ref, key_ref, value_ref, out_grad_ref, log_ref, raw_query_ref,
    raw_key_ref, inv_query_ref, inv_key_ref, query_gain_ref, key_gain_ref, cos_ref, sin_ref,
    doc_col_ref, doc_row_ref, query_out, key_out, value_out, query_sum_ref, key_sum_ref,
    query_gain_out, key_gain_out, query_grad, key_grad, value_grad
):
    key_grad[...] = jnp.zeros(key_grad.shape, jnp.float32)
    value_grad[...] = jnp.zeros(value_grad.shape, jnp.float32)
    for first in range(0, query_ref.shape[0], block):
        stop = first + block
        keys = key_ref[:stop, :]
        queries = query_ref[first:stop, :]
        out_grads = out_grad_ref[first:stop, :]
        scores = score_t(
            keys, queries, doc_col_ref[:stop, :], doc_row_ref[:, first:stop], first, factor
        )
        probs = jnp.exp(scores - log_ref[0, :, first:stop])
        prob_grads = times_t(value_ref[:stop, :], out_grads)
        mean = jnp.sum(probs * prob_grads, 0, keepdims=True)
        score_grads = (probs * (prob_grads - mean)).astype(jnp.bfloat16)
        value_grad[:stop, :] += jnp.dot(
            probs.astype(jnp.bfloat16), out_grads, preferred_element_type=jnp.float32
        )
        key_grad[:stop, :] += jnp.dot(score_grads, queries, preferred_element_type=jnp.float32)
        query_grad[first:stop, :] = first_t(keys, score_grads).T
    cosines, sines = cos_ref[...], -sin_ref[...]
    value_out[...] = value_grad[...].astype(jnp.bfloat16)
    head = pl.program_id(0)
    for grad, raw_ref, inv_ref, gain_ref, out_ref, sum_ref, gain_out in (
        (
            query_grad, raw_query_ref, inv_query_ref, query_gain_ref, query_out, query_sum_ref,
            query_gain_out
        ),
        (key_grad, raw_key_ref, inv_key_ref, key_gain_ref, key_out, key_sum_ref, key_gain_out),
    ):
        norm_grad = turn(grad[...] * factor, cosines, sines)
        raw = raw_ref[...]
        scaled = norm_grad * gain_ref[...]
        out_ref[...] = scaled
        part = jnp.sum(scaled * raw, -1, keepdims=True)
        gain_out[...] = jnp.sum(norm_grad * raw * inv_ref[...], 0, keepdims=True)

        @pl.when(head == 0)
        def _():
            sum_ref[...] = part

        @pl.when(head > 0)
        def _():
            sum_ref[...] += part


def attend_back(
    parts, out_grads, logs, qkv, inv_query, inv_key, query_gain, key_gain, tables, doc_ids, block,
    factor
):
    length = qkv.shape[0]
    head_cols = qkv.shape[1] // 3
    heads = head_cols // HEAD_DIM
    head_spec = pl.BlockSpec((length, HEAD_DIM), lambda h: (0, h))
    gain_spec = pl.BlockSpec((1, HEAD_DIM), lambda h: (0, h))

    def whole(shape):
        return pl.BlockSpec(shape, lambda h: (0, 0))

    wide = jax.ShapeDtypeStruct((length, head_cols), jnp.float32)
    narrow = jax.ShapeDtypeStruct((length, head_cols), jnp.bfloat16)
    column = jax.ShapeDtypeStruct((length, 1), jnp.float32)
    gains = jax.ShapeDtypeStruct((1, head_cols), jnp.float32)
    return pl.pallas_call(
        functools.partial(attend_back_kernel, block, factor),
        grid=(heads,),
        in_specs=[head_spec] * 4
        + [
            pl.BlockSpec((1, 1, length), lambda h: (h, 0, 0)),
            head_spec,
            pl.BlockSpec((length, HEAD_DIM), lambda h: (0, heads + h)),
            whole((length, 1)),
            whole((length, 1)),
            gain_spec,
            gain_spec,
            whole((length, HEAD_DIM)),
            whole((length, HEAD_DIM)),
            whole((length, 1)),
            whole((1, length)),
        ],
        out_specs=[
            head_spec,
            head_spec,
            head_spec,
            whole((length, 1)),
            whole((length, 1)),
            gain_spec,
            gain_spec,
        ],
        out_shape=[wide, wide, narrow, column, column, gains, gains],
        scratch_shapes=[pltpu.VMEM((length, HEAD_DIM), jnp.float32)] * 3,
        compiler_params=kernel_params(),
        cost_estimate=cost(40 * head_cols * length * length, 40 * length * head_cols),
        name="attend_back",
    )(
        *parts,
        out_grads,
        logs,
        qkv,
        qkv,
        inv_query,
        inv_key,
        query_gain[None, :],
        key_gain[None, :],
        tables[0],
        tables[1],
        doc_ids[:, None],
        doc_ids[None, :],
    )


def placings(routes, owners, capacity):
    tok_count = routes.shape[0]
    named = jnp.any(owners[:, None, None] == routes[None, :, :], -1)
    before = (
        jnp.arange(tok_count)[:, None] < jnp.arange(tok_count)[None, :]
    ).astype(jnp.bfloat16)
    slot = jnp.dot(named.astype(jnp.bfloat16), before, preferred_element_type=jnp.float32)
    hit = (slot[:, None, :] == jnp.arange(capacity, dtype=jnp.float32)[None, :, None]) & named[
        :, None, :
    ]
    return hit.astype(jnp.bfloat16).reshape(owners.shape[0] * capacity, tok_count)


def local(
    tokens,
    out_grad,
    segments,
    routes,
    attn_gain,
    ffn_gain,
    query_gain,
    key_gain,
    w_query,
    w_key,
    w_value,
    w_out,
    router,
    w_gate,
    w_up,
    w_down,
):
    rows_total = lax.axis_size("row")
    cols_total = lax.axis_size("col")
    devices = rows_total * cols_total
    place = lax.axis_index("col")
    tok_count, width = tokens.shape
    top_count = routes.shape[1]
    expert_count = router.shape[1]
    capacity = tok_count * top_count * 3 // (expert_count * 2)
    capacity = -(-capacity // 16) * 16
    local_units = w_gate.shape[1]
    ff_units = local_units * devices // expert_count
    units = min(local_units, ff_units)
    owned = local_units // units
    head_cols = w_query.shape[1]
    doc_ids = segments[0]
    length = doc_ids.shape[0]
    block = min(length, 256)
    factor = 1.0 / HEAD_DIM**0.5
    extra = -(-2 * expert_count // 128) * 128

    inputs_f = tokens.astype(jnp.float32)
    inv_first = rms_scale(inputs_f)
    normal_a = (inputs_f * inv_first * attn_gain).astype(jnp.bfloat16)
    wqkv = lax.all_gather(
        jnp.concatenate([w_query, w_key, w_value], 1), "row", axis=0, tiled=True
    )
    wo_full = lax.all_gather(w_out, "row", axis=1, tiled=True)
    a_blocks = ring_blocks(normal_a, "col")
    g_blocks = [out_grad, shift(after(out_grad, a_blocks[-1]), "col")]

    route_blocks = hop_blocks(routes, "col")
    plane_ids = (jnp.arange(rows_total) * cols_total + place)[:, None] * local_units
    owners = ((plane_ids + jnp.arange(owned)[None, :] * units) // ff_units).reshape(-1)
    row_place = lax.axis_index("row")
    my_ids = (
        (row_place * cols_total + place) * local_units + jnp.arange(owned) * units
    ) // ff_units
    extra_ids = jnp.arange(extra)
    marks = jnp.concatenate(
        [
            (extra_ids[None, None, :] == my_ids[:, None, None]).astype(jnp.float32),
            (extra_ids[None, None, :] == my_ids[:, None, None] + expert_count).astype(
                jnp.float32
            ),
            jnp.zeros((owned, 6, extra), jnp.float32),
        ],
        1,
    )
    placed = [placings(block_routes, owners, capacity) for block_routes in route_blocks]

    queue = []

    def in_plane(table, *earlier):
        if queue or earlier:
            table = after(table, *queue[-1:], *earlier)
        queue.append(lax.all_to_all(table, "row", split_axis=0, concat_axis=0, tiled=True))
        return queue[-1]

    def to_experts(values, back, *earlier):
        table = jnp.dot(placed[back], values, preferred_element_type=jnp.float32)
        table = table.astype(jnp.bfloat16).reshape(rows_total, owned, capacity, -1)
        return in_plane(table, *earlier)

    def to_tokens(table, back, *earlier):
        home = in_plane(table, *earlier)
        return first_t(
            placed[back], home.reshape(rows_total * owned * capacity, table.shape[-1])
        )

    g_rows = [to_experts(out_grad, 0)]
    seq_rows = after(natural(a_blocks, place), g_rows[0])
    qkv = jnp.dot(seq_rows, wqkv, preferred_element_type=jnp.float32)
    query_raw = qkv[:, :head_cols]
    key_raw = qkv[:, head_cols : 2 * head_cols]
    squares = exchange_sum(
        jnp.stack([jnp.sum(query_raw * query_raw, -1), jnp.sum(key_raw * key_raw, -1)]), "col"
    )
    g_blocks.append(shift(after(g_blocks[1], squares), "col"))
    g_rows.append(to_experts(after(g_blocks[1], qkv), 1))
    inv_query = lax.rsqrt(squares[0] / width + EPSILON)[:, None]
    inv_key = lax.rsqrt(squares[1] / width + EPSILON)[:, None]
    cosines, sine_table = rope_tables(length, HEAD_DIM)
    tables = (
        jnp.concatenate([cosines, cosines], -1),
        jnp.concatenate([-sine_table, sine_table], -1),
    )
    *heads_out, attended, logs = attend(
        qkv, inv_query, inv_key, query_gain, key_gain, tables, doc_ids, block, factor
    )
    attended = after(attended, g_blocks[2])
    raw_grads = [down_t(rows, w_down, units) for rows in g_rows]
    g_rows.append(to_experts(g_blocks[2], 2))
    parts = [
        jnp.dot(
            block_of(attended, place - back, cols_total),
            wo_full,
            preferred_element_type=jnp.float32,
        )
        for back in range(cols_total)
    ]
    parts[2] = after(parts[2], raw_grads[0])
    parts[3] = after(parts[3], raw_grads[1])
    parts[0] = after(parts[0], g_rows[2])
    attn = ring_sum(parts, "col")
    residual = inputs_f + attn
    inv_second = rms_scale(residual)
    normal_b = (residual * inv_second * ffn_gain).astype(jnp.bfloat16)
    expert_probs = jax.nn.softmax(
        jnp.dot(normal_b, router, preferred_element_type=jnp.float32), axis=-1
    )

    high, low = split_two(expert_probs)
    packed_b = jnp.concatenate(
        [normal_b, high, low, jnp.zeros((tok_count, extra - 2 * expert_count), jnp.bfloat16)], 1
    )
    b_blocks = [packed_b, shift(packed_b, "col")]
    b_rows = [to_experts(packed_b, 0)]
    raw_grads.append(down_t(g_rows[2], w_down, units))
    core = []

    def run_core():
        back = len(core)
        core.append(expert_core(b_rows[back], w_gate, w_up, raw_grads[back], marks, units))

    b_rows.append(to_experts(after(b_blocks[1], raw_grads[2]), 1))
    run_core()
    for back in range(2, cols_total):
        if back > 2:
            g_blocks.append(shift(after(g_blocks[-1], b_blocks[-1]), "col"))
            b_blocks[-1] = after(b_blocks[-1], g_blocks[-1])
        b_blocks.append(shift(b_blocks[-1], "col"))
        if back > 2:
            g_rows.append(to_experts(after(g_blocks[back], core[-1][1]), back))
            run_core()
            raw_grads.append(down_t(g_rows[back], w_down, units))
        b_rows.append(to_experts(after(b_blocks[back], core[-1][1]), back))
        if back == 2:
            run_core()
    last = cols_total - 1
    share = to_tokens(core[1][0], 1, raw_grads[last], core[-1][1])
    grad_packed = share.astype(jnp.bfloat16)
    run_core()
    hiddens = [part[1] for part in core]
    order = list(range(1, cols_total)) + [0]
    out_groups = [order[:2]] + [[back] for back in order[2:]]

    def expert_outs(group, *earlier):
        first = after(hiddens[group[0]], *earlier)
        return expert_out([first] + [hiddens[b] for b in group[1:]], w_down, rows_total)

    grad_gates = [after(core[0][2], grad_packed)] + [part[2] for part in core[1:]]
    gate_grad = in_grads(b_rows, grad_gates, width)
    outs = [expert_outs(out_groups[0], grad_packed)]
    beside = [hiddens[last]]
    for back in range(2, cols_total):
        share = to_tokens(core[back][0], back, *beside)
        grad_packed = (shift(grad_packed, "col").astype(jnp.float32) + share).astype(
            jnp.bfloat16
        )
        if back == 2:
            grad_ups = [after(core[0][3], grad_packed)] + [part[3] for part in core[1:]]
            up_grad = in_grads(b_rows, grad_ups, width)
        if back < last:
            outs.append(expert_outs(out_groups[back - 1], grad_packed))
            beside = [gate_grad, outs[0]] if back == 2 else [outs[-2]]
    share = to_tokens(core[0][0], 0, up_grad, outs[-1])
    down_grad = down_grads([after(hiddens[0], grad_packed)] + hiddens[1:], g_rows)
    outs += [expert_outs(group, grad_packed) for group in out_groups[len(outs) :]]
    share = after(share, down_grad, *outs)
    grad_packed = shift(grad_packed, "col").astype(jnp.float32) + share

    homes = []

    def outs_home(number):
        home = in_plane(outs[number])
        homes.append(home)
        for slot, back in enumerate(out_groups[number]):
            rows = home[:, slot * owned : (slot + 1) * owned]
            rows = rows.reshape(rows_total * owned * capacity, width)
            out_shares[back] = first_t(placed[back], rows)

    out_shares = {}
    outs_home(0)

    grad_f = out_grad.astype(jnp.float32)
    grad_probs = (
        grad_packed[:, width : width + expert_count]
        + grad_packed[:, width + expert_count : width + 2 * expert_count]
    )
    grad_logits = (
        expert_probs * (grad_probs - jnp.sum(expert_probs * grad_probs, -1, keepdims=True))
    ).astype(jnp.bfloat16)
    grad_normal_b = grad_packed[:, :width] + times_t(grad_logits, router)
    grad_norm_second, ffn_gain_local = norm_back(residual, inv_second, ffn_gain, grad_normal_b)
    grad_residual = grad_f + grad_norm_second
    grad_attn = grad_residual.astype(jnp.bfloat16)
    small = jnp.concatenate(
        [grad_logits]
        + [part.reshape(tok_count, -1) for part in split_two(ffn_gain_local)]
        + [jnp.zeros((tok_count, 128 - expert_count - 2 * width // tok_count), jnp.bfloat16)],
        1,
    )

    grad_blocks = ring_blocks(grad_attn, "col")
    grad_out_heads = natural(
        [times_t(block_grad, wo_full).astype(jnp.bfloat16) for block_grad in grad_blocks], place
    )
    grad_out_heads = after(grad_out_heads, out_shares[1])
    for number in range(1, len(outs)):
        outs_home(number)
    moe = shift(after(out_shares[1].astype(jnp.bfloat16), grad_blocks[-1]), "col")
    (
        query_scaled,
        key_scaled,
        grad_value_b,
        query_sum,
        key_sum,
        query_gain_local,
        key_gain_local,
    ) = attend_back(
        heads_out,
        grad_out_heads,
        logs,
        qkv,
        inv_query,
        inv_key,
        query_gain,
        key_gain,
        tables,
        doc_ids,
        block,
        factor,
    )
    query_sum = after(query_sum, moe)
    sums = exchange_sum(jnp.stack([query_sum[:, 0], key_sum[:, 0]]), "col")
    moe = (moe.astype(jnp.float32) + out_shares[2]).astype(jnp.bfloat16)
    small_blocks = hop_blocks(after(small, query_sum), "col")
    small_rows = natural(small_blocks, place)
    router_local = first_t(natural(b_blocks, place)[:, :width], small_rows[:, :expert_count])
    gain_width = width // tok_count
    gain_parts = small_rows[:, expert_count : expert_count + 2 * gain_width].astype(jnp.float32)
    gain_parts = gain_parts[:, :gain_width] + gain_parts[:, gain_width:]
    ffn_gain_part = jnp.sum(gain_parts.reshape(cols_total, width), 0)
    early = jnp.concatenate(
        [
            router_local.reshape(rows_total, -1, expert_count),
            ffn_gain_part.reshape(rows_total, -1, expert_count),
        ],
        1,
    )
    early_table = early
    early = jnp.sum(in_plane(early), 0)
    grad_query_b = (
        inv_query * query_scaled
        - query_raw * inv_query * inv_query * inv_query * (sums[0] / width)[:, None]
    ).astype(jnp.bfloat16)
    grad_key_b = (
        inv_key * key_scaled - key_raw * inv_key * inv_key * inv_key * (sums[1] / width)[:, None]
    ).astype(jnp.bfloat16)
    grad_qkv = jnp.concatenate([grad_query_b, grad_key_b, grad_value_b], 1)
    grad_qkv = after(grad_qkv, homes[1], *small_blocks[1:])
    da_parts = [
        times_t(block_of(grad_qkv, place - back, cols_total), wqkv) for back in range(cols_total)
    ]
    da_total = da_parts[1].astype(jnp.bfloat16)
    incoming = natural([after(grad_blocks[0], da_total)] + grad_blocks[1:], place)
    wout_local = first_t(incoming, attended).astype(jnp.bfloat16)
    for back in range(2, cols_total):
        da_came = shift(da_total, "col")
        if back == 2:
            da_came = after(da_came, early_table, wout_local)
        da_total = (da_came.astype(jnp.float32) + da_parts[back]).astype(jnp.bfloat16)
        if back == 2:
            da_second = da_total
    moe = after(moe, da_came)
    for back in order[2:]:
        moe = shift(moe, "col").astype(jnp.float32) + out_shares[back]
        if back:
            moe = moe.astype(jnp.bfloat16)
    output = (residual + moe).astype(jnp.bfloat16)
    grad_normal_a = shift(da_total, "col").astype(jnp.float32) + da_parts[0]
    wqkv_local = first_t(seq_rows, after(grad_qkv, da_second, early)).astype(jnp.bfloat16)
    attn_gain_local = (
        jnp.sum(wqkv.astype(jnp.float32) * wqkv_local.astype(jnp.float32), -1) / attn_gain
    )
    late = jnp.concatenate([attn_gain_local, query_gain_local[0], key_gain_local[0]])
    late = jnp.concatenate([early.reshape(-1), late]).reshape(1, -1, 128)
    spread = in_plane(jnp.broadcast_to(late, (rows_total,) + late.shape[1:]))
    spread = spread.reshape(rows_total, -1)
    late = jnp.sum(spread[:, early.size :], 0)
    early = spread[:, : early.size].reshape((rows_total,) + early.shape)
    attn_gain_grad = exchange_sum(late[:width], "col", place)

    core_place = row_place % 2

    def over_cores(value):
        halves = value.reshape(rows_total // 2, 2, -1, value.shape[-1])
        other = lax.ppermute(
            lax.dynamic_index_in_dim(halves, 1 - core_place, 1, False),
            "row",
            [(i, i ^ 1) for i in range(rows_total)],
        )
        return (
            lax.dynamic_index_in_dim(halves, core_place, 1, False).astype(jnp.float32) + other
        ).astype(jnp.bfloat16)

    pair = jnp.concatenate([over_cores(wqkv_local), over_cores(wout_local)], -1)
    pair = lax.all_to_all(
        after(pair, queue[-1]),
        "row",
        split_axis=0,
        concat_axis=0,
        tiled=True,
        axis_index_groups=[list(range(core, rows_total, 2)) for core in range(2)],
    )
    weight_grads = jnp.sum(pair.astype(jnp.float32), 0)
    wqkv_grad = weight_grads[:, : 3 * head_cols]
    out_proj_grad = weight_grads[:, 3 * head_cols :].T
    router_grad = early[:, : width // rows_total].reshape(width, expert_count)
    ffn_gain_grad = early[:, width // rows_total :].reshape(width)
    grad_norm_first, _ = norm_back(inputs_f, inv_first, attn_gain, grad_normal_a)
    input_grad = grad_residual + grad_norm_first
    return (
        output,
        input_grad,
        attn_gain_grad,
        ffn_gain_grad,
        late[width : width + head_cols],
        late[width + head_cols :],
        wqkv_grad[:, :head_cols],
        wqkv_grad[:, head_cols : 2 * head_cols],
        wqkv_grad[:, 2 * head_cols :],
        out_proj_grad,
        router_grad,
        gate_grad,
        up_grad,
        down_grad,
    )


def solution(mesh):
    return jax.shard_map(
        local,
        mesh=mesh,
        in_specs=(
            P(("row", "col"), None),
            P(("row", "col"), None),
            P("row", None),
            P(("row", "col"), None),
            P(),
            P(),
            P("col"),
            P("col"),
            P("row", "col"),
            P("row", "col"),
            P("row", "col"),
            P("col", "row"),
            P(),
            P(None, ("row", "col")),
            P(None, ("row", "col")),
            P(("row", "col"), None),
        ),
        out_specs=(
            P(("row", "col"), None),
            P(("row", "col"), None),
            P(),
            P(),
            P("col"),
            P("col"),
            P("row", "col"),
            P("row", "col"),
            P("row", "col"),
            P("col", "row"),
            P(),
            P(None, ("row", "col")),
            P(None, ("row", "col")),
            P(("row", "col"), None),
        ),
        check_vma=False,
    )
```

```python
import functools

import jax
import jax.numpy as jnp
from jax import lax
from jax.experimental import pallas as pl
from jax.experimental.pallas import tpu as pltpu
from jax.sharding import PartitionSpec as P

HEAD_DIM = 128
VMEM_BYTES = 52 * 2**20


EPSILON = 1e-05
ROPE_BASE = 10000.0
MASKED = -1e30


def rms_scale(values):
    return lax.rsqrt(jnp.mean(values * values, -1, keepdims=True) + EPSILON)


def norm_back(values, scale, gain, grad_in):
    scaled_grad = grad_in * gain
    gain_grad = jnp.sum(grad_in * values * scale, 0)
    value_grad = scale * scaled_grad - values * scale * scale * scale * jnp.mean(
        scaled_grad * values, -1, keepdims=True
    )
    return (value_grad, gain_grad)


def times_t(left, right):
    return lax.dot_general(
        left, right, (((1,), (1,)), ((), ())), preferred_element_type=jnp.float32
    )


def rope_tables(length, head_size):
    half = head_size // 2
    freq = jnp.exp(jnp.arange(half, dtype=jnp.float32) * (-2.0 * jnp.log(ROPE_BASE) / head_size))
    angles = jnp.arange(length, dtype=jnp.float32)[:, None] * freq[None, :]
    return (jnp.cos(angles), jnp.sin(angles))


def first_t(left, right):
    return lax.dot_general(
        left, right, (((0,), (0,)), ((), ())), preferred_element_type=jnp.float32
    )


def shift(value, axis, step=1):
    count = lax.axis_size(axis)
    return lax.ppermute(value, axis, [(i, (i + step) % count) for i in range(count)])


def after(value, *earlier):
    return lax.optimization_barrier((value,) + earlier)[0]


def ring_blocks(value, axis, waits=()):
    blocks = [value]
    for hop in range(lax.axis_size(axis) - 1):
        sent = blocks[-1]
        if hop < len(waits):
            sent = after(sent, waits[hop])
        blocks.append(shift(sent, axis))
    return blocks


def hop_blocks(value, axis):
    return [value] + [shift(value, axis, step) for step in range(1, lax.axis_size(axis))]


def ring_sum(parts, axis):
    total = parts[1].astype(jnp.bfloat16)
    for part in parts[2:]:
        total = (shift(total, axis).astype(jnp.float32) + part).astype(jnp.bfloat16)
    return shift(total, axis).astype(jnp.float32) + parts[0]


def exchange_sum(value, axis, place=None):
    parts = [value] + [shift(value, axis, step) for step in range(1, lax.axis_size(axis))]
    if place is None:
        return sum(parts[1:], parts[0])
    return jnp.sum(natural([part[None] for part in parts], place), 0)


def butterfly_sum(value, axis):
    count = lax.axis_size(axis)
    step = 1
    while step < count:
        value = value + lax.ppermute(value, axis, [(i, i ^ step) for i in range(count)])
        step *= 2
    return value


def natural(blocks, place):
    size = blocks[0].shape[0]
    count = len(blocks)
    whole = jnp.zeros((count * size,) + blocks[0].shape[1:], blocks[0].dtype)
    for back, block in enumerate(blocks):
        whole = lax.dynamic_update_slice_in_dim(
            whole, block, ((place - back) % count) * size, 0
        )
    return whole


def block_of(whole, index, count):
    size = whole.shape[0] // count
    return lax.dynamic_slice_in_dim(whole, (index % count) * size, size, 0)


def split_two(values):
    high = lax.reduce_precision(values, 8, 7)
    return high.astype(jnp.bfloat16), (values - high).astype(jnp.bfloat16)


def kernel_params():
    return pltpu.CompilerParams(vmem_limit_bytes=VMEM_BYTES)


def cost(flops, moved):
    return pl.CostEstimate(flops=int(flops), bytes_accessed=int(moved), transcendentals=0)


def down_t_kernel(grad_ref, down_ref, out_ref):
    rows = out_ref.shape[1]
    grads = grad_ref[...].reshape(rows, grad_ref.shape[-1])
    out_ref[0] = times_t(grads, down_ref[...])


def down_t(grads, w_down, units):
    sources, owned, cap, width = grads.shape
    rows = sources * cap
    tile = min(units, 512)
    tiles = units // tile
    return pl.pallas_call(
        down_t_kernel,
        grid=(owned, tiles),
        in_specs=[
            pl.BlockSpec((sources, 1, cap, width), lambda l, f: (0, l, 0, 0)),
            pl.BlockSpec((tile, width), lambda l, f: (l * tiles + f, 0)),
        ],
        out_specs=pl.BlockSpec((1, rows, tile), lambda l, f: (l, 0, f)),
        out_shape=jax.ShapeDtypeStruct((owned, rows, units), jnp.float32),
        compiler_params=kernel_params(),
        cost_estimate=cost(
            2 * owned * rows * units * width, 2 * owned * (rows + units) * width
        ),
        name="down_t",
    )(grads, w_down)


def expert_kernel(
    rows_ref, gate_ref, up_ref, down_grad_ref, mark_ref, back_ref, hid_ref, dgate_ref, dup_ref,
    total, scalar
):
    step = pl.program_id(1)
    rows, width = total.shape
    packed = rows_ref[...].reshape(rows, rows_ref.shape[-1])
    inputs = packed[:, :width]
    mark = mark_ref[0]
    gate = jnp.sum(
        packed[:, width:].astype(jnp.float32) * (mark[0:1] + mark[1:2]), -1, keepdims=True
    )
    gate_pre = jnp.dot(inputs, gate_ref[...], preferred_element_type=jnp.float32)
    up_pre = jnp.dot(inputs, up_ref[...], preferred_element_type=jnp.float32)
    sigmoid = jax.nn.sigmoid(gate_pre)
    active = gate_pre * sigmoid
    hidden = active * up_pre
    raw_grad = down_grad_ref[0]
    gate_part = jnp.sum(hidden * raw_grad, -1, keepdims=True)
    grad_hidden = raw_grad * gate
    grad_gate = (grad_hidden * up_pre * sigmoid * (1.0 + gate_pre * (1.0 - sigmoid))).astype(
        jnp.bfloat16
    )
    grad_up = (grad_hidden * active).astype(jnp.bfloat16)
    hid_ref[0] = (hidden * gate).astype(jnp.bfloat16)
    dgate_ref[0] = grad_gate
    dup_ref[0] = grad_up
    back = times_t(grad_gate, gate_ref[...]) + times_t(grad_up, up_ref[...])

    @pl.when(step == 0)
    def _():
        total[...] = back
        scalar[...] = jnp.broadcast_to(gate_part, scalar.shape)

    @pl.when(step > 0)
    def _():
        total[...] += back
        scalar[...] += jnp.broadcast_to(gate_part, scalar.shape)

    @pl.when(step == pl.num_programs(1) - 1)
    def _():
        sources, _, cap, packed_width = back_ref.shape
        back_ref[:, :, :, :width] = (
            total[...].astype(jnp.bfloat16).reshape(sources, 1, cap, width)
        )
        value = scalar[:, 0:1]
        high = value.astype(jnp.bfloat16).astype(jnp.float32)
        low = value - high
        extra = high * mark[0:1] + low * mark[1:2]
        back_ref[:, :, :, width:] = extra.astype(jnp.bfloat16).reshape(
            sources, 1, cap, packed_width - width
        )


def expert_core(packed, w_gate, w_up, raw_grad, marks, units):
    sources, owned, cap, packed_width = packed.shape
    rows = sources * cap
    width = w_gate.shape[0]
    tile = min(units, 512)
    tiles = units // tile
    hidden_shape = jax.ShapeDtypeStruct((owned, rows, units), jnp.bfloat16)
    hidden_spec = pl.BlockSpec((1, rows, tile), lambda l, f: (l, 0, f))
    weight_spec = pl.BlockSpec((width, tile), lambda l, f: (0, l * tiles + f))
    packed_spec = pl.BlockSpec((sources, 1, cap, packed_width), lambda l, f: (0, l, 0, 0))
    return pl.pallas_call(
        expert_kernel,
        grid=(owned, tiles),
        in_specs=[
            packed_spec,
            weight_spec,
            weight_spec,
            hidden_spec,
            pl.BlockSpec((1, 8, packed_width - width), lambda l, f: (l, 0, 0)),
        ],
        out_specs=[packed_spec, hidden_spec, hidden_spec, hidden_spec],
        out_shape=[
            jax.ShapeDtypeStruct(packed.shape, jnp.bfloat16),
            hidden_shape,
            hidden_shape,
            hidden_shape,
        ],
        scratch_shapes=[
            pltpu.VMEM((rows, width), jnp.float32),
            pltpu.VMEM((rows, 128), jnp.float32),
        ],
        compiler_params=kernel_params(),
        cost_estimate=cost(
            8 * owned * rows * units * width, 4 * owned * (rows + 2 * units) * width
        ),
        name="expert_core",
    )(packed, w_gate, w_up, raw_grad, marks)


def expert_out_kernel(*refs):
    *hid_refs, down_ref, out_ref = refs

    for block, hid_ref in enumerate(hid_refs):

        @pl.when(pl.program_id(0) == block)
        def _():
            out = jnp.dot(hid_ref[0], down_ref[...], preferred_element_type=jnp.float32)
            out_ref[...] = out.astype(jnp.bfloat16).reshape(out_ref.shape)


def expert_out(hiddens, w_down, sources):
    count = len(hiddens)
    owned, rows, units = hiddens[0].shape
    width = w_down.shape[1]
    cap = rows // sources
    tile = min(width, 1024)
    return pl.pallas_call(
        expert_out_kernel,
        grid=(count, owned, width // tile),
        in_specs=[pl.BlockSpec((1, rows, units), lambda b, l, d: (l, 0, 0))] * count
        + [pl.BlockSpec((units, tile), lambda b, l, d: (l, d))],
        out_specs=pl.BlockSpec(
            (sources, 1, cap, tile), lambda b, l, d: (0, b * owned + l, 0, d)
        ),
        out_shape=jax.ShapeDtypeStruct((sources, count * owned, cap, width), jnp.bfloat16),
        compiler_params=kernel_params(),
        cost_estimate=cost(
            2 * count * owned * rows * units * width, 2 * count * owned * (rows + units) * width
        ),
        name="expert_out",
    )(*hiddens, w_down)


def in_grads_kernel(count, *refs):
    row_refs, grad_refs, out_ref = refs[:count], refs[count : 2 * count], refs[2 * count]
    rows = grad_refs[0].shape[1]
    total = None
    for row_ref, grad_ref in zip(row_refs, grad_refs):
        part = first_t(row_ref[...].reshape(rows, row_ref.shape[-1]), grad_ref[0])
        total = part if total is None else total + part
    out_ref[...] = total


def in_grads(packed, grads, width):
    count = len(packed)
    sources, owned, cap, _ = packed[0].shape
    _, rows, units = grads[0].shape
    tile = min(width, 512)
    return pl.pallas_call(
        functools.partial(in_grads_kernel, count),
        grid=(owned, width // tile),
        in_specs=[pl.BlockSpec((sources, 1, cap, tile), lambda l, d: (0, l, 0, d))] * count
        + [pl.BlockSpec((1, rows, units), lambda l, d: (l, 0, 0))] * count,
        out_specs=pl.BlockSpec((tile, units), lambda l, d: (d, l)),
        out_shape=jax.ShapeDtypeStruct((width, owned * units), jnp.float32),
        compiler_params=kernel_params(),
        cost_estimate=cost(
            2 * owned * count * rows * units * width, 4 * owned * units * width
        ),
        name="in_grads",
    )(*packed, *grads)


def down_grads_kernel(count, *refs):
    hid_refs, grad_refs = refs[:count], refs[count : 2 * count]
    out_ref = refs[2 * count]
    rows = hid_refs[0].shape[1]
    total = None
    for hid_ref, grad_ref in zip(hid_refs, grad_refs):
        part = first_t(hid_ref[0], grad_ref[...].reshape(rows, grad_ref.shape[-1]))
        total = part if total is None else total + part
    out_ref[...] = total


def down_grads(hiddens, grads):
    count = len(hiddens)
    sources, owned, cap, width = grads[0].shape
    _, rows, units = hiddens[0].shape
    tile = min(units, 256)
    tiles = units // tile
    return pl.pallas_call(
        functools.partial(down_grads_kernel, count),
        grid=(owned, tiles),
        in_specs=[pl.BlockSpec((1, rows, tile), lambda l, f: (l, 0, f))] * count
        + [pl.BlockSpec((sources, 1, cap, width), lambda l, f: (0, l, 0, 0))] * count,
        out_specs=pl.BlockSpec((tile, width), lambda l, f: (l * tiles + f, 0)),
        out_shape=jax.ShapeDtypeStruct((owned * units, width), jnp.float32),
        compiler_params=kernel_params(),
        cost_estimate=cost(
            2 * owned * count * rows * units * width, 4 * owned * units * width
        ),
        name="down_grads",
    )(*hiddens, *grads)


def turn(values, cosines, sines):
    return values * cosines + pltpu.roll(values, values.shape[-1] // 2, 1) * sines


def score_t(keys, queries, key_docs, query_docs, first, factor):
    scores = times_t(keys, queries) * factor
    key_pos = lax.broadcasted_iota(jnp.int32, scores.shape, 0)
    query_pos = first + lax.broadcasted_iota(jnp.int32, scores.shape, 1)
    return jnp.where((key_pos <= query_pos) & (key_docs == query_docs), scores, MASKED)


def attend_kernel(
    block, factor, query_ref, key_ref, value_ref, inv_query_ref, inv_key_ref, query_gain_ref,
    key_gain_ref, cos_ref, sin_ref, doc_col_ref, doc_row_ref, query_out, key_out, value_out,
    attended_ref, log_ref
):
    cosines, sines = cos_ref[...], sin_ref[...]
    queries = turn(query_ref[...] * inv_query_ref[...] * query_gain_ref[...], cosines, sines)
    keys = turn(key_ref[...] * inv_key_ref[...] * key_gain_ref[...], cosines, sines)
    query_out[...] = queries.astype(jnp.bfloat16)
    key_out[...] = keys.astype(jnp.bfloat16)
    value_out[...] = value_ref[...].astype(jnp.bfloat16)
    for first in range(0, query_ref.shape[0], block):
        stop = first + block
        scores = score_t(
            key_out[:stop, :],
            query_out[first:stop, :],
            doc_col_ref[:stop, :],
            doc_row_ref[:, first:stop],
            first,
            factor,
        )
        peak = jnp.max(scores, 0, keepdims=True)
        exps = jnp.exp(scores - peak)
        total = jnp.sum(exps, 0, keepdims=True)
        log_ref[0, :, first:stop] = peak + jnp.log(total)
        weights = (exps * (1.0 / total)).astype(jnp.bfloat16)
        attended_ref[first:stop, :] = first_t(value_out[:stop, :], weights).T.astype(jnp.bfloat16)


def attend(qkv, inv_query, inv_key, query_gain, key_gain, tables, doc_ids, block, factor):
    length = qkv.shape[0]
    head_cols = qkv.shape[1] // 3
    heads = head_cols // HEAD_DIM
    head_spec = pl.BlockSpec((length, HEAD_DIM), lambda h: (0, h))
    gain_spec = pl.BlockSpec((1, HEAD_DIM), lambda h: (0, h))

    def whole(shape):
        return pl.BlockSpec(shape, lambda h: (0, 0))

    out = jax.ShapeDtypeStruct((length, head_cols), jnp.bfloat16)
    return pl.pallas_call(
        functools.partial(attend_kernel, block, factor),
        grid=(heads,),
        in_specs=[
            head_spec,
            pl.BlockSpec((length, HEAD_DIM), lambda h: (0, heads + h)),
            pl.BlockSpec((length, HEAD_DIM), lambda h: (0, 2 * heads + h)),
            whole((length, 1)),
            whole((length, 1)),
            gain_spec,
            gain_spec,
            whole((length, HEAD_DIM)),
            whole((length, HEAD_DIM)),
            whole((length, 1)),
            whole((1, length)),
        ],
        out_specs=[head_spec] * 4 + [pl.BlockSpec((1, 1, length), lambda h: (h, 0, 0))],
        out_shape=[out] * 4 + [jax.ShapeDtypeStruct((heads, 1, length), jnp.float32)],
        compiler_params=kernel_params(),
        cost_estimate=cost(24 * head_cols * length * length, 20 * length * head_cols),
        name="attend",
    )(
        qkv,
        qkv,
        qkv,
        inv_query,
        inv_key,
        query_gain[None, :],
        key_gain[None, :],
        tables[0],
        tables[1],
        doc_ids[:, None],
        doc_ids[None, :],
    )


def attend_back_kernel(
    block, factor, query_ref, key_ref, value_ref, out_grad_ref, log_ref, raw_query_ref,
    raw_key_ref, inv_query_ref, inv_key_ref, query_gain_ref, key_gain_ref, cos_ref, sin_ref,
    doc_col_ref, doc_row_ref, query_out, key_out, value_out, query_sum_ref, key_sum_ref,
    query_gain_out, key_gain_out, query_grad, key_grad, value_grad
):
    key_grad[...] = jnp.zeros(key_grad.shape, jnp.float32)
    value_grad[...] = jnp.zeros(value_grad.shape, jnp.float32)
    for first in range(0, query_ref.shape[0], block):
        stop = first + block
        keys = key_ref[:stop, :]
        queries = query_ref[first:stop, :]
        out_grads = out_grad_ref[first:stop, :]
        scores = score_t(
            keys, queries, doc_col_ref[:stop, :], doc_row_ref[:, first:stop], first, factor
        )
        probs = jnp.exp(scores - log_ref[0, :, first:stop])
        prob_grads = times_t(value_ref[:stop, :], out_grads)
        mean = jnp.sum(probs * prob_grads, 0, keepdims=True)
        score_grads = (probs * (prob_grads - mean)).astype(jnp.bfloat16)
        value_grad[:stop, :] += jnp.dot(
            probs.astype(jnp.bfloat16), out_grads, preferred_element_type=jnp.float32
        )
        key_grad[:stop, :] += jnp.dot(score_grads, queries, preferred_element_type=jnp.float32)
        query_grad[first:stop, :] = first_t(keys, score_grads).T
    cosines, sines = cos_ref[...], -sin_ref[...]
    value_out[...] = value_grad[...].astype(jnp.bfloat16)
    head = pl.program_id(0)
    for grad, raw_ref, inv_ref, gain_ref, out_ref, sum_ref, gain_out in (
        (
            query_grad, raw_query_ref, inv_query_ref, query_gain_ref, query_out, query_sum_ref,
            query_gain_out
        ),
        (key_grad, raw_key_ref, inv_key_ref, key_gain_ref, key_out, key_sum_ref, key_gain_out),
    ):
        norm_grad = turn(grad[...] * factor, cosines, sines)
        raw = raw_ref[...]
        scaled = norm_grad * gain_ref[...]
        out_ref[...] = scaled
        part = jnp.sum(scaled * raw, -1, keepdims=True)
        gain_out[...] = jnp.sum(norm_grad * raw * inv_ref[...], 0, keepdims=True)

        @pl.when(head == 0)
        def _():
            sum_ref[...] = part

        @pl.when(head > 0)
        def _():
            sum_ref[...] += part


def attend_back(
    parts, out_grads, logs, qkv, inv_query, inv_key, query_gain, key_gain, tables, doc_ids, block,
    factor
):
    length = qkv.shape[0]
    head_cols = qkv.shape[1] // 3
    heads = head_cols // HEAD_DIM
    head_spec = pl.BlockSpec((length, HEAD_DIM), lambda h: (0, h))
    gain_spec = pl.BlockSpec((1, HEAD_DIM), lambda h: (0, h))

    def whole(shape):
        return pl.BlockSpec(shape, lambda h: (0, 0))

    wide = jax.ShapeDtypeStruct((length, head_cols), jnp.float32)
    narrow = jax.ShapeDtypeStruct((length, head_cols), jnp.bfloat16)
    column = jax.ShapeDtypeStruct((length, 1), jnp.float32)
    gains = jax.ShapeDtypeStruct((1, head_cols), jnp.float32)
    return pl.pallas_call(
        functools.partial(attend_back_kernel, block, factor),
        grid=(heads,),
        in_specs=[head_spec] * 4
        + [
            pl.BlockSpec((1, 1, length), lambda h: (h, 0, 0)),
            head_spec,
            pl.BlockSpec((length, HEAD_DIM), lambda h: (0, heads + h)),
            whole((length, 1)),
            whole((length, 1)),
            gain_spec,
            gain_spec,
            whole((length, HEAD_DIM)),
            whole((length, HEAD_DIM)),
            whole((length, 1)),
            whole((1, length)),
        ],
        out_specs=[
            head_spec,
            head_spec,
            head_spec,
            whole((length, 1)),
            whole((length, 1)),
            gain_spec,
            gain_spec,
        ],
        out_shape=[wide, wide, narrow, column, column, gains, gains],
        scratch_shapes=[pltpu.VMEM((length, HEAD_DIM), jnp.float32)] * 3,
        compiler_params=kernel_params(),
        cost_estimate=cost(40 * head_cols * length * length, 40 * length * head_cols),
        name="attend_back",
    )(
        *parts,
        out_grads,
        logs,
        qkv,
        qkv,
        inv_query,
        inv_key,
        query_gain[None, :],
        key_gain[None, :],
        tables[0],
        tables[1],
        doc_ids[:, None],
        doc_ids[None, :],
    )


def placings(routes, owners, capacity):
    tok_count = routes.shape[0]
    named = jnp.any(owners[:, None, None] == routes[None, :, :], -1)
    before = (
        jnp.arange(tok_count)[:, None] < jnp.arange(tok_count)[None, :]
    ).astype(jnp.bfloat16)
    slot = jnp.dot(named.astype(jnp.bfloat16), before, preferred_element_type=jnp.float32)
    hit = (slot[:, None, :] == jnp.arange(capacity, dtype=jnp.float32)[None, :, None]) & named[
        :, None, :
    ]
    return hit.astype(jnp.bfloat16).reshape(owners.shape[0] * capacity, tok_count)


def local(
    tokens,
    out_grad,
    segments,
    routes,
    attn_gain,
    ffn_gain,
    query_gain,
    key_gain,
    w_query,
    w_key,
    w_value,
    w_out,
    router,
    w_gate,
    w_up,
    w_down,
):
    rows_total = lax.axis_size("row")
    cols_total = lax.axis_size("col")
    devices = rows_total * cols_total
    place = lax.axis_index("col")
    tok_count, width = tokens.shape
    top_count = routes.shape[1]
    expert_count = router.shape[1]
    capacity = tok_count * top_count * 3 // (expert_count * 2)
    capacity = -(-capacity // 16) * 16
    local_units = w_gate.shape[1]
    ff_units = local_units * devices // expert_count
    units = min(local_units, ff_units)
    owned = local_units // units
    head_cols = w_query.shape[1]
    doc_ids = segments[0]
    length = doc_ids.shape[0]
    block = min(length, 256)
    factor = 1.0 / HEAD_DIM**0.5
    extra = -(-2 * expert_count // 128) * 128

    inputs_f = tokens.astype(jnp.float32)
    inv_first = rms_scale(inputs_f)
    normal_a = (inputs_f * inv_first * attn_gain).astype(jnp.bfloat16)
    wqkv = lax.all_gather(
        jnp.concatenate([w_query, w_key, w_value], 1), "row", axis=0, tiled=True
    )
    wo_full = lax.all_gather(w_out, "row", axis=1, tiled=True)
    a_blocks = ring_blocks(normal_a, "col")
    g_blocks = [out_grad, shift(after(out_grad, a_blocks[-1]), "col")]

    route_blocks = hop_blocks(routes, "col")
    plane_ids = (jnp.arange(rows_total) * cols_total + place)[:, None] * local_units
    owners = ((plane_ids + jnp.arange(owned)[None, :] * units) // ff_units).reshape(-1)
    row_place = lax.axis_index("row")
    my_ids = (
        (row_place * cols_total + place) * local_units + jnp.arange(owned) * units
    ) // ff_units
    extra_ids = jnp.arange(extra)
    marks = jnp.concatenate(
        [
            (extra_ids[None, None, :] == my_ids[:, None, None]).astype(jnp.float32),
            (extra_ids[None, None, :] == my_ids[:, None, None] + expert_count).astype(
                jnp.float32
            ),
            jnp.zeros((owned, 6, extra), jnp.float32),
        ],
        1,
    )
    placed = [placings(block_routes, owners, capacity) for block_routes in route_blocks]

    queue = []

    def in_plane(table, *earlier):
        if queue or earlier:
            table = after(table, *queue[-1:], *earlier)
        queue.append(lax.all_to_all(table, "row", split_axis=0, concat_axis=0, tiled=True))
        return queue[-1]

    def to_experts(values, back, *earlier):
        table = jnp.dot(placed[back], values, preferred_element_type=jnp.float32)
        table = table.astype(jnp.bfloat16).reshape(rows_total, owned, capacity, -1)
        return in_plane(table, *earlier)

    def to_tokens(table, back, *earlier):
        home = in_plane(table, *earlier)
        return first_t(
            placed[back], home.reshape(rows_total * owned * capacity, table.shape[-1])
        )

    g_rows = [to_experts(out_grad, 0)]
    seq_rows = after(natural(a_blocks, place), g_rows[0])
    qkv = jnp.dot(seq_rows, wqkv, preferred_element_type=jnp.float32)
    query_raw = qkv[:, :head_cols]
    key_raw = qkv[:, head_cols : 2 * head_cols]
    squares = exchange_sum(
        jnp.stack([jnp.sum(query_raw * query_raw, -1), jnp.sum(key_raw * key_raw, -1)]), "col"
    )
    g_blocks.append(shift(after(g_blocks[1], squares), "col"))
    g_rows.append(to_experts(after(g_blocks[1], qkv), 1))
    inv_query = lax.rsqrt(squares[0] / width + EPSILON)[:, None]
    inv_key = lax.rsqrt(squares[1] / width + EPSILON)[:, None]
    cosines, sine_table = rope_tables(length, HEAD_DIM)
    tables = (
        jnp.concatenate([cosines, cosines], -1),
        jnp.concatenate([-sine_table, sine_table], -1),
    )
    *heads_out, attended, logs = attend(
        qkv, inv_query, inv_key, query_gain, key_gain, tables, doc_ids, block, factor
    )
    attended = after(attended, g_blocks[2])
    raw_grads = [down_t(rows, w_down, units) for rows in g_rows]
    g_rows.append(to_experts(g_blocks[2], 2))
    parts = [
        jnp.dot(
            block_of(attended, place - back, cols_total),
            wo_full,
            preferred_element_type=jnp.float32,
        )
        for back in range(cols_total)
    ]
    parts[2] = after(parts[2], raw_grads[0])
    parts[3] = after(parts[3], raw_grads[1])
    parts[0] = after(parts[0], g_rows[2])
    attn = ring_sum(parts, "col")
    residual = inputs_f + attn
    inv_second = rms_scale(residual)
    normal_b = (residual * inv_second * ffn_gain).astype(jnp.bfloat16)
    expert_probs = jax.nn.softmax(
        jnp.dot(normal_b, router, preferred_element_type=jnp.float32), axis=-1
    )

    high, low = split_two(expert_probs)
    packed_b = jnp.concatenate(
        [normal_b, high, low, jnp.zeros((tok_count, extra - 2 * expert_count), jnp.bfloat16)], 1
    )
    b_blocks = [packed_b, shift(packed_b, "col")]
    b_rows = [to_experts(packed_b, 0)]
    raw_grads.append(down_t(g_rows[2], w_down, units))
    core = []

    def run_core():
        back = len(core)
        core.append(expert_core(b_rows[back], w_gate, w_up, raw_grads[back], marks, units))

    b_rows.append(to_experts(after(b_blocks[1], raw_grads[2]), 1))
    run_core()
    for back in range(2, cols_total):
        if back > 2:
            g_blocks.append(shift(after(g_blocks[-1], b_blocks[-1]), "col"))
            b_blocks[-1] = after(b_blocks[-1], g_blocks[-1])
        b_blocks.append(shift(b_blocks[-1], "col"))
        if back > 2:
            g_rows.append(to_experts(after(g_blocks[back], core[-1][1]), back))
            run_core()
            raw_grads.append(down_t(g_rows[back], w_down, units))
        b_rows.append(to_experts(after(b_blocks[back], core[-1][1]), back))
        if back == 2:
            run_core()
    last = cols_total - 1
    share = to_tokens(core[1][0], 1, raw_grads[last], core[-1][1])
    grad_packed = share.astype(jnp.bfloat16)
    run_core()
    hiddens = [part[1] for part in core]
    order = list(range(1, cols_total)) + [0]
    out_groups = [order[:2]] + [[back] for back in order[2:]]

    def expert_outs(group, *earlier):
        first = after(hiddens[group[0]], *earlier)
        return expert_out([first] + [hiddens[b] for b in group[1:]], w_down, rows_total)

    grad_gates = [after(core[0][2], grad_packed)] + [part[2] for part in core[1:]]
    gate_grad = in_grads(b_rows, grad_gates, width)
    outs = [expert_outs(out_groups[0], grad_packed)]
    beside = [hiddens[last]]
    for back in range(2, cols_total):
        share = to_tokens(core[back][0], back, *beside)
        grad_packed = (shift(grad_packed, "col").astype(jnp.float32) + share).astype(
            jnp.bfloat16
        )
        if back == 2:
            grad_ups = [after(core[0][3], grad_packed)] + [part[3] for part in core[1:]]
            up_grad = in_grads(b_rows, grad_ups, width)
        if back < last:
            outs.append(expert_outs(out_groups[back - 1], grad_packed))
            beside = [gate_grad, outs[0]] if back == 2 else [outs[-2]]
    share = to_tokens(core[0][0], 0, up_grad, outs[-1])
    down_grad = down_grads([after(hiddens[0], grad_packed)] + hiddens[1:], g_rows)
    outs += [expert_outs(group, grad_packed) for group in out_groups[len(outs) :]]
    share = after(share, down_grad, *outs)
    grad_packed = shift(grad_packed, "col").astype(jnp.float32) + share

    homes = []

    def outs_home(number):
        home = in_plane(outs[number])
        homes.append(home)
        for slot, back in enumerate(out_groups[number]):
            rows = home[:, slot * owned : (slot + 1) * owned]
            rows = rows.reshape(rows_total * owned * capacity, width)
            out_shares[back] = first_t(placed[back], rows)

    out_shares = {}
    outs_home(0)

    grad_f = out_grad.astype(jnp.float32)
    grad_probs = (
        grad_packed[:, width : width + expert_count]
        + grad_packed[:, width + expert_count : width + 2 * expert_count]
    )
    grad_logits = (
        expert_probs * (grad_probs - jnp.sum(expert_probs * grad_probs, -1, keepdims=True))
    ).astype(jnp.bfloat16)
    grad_normal_b = grad_packed[:, :width] + times_t(grad_logits, router)
    grad_norm_second, ffn_gain_local = norm_back(residual, inv_second, ffn_gain, grad_normal_b)
    grad_residual = grad_f + grad_norm_second
    grad_attn = grad_residual.astype(jnp.bfloat16)
    small = jnp.concatenate(
        [grad_logits]
        + [part.reshape(tok_count, -1) for part in split_two(ffn_gain_local)]
        + [jnp.zeros((tok_count, 128 - expert_count - 2 * width // tok_count), jnp.bfloat16)],
        1,
    )

    grad_blocks = ring_blocks(grad_attn, "col")
    grad_out_heads = natural(
        [times_t(block_grad, wo_full).astype(jnp.bfloat16) for block_grad in grad_blocks], place
    )
    grad_out_heads = after(grad_out_heads, out_shares[1])
    for number in range(1, len(outs)):
        outs_home(number)
    moe = shift(after(out_shares[1].astype(jnp.bfloat16), grad_blocks[-1]), "col")
    (
        query_scaled,
        key_scaled,
        grad_value_b,
        query_sum,
        key_sum,
        query_gain_local,
        key_gain_local,
    ) = attend_back(
        heads_out,
        grad_out_heads,
        logs,
        qkv,
        inv_query,
        inv_key,
        query_gain,
        key_gain,
        tables,
        doc_ids,
        block,
        factor,
    )
    query_sum = after(query_sum, moe)
    sums = exchange_sum(jnp.stack([query_sum[:, 0], key_sum[:, 0]]), "col")
    moe = (moe.astype(jnp.float32) + out_shares[2]).astype(jnp.bfloat16)
    small_blocks = hop_blocks(after(small, query_sum), "col")
    small_rows = natural(small_blocks, place)
    router_local = first_t(natural(b_blocks, place)[:, :width], small_rows[:, :expert_count])
    gain_width = width // tok_count
    gain_parts = small_rows[:, expert_count : expert_count + 2 * gain_width].astype(jnp.float32)
    gain_parts = gain_parts[:, :gain_width] + gain_parts[:, gain_width:]
    ffn_gain_part = jnp.sum(gain_parts.reshape(cols_total, width), 0)
    early = jnp.concatenate(
        [
            router_local.reshape(rows_total, -1, expert_count),
            ffn_gain_part.reshape(rows_total, -1, expert_count),
        ],
        1,
    )
    early_table = early
    early = jnp.sum(in_plane(early), 0)
    grad_query_b = (
        inv_query * query_scaled
        - query_raw * inv_query * inv_query * inv_query * (sums[0] / width)[:, None]
    ).astype(jnp.bfloat16)
    grad_key_b = (
        inv_key * key_scaled - key_raw * inv_key * inv_key * inv_key * (sums[1] / width)[:, None]
    ).astype(jnp.bfloat16)
    grad_qkv = jnp.concatenate([grad_query_b, grad_key_b, grad_value_b], 1)
    grad_qkv = after(grad_qkv, homes[1], *small_blocks[1:])
    da_parts = [
        times_t(block_of(grad_qkv, place - back, cols_total), wqkv) for back in range(cols_total)
    ]
    da_total = da_parts[1].astype(jnp.bfloat16)
    incoming = natural([after(grad_blocks[0], da_total)] + grad_blocks[1:], place)
    wout_local = first_t(incoming, attended).astype(jnp.bfloat16)
    for back in range(2, cols_total):
        da_came = shift(da_total, "col")
        if back == 2:
            da_came = after(da_came, early_table, wout_local)
        da_total = (da_came.astype(jnp.float32) + da_parts[back]).astype(jnp.bfloat16)
        if back == 2:
            da_second = da_total
        if back == last:
            da_total = after(da_total, early)
    moe = after(moe, da_came)
    for back in order[2:]:
        moe = shift(moe, "col").astype(jnp.float32) + out_shares[back]
        if back:
            moe = moe.astype(jnp.bfloat16)
    output = (residual + moe).astype(jnp.bfloat16)
    grad_normal_a = shift(da_total, "col").astype(jnp.float32) + da_parts[0]
    wqkv_local = first_t(seq_rows, after(grad_qkv, da_second, homes[-1])).astype(jnp.bfloat16)
    attn_gain_local = (
        jnp.sum(wqkv.astype(jnp.float32) * wqkv_local.astype(jnp.float32), -1) / attn_gain
    )
    late = jnp.concatenate([attn_gain_local, query_gain_local[0], key_gain_local[0]])
    late = jnp.concatenate([early.reshape(-1), late]).reshape(1, -1, 128)
    spread = in_plane(jnp.broadcast_to(late, (rows_total,) + late.shape[1:]))
    spread = spread.reshape(rows_total, -1)
    late = jnp.sum(spread[:, early.size :], 0)
    early = spread[:, : early.size].reshape((rows_total,) + early.shape)
    attn_gain_grad = exchange_sum(late[:width], "col", place)

    core_place = row_place % 2

    def over_cores(value):
        halves = value.reshape(rows_total // 2, 2, -1, value.shape[-1])
        other = lax.ppermute(
            lax.dynamic_index_in_dim(halves, 1 - core_place, 1, False),
            "row",
            [(i, i ^ 1) for i in range(rows_total)],
        )
        return (
            lax.dynamic_index_in_dim(halves, core_place, 1, False).astype(jnp.float32) + other
        ).astype(jnp.bfloat16)

    pair = jnp.concatenate([over_cores(wqkv_local), over_cores(wout_local)], -1)
    pair = lax.all_to_all(
        after(pair, queue[-1]),
        "row",
        split_axis=0,
        concat_axis=0,
        tiled=True,
        axis_index_groups=[list(range(core, rows_total, 2)) for core in range(2)],
    )
    weight_grads = jnp.sum(pair.astype(jnp.float32), 0)
    wqkv_grad = weight_grads[:, : 3 * head_cols]
    out_proj_grad = weight_grads[:, 3 * head_cols :].T
    router_grad = early[:, : width // rows_total].reshape(width, expert_count)
    ffn_gain_grad = early[:, width // rows_total :].reshape(width)
    grad_norm_first, _ = norm_back(inputs_f, inv_first, attn_gain, grad_normal_a)
    input_grad = grad_residual + grad_norm_first
    return (
        output,
        input_grad,
        attn_gain_grad,
        ffn_gain_grad,
        late[width : width + head_cols],
        late[width + head_cols :],
        wqkv_grad[:, :head_cols],
        wqkv_grad[:, head_cols : 2 * head_cols],
        wqkv_grad[:, 2 * head_cols :],
        out_proj_grad,
        router_grad,
        gate_grad,
        up_grad,
        down_grad,
    )


def solution(mesh):
    return jax.shard_map(
        local,
        mesh=mesh,
        in_specs=(
            P(("row", "col"), None),
            P(("row", "col"), None),
            P("row", None),
            P(("row", "col"), None),
            P(),
            P(),
            P("col"),
            P("col"),
            P("row", "col"),
            P("row", "col"),
            P("row", "col"),
            P("col", "row"),
            P(),
            P(None, ("row", "col")),
            P(None, ("row", "col")),
            P(("row", "col"), None),
        ),
        out_specs=(
            P(("row", "col"), None),
            P(("row", "col"), None),
            P(),
            P(),
            P("col"),
            P("col"),
            P("row", "col"),
            P("row", "col"),
            P("row", "col"),
            P("col", "row"),
            P(),
            P(None, ("row", "col")),
            P(None, ("row", "col")),
            P(("row", "col"), None),
        ),
        check_vma=False,
    )
```
